256 devices in a mesh: seq: 16 (over z, core), grp: 16 (over y, x).
Axes of the slice: x: 4, y: 4, z: 8, core: 2. Of those that a mesh axis runs over, the one named last changes fastest.
Arguments:
- query_rows: bfloat16 [131072, 2048], P(('seq', 'grp')), may hold values from -5 to 5
- key_rows: bfloat16 [131072, 2048], P(('seq', 'grp')), may hold values from -5 to 5
- value_rows: bfloat16 [131072, 2048], P(('seq', 'grp')), may hold values from -6 to 6
- pick_column: int32 [16, 16, 16, 3], replicated, may hold values from 0 to 15, all different within a row; in each aligned block of 16 rows (0 to 15, 16 to 31, ..., all dimensions but the last counted through in order) at most 4 rows name the same one
- pick_back: int32 [16, 16, 16, 3], replicated, may hold values from 0 to 7
Outputs:
- attended: bfloat16 [131072, 2048], P(('seq', 'grp'))
The draws below stay inside these ranges and needn't reach their ends.
Inputs may be any that keep to these rules, and one draw needn't show every extreme that they name: Rows of pick_column are taken in the order of its first three dimensions; each names 3 different columns. In each aligned block of 16 rows no column is named by more than 4 rows, a bound that some block reaches.
All inputs are finite; a program needn't handle non-finite values.
Results may differ from the reference program's by a relative error of at most 0.014.
Values may be sent and summed in bfloat16 or wider, within the bound.
No kernel may reach another device: no remote copies, remote signals or barrier semaphores. Data moves between devices by JAX's collectives and lax.ppermute only.
A program may use at most 128 MiB of HBM per device.

```python
import math
import jax
import jax.numpy as jnp
import numpy as np
from jax import lax

HEADS = 16
DH = 128
BLK = 512
TOPK = 3
TOK_DEV = 512
BPD = 1
TOKENS = 131072
NLOC = 16
CAP = 4
DBACK = 8
N_GRP = 16


def draw_query_rows(key, part):
    key = jax.random.fold_in(key, 11)
    first_key = jax.random.fold_in(key, 0)
    drawn = jax.random.normal(first_key, (TOKENS, HEADS * DH), jnp.float32)
    return jnp.clip(drawn, -5.0, 5.0).astype(jnp.bfloat16)


def draw_key_rows(key, part):
    key = jax.random.fold_in(key, 23)
    first_key = jax.random.fold_in(key, 0)
    drawn = jax.random.normal(first_key, (TOKENS, HEADS * DH), jnp.float32)
    return jnp.clip(drawn, -5.0, 5.0).astype(jnp.bfloat16)


def touch_ends(array, own_key, smallest, top_value):
    spot = [jax.random.randint(jax.random.fold_in(own_key, axis), (), 0, length) for axis, length in enumerate(array.shape)]
    longest = array.shape.index(max(array.shape))
    beside = spot[:longest] + [(spot[longest] + 1) % array.shape[longest]] + spot[longest + 1:]
    return array.at[tuple(spot)].set(smallest).at[tuple(beside)].set(top_value)


def levels(rng, extent, cuts, least, high):
    gain = 1.0
    for position, blocks in cuts:
        draws = jax.random.uniform(jax.random.fold_in(jax.random.fold_in(rng, 6), position), (blocks,), jnp.float32, least / len(cuts), high / len(cuts))
        gain = gain * jnp.repeat(jnp.exp(draws), extent[position] // blocks).reshape((-1,) + (1,) * (len(extent) - 1 - position))
    return gain


def assign_block(stream_key, own, number, rows, count, top, reach, lean):
    sequence = jax.random.permutation(stream_key, count)
    heavy_load, ordinary = portions_of(count, rows * top, reach, lean, True), portions_of(count, rows * top, reach, lean, False)
    places = jnp.arange(count)

    def named(lengths, offset_by):
        used = int((lengths > 0).sum())
        fixed = max(1, used // 4)
        moved = fixed + (places - fixed + offset_by * (used - fixed)) % max(1, count - fixed)
        return jnp.zeros((count,), jnp.int32).at[sequence[jnp.where(places < fixed, places, moved)]].set(jnp.asarray(lengths, jnp.int32))

    lengths = jnp.where(number % 4 == 0, named(heavy_load, number // 4), named(ordinary, number - number // 4 - 1))
    mixed = jax.random.permutation(jax.random.fold_in(own, 3), count)
    source_of, sink = mixed[0:count // 2 * 2:2], mixed[1:count // 2 * 2:2]
    slack = jnp.minimum(lengths[source_of] - 1, reach - lengths[sink]) // 2
    slack = jnp.where((source_of == sequence[0]) | (sink == sequence[0]) | (lengths[sink] == 0), 0, jnp.maximum(slack, 0))
    moved = jax.random.randint(jax.random.fold_in(own, 4), (count // 2,), 0, 1 << 20) % (slack + 1)
    lengths = lengths.at[source_of].add(-moved).at[sink].add(moved)
    members = jnp.searchsorted(jnp.cumsum(lengths), jnp.arange(rows * top), side="right").astype(jnp.int32)
    table = members.reshape(top, rows).T
    table = table[jax.random.permutation(jax.random.fold_in(own, 1), rows)]
    offset_by = jax.random.randint(jax.random.fold_in(own, 2), (rows, 1), 0, top)
    return jnp.take_along_axis(table, (jnp.arange(top)[None, :] + offset_by) % top, axis=1)


def portions_of(number_of, total, reach, skew, full):
    portions = [(1 << 20) // math.isqrt(standing ** skew) + 1 for standing in range(1, number_of + 1)]
    largest = reach if full else min(reach, max(-(-total // number_of), total * portions[0] // sum(portions)))
    least = 1 if total - largest >= number_of - 1 else 0
    holding, spare = [largest] + [least] * (number_of - 1), total - largest - least * (number_of - 1)
    while spare > 0:
        candidates = [i for i in range(1, number_of) if holding[i] < largest] or [i for i in range(1, number_of) if holding[i] < reach]
        mass, remaining = sum([portions[i] for i in candidates]), spare
        for i in candidates:
            extra = min(reach - holding[i], max(1, remaining * portions[i] // mass), spare)
            holding[i] = holding[i] + extra
            spare = spare - extra
    return np.array(holding)


def gaussian(rng, shape, deviation, reach, shards=(), kind=jnp.bfloat16):
    values = jax.random.normal(rng, shape, jnp.float32) * deviation
    if len(shards) > 0:
        values = levels(rng, shape, shards, -0.22, 0.18) * values
    return jnp.clip(values, min=-reach, max=reach).astype(kind)


def setup_inputs(seed: int = 0) -> dict:
    key_list = jax.random.split(jax.random.key(seed), 6)
    query_rows = draw_query_rows(jax.random.fold_in(key_list[5], 71), 0)
    key_rows = draw_key_rows(jax.random.fold_in(key_list[5], 71), 0)
    value_rows = gaussian(key_list[2], (TOKENS, HEADS * DH), 1.0, 6.0, ((0, 256),))
    pick_column_keys = jax.random.split(jax.random.fold_in(key_list[3], 1), N_GRP * HEADS * NLOC // (HEADS * BPD))
    pick_column_turns = jax.random.permutation(jax.random.fold_in(key_list[3], 3), N_GRP * HEADS * NLOC // (HEADS * BPD))
    pick_column = jax.vmap(lambda own, number: assign_block(jax.random.fold_in(key_list[3], 2), own, number, HEADS * BPD, N_GRP, TOPK, CAP, 2))(pick_column_keys, pick_column_turns).reshape((N_GRP, HEADS, NLOC, TOPK))
    pick_back = touch_ends(jax.random.randint(key_list[4], (N_GRP, HEADS, NLOC, TOPK), 0, DBACK), jax.random.fold_in(key_list[4], 1), 0, DBACK - 1).astype(jnp.int32)
    return dict(query_rows=query_rows, key_rows=key_rows, value_rows=value_rows, pick_column=pick_column, pick_back=pick_back)


def finish(scores, value_tiles, einsum_form):
    block_peak = lax.optimization_barrier(jnp.max(scores, axis=-1).astype(jnp.bfloat16)).astype(jnp.float32)
    exp_scores = jnp.exp(scores - block_peak[..., None])
    row_total = lax.optimization_barrier(jnp.sum(exp_scores, axis=-1).astype(jnp.bfloat16)).astype(jnp.float32)
    weights = exp_scores.astype(jnp.bfloat16)
    partial_out = jnp.einsum(einsum_form, weights.astype(jnp.float32), value_tiles.astype(jnp.float32)).astype(jnp.bfloat16)
    return block_peak, row_total, partial_out


def merge_blocks(own_stats, picked, usable):
    own_peak, own_total, own_part = own_stats
    pick_peak, pick_total, pick_part = picked
    pick_peak = jnp.where(usable[..., None], pick_peak, -jnp.inf)
    row_top = jnp.maximum(own_peak, jnp.max(pick_peak, axis=1))
    own_scale = jnp.exp(own_peak - row_top)
    pick_scales = jnp.exp(pick_peak - row_top[:, None, :])
    numerator = own_scale[..., None] * own_part.astype(jnp.float32) + jnp.sum(pick_scales[..., None] * pick_part.astype(jnp.float32), axis=1)
    denominator = own_scale * own_total + jnp.sum(pick_scales * pick_total, axis=1)
    return numerator / denominator[..., None]


def reference(query_rows, key_rows, value_rows, pick_column, pick_back):
    block_count = query_rows.shape[0] // BLK
    per_device = TOK_DEV // BLK
    query_heads = query_rows.reshape(block_count, BLK, HEADS, DH)
    key_heads = key_rows.reshape(block_count, BLK, HEADS, DH)
    value_heads = value_rows.reshape(block_count, BLK, HEADS, DH)
    head_ids = jnp.arange(HEADS, dtype=jnp.int32)
    causal = jnp.arange(BLK)[:, None] >= jnp.arange(BLK)[None, :]
    scaling = DH ** -0.5

    def one_block(block_id):
        column = (block_id // per_device) % N_GRP
        row_id = (block_id // (per_device * N_GRP)) * per_device + block_id % per_device
        pick_cols = pick_column[column, :, row_id, :]
        steps_back = pick_back[column, :, row_id, :]
        local_row = row_id - steps_back - per_device * (pick_cols >= column).astype(jnp.int32)
        usable = local_row >= 0
        local_row = jnp.maximum(local_row, 0)
        chosen = ((local_row // per_device) * N_GRP + pick_cols) * per_device + local_row % per_device
        query_block = query_heads[block_id].astype(jnp.float32)
        own_scores = jnp.einsum("qhd,khd->hqk", query_block, key_heads[block_id].astype(jnp.float32)) * scaling
        own_scores = jnp.where(causal[None], own_scores, -jnp.inf)
        own_stats = finish(own_scores, value_heads[block_id], "hqk,khd->hqd")
        key_sel = key_heads[chosen, :, head_ids[:, None], :]
        value_sel = value_heads[chosen, :, head_ids[:, None], :]
        sel_scores = jnp.einsum("qhd,hjkd->hjqk", query_block, key_sel.astype(jnp.float32)) * scaling
        picked = finish(sel_scores, value_sel, "hjqk,hjkd->hjqd")
        joined = merge_blocks(own_stats, picked, usable)
        return jnp.transpose(joined, (1, 0, 2)).reshape(BLK, HEADS * DH).astype(jnp.bfloat16)

    attended = lax.map(one_block, jnp.arange(block_count, dtype=jnp.int32))
    return attended.reshape(block_count * BLK, HEADS * DH)
```

```python
import functools

import jax
import jax.numpy as jnp
from jax import lax
from jax.experimental import pallas as pl
from jax.experimental.pallas import tpu as pltpu
from jax.sharding import PartitionSpec as P

HEADS = 16
DH = 128
BLK = 512
TOPK = 3
CAP = 4
ROWS = 16
V_PARTS = (64, 64)
GROUP = 8
SHIFT_ORDER = (8, 7, 9, 6, 10, 5, 11, 4, 12, 3, 13, 2, 14, 1, 15, 0)
EXP2_SCALE = DH ** (-0.5) * 1.4426950408889634
VMEM_BYTES = 56 * 1024 * 1024
AXES = ("seq", "grp")


def any_spec():
    return pl.BlockSpec(memory_space=pl.ANY)


def vmem_spec():
    return pl.BlockSpec(memory_space=pltpu.VMEM)


def smem_spec():
    return pl.BlockSpec(memory_space=pltpu.SMEM)


def params():
    return pltpu.CompilerParams(vmem_limit_bytes=VMEM_BYTES)


def cost(flops, moved, exps=0):
    return pl.CostEstimate(flops=flops, bytes_accessed=moved, transcendentals=exps)


def split_heads_kernel(row_ref, head_ref):
    for head in range(HEADS):
        head_ref[head] = row_ref[:, pl.ds(head * DH, DH)]


def split_heads(rows):
    return pl.pallas_call(
        split_heads_kernel,
        grid=(4,),
        in_specs=[pl.BlockSpec((BLK // 4, HEADS * DH), lambda i: (i, 0))],
        out_specs=pl.BlockSpec((HEADS, BLK // 4, DH), lambda i: (0, i, 0)),
        out_shape=jax.ShapeDtypeStruct((HEADS, BLK, DH), jnp.bfloat16),
        compiler_params=params(),
        cost_estimate=cost(0, 4 * BLK * HEADS * DH),
        name="split_heads",
    )(rows)


def put_pieces(seq, held, piece_refs, sem):
    copies = [
        pltpu.make_async_copy(held.at[lax.rem(seq + shift, ROWS)], piece_refs[shift], sem.at[shift])
        for shift in range(ROWS)
    ]
    for copy in copies:
        copy.start()
    for copy in copies:
        copy.wait()


def turn_kernel(seq_ref, value_ref, query_ref, *rest):
    piece_refs, held, sem = rest[:ROWS], rest[ROWS], rest[ROWS + 1]
    for head in range(HEADS):
        columns = pl.ds(head * DH, DH)
        held[head, pl.ds(0, DH), :] = value_ref[:, columns].T
        held[head, pl.ds(DH, DH), :] = query_ref[:, columns].T
    put_pieces(seq_ref[0], held, piece_refs, sem)


def turn(seq, value_rows, query_rows):
    shape = (2 * DH, BLK)
    return pl.pallas_call(
        turn_kernel,
        in_specs=[smem_spec(), vmem_spec(), vmem_spec()],
        out_specs=[any_spec()] * ROWS,
        out_shape=[jax.ShapeDtypeStruct(shape, jnp.bfloat16)] * ROWS,
        scratch_shapes=[
            pltpu.VMEM((ROWS,) + shape, jnp.bfloat16),
            pltpu.SemaphoreType.DMA((ROWS,)),
        ],
        compiler_params=params(),
        cost_estimate=cost(0, 8 * BLK * HEADS * DH),
        name="turn",
    )(seq, value_rows, query_rows)


def nothing_kernel(*refs):
    pass


def after(arrays, earlier):
    count = len(arrays)
    return pl.pallas_call(
        nothing_kernel,
        in_specs=[any_spec()] * (count + len(earlier)),
        out_specs=[any_spec()] * count,
        out_shape=[jax.ShapeDtypeStruct(a.shape, a.dtype) for a in arrays],
        input_output_aliases={i: i for i in range(count)},
        cost_estimate=cost(0, 0),
        name="after",
    )(*arrays, *earlier)


def gather_kernel(parts, pieces, extra, seq_ref, block_ref, *rest):
    if pieces:
        in_refs, rest = rest[:pieces], rest[pieces + extra :]
        all_ref, rest = rest[0], rest[1:]
    else:
        in_refs, rest = rest[:1], rest[1 + extra :]
    send_refs, rest = rest[: len(parts)], rest[len(parts) :]
    if pieces:
        held, in_sem, out_sem = rest
        seq = seq_ref[0]
        copies = [
            pltpu.make_async_copy(
                in_refs[shift], held.at[lax.rem(seq + ROWS - shift, ROWS)], in_sem.at[shift]
            )
            for shift in range(pieces)
        ]
        for copy in copies:
            copy.start()
        for copy in copies:
            copy.wait()
        whole = pltpu.make_async_copy(held, all_ref, in_sem.at[0])
        whole.start()
    else:
        out_sem = rest[0]
        held = in_refs[0]
        whole = None

    start = 0
    for part, (rows, send_ref) in enumerate(zip(parts, send_refs)):

        def send(slot, carry, start=start, rows=rows, send_ref=send_ref, part=part):
            pltpu.make_async_copy(
                held.at[block_ref[slot], pl.ds(start, rows)], send_ref.at[slot], out_sem.at[part]
            ).start()
            return carry

        lax.fori_loop(0, ROWS * CAP, send, 0)
        start += rows
    for part, send_ref in enumerate(send_refs):
        pltpu.make_async_copy(send_ref, send_ref, out_sem.at[part]).wait()
    if whole is not None:
        whole.wait()


def gather(seq, send_block, arrays, parts, name, earlier=()):
    pieces = len(arrays) if len(arrays) > 1 else 0
    rows, columns = arrays[0].shape[-2:]
    sends = [jax.ShapeDtypeStruct((ROWS * CAP, part, columns), jnp.bfloat16) for part in parts]
    scratch = [pltpu.SemaphoreType.DMA((len(parts),))]
    if pieces:
        out_shape = [jax.ShapeDtypeStruct((ROWS, rows, columns), jnp.bfloat16)] + sends
        scratch = [
            pltpu.VMEM((ROWS, rows, columns), jnp.bfloat16),
            pltpu.SemaphoreType.DMA((pieces,)),
        ] + scratch
        in_specs = [any_spec()] * pieces
    else:
        out_shape = sends
        in_specs = [vmem_spec()]
    return pl.pallas_call(
        functools.partial(gather_kernel, parts, pieces, len(earlier)),
        in_specs=[smem_spec(), smem_spec()] + in_specs + [any_spec()] * len(earlier),
        out_specs=[any_spec()] * len(out_shape),
        out_shape=out_shape,
        scratch_shapes=scratch,
        compiler_params=params(),
        cost_estimate=cost(0, 2 * ROWS * (CAP + 1) * sum(parts) * columns),
        name=name,
    )(seq, send_block, *arrays, *earlier)


def weights_kernel(owner_ref, rank_ref, usable_ref, query_ref, own_ref, *rest):
    picks, (weight_ref, inverse_ref, scores) = rest[:TOPK], rest[TOPK:]
    row = pl.program_id(0)
    query = query_ref[0, 0]

    key_at = lax.broadcasted_iota(jnp.int32, (BLK, BLK), 0)
    query_at = lax.broadcasted_iota(jnp.int32, (BLK, BLK), 1)
    own = jnp.dot(own_ref[0], query, preferred_element_type=jnp.float32) * EXP2_SCALE
    own = jnp.where(query_at >= key_at, own, -jnp.inf)
    scores[0] = own
    inverse_ref[0] = jnp.max(own, axis=0, keepdims=True)

    for j in range(TOPK):

        @pl.when(usable_ref[row * TOPK + j] > 0)
        def _(j=j):
            picked = jnp.dot(picks[j][0, 0], query, preferred_element_type=jnp.float32)
            picked = picked * EXP2_SCALE
            scores[1 + j] = picked
            inverse_ref[0] = jnp.maximum(inverse_ref[0], jnp.max(picked, axis=0, keepdims=True))

    top = inverse_ref[0]
    exps = jnp.exp2(scores[0] - top)
    weight_ref[0, 0] = exps.astype(jnp.bfloat16)
    inverse_ref[0] = jnp.sum(exps, axis=0, keepdims=True)
    for j in range(TOPK):
        is_usable = usable_ref[row * TOPK + j] > 0

        @pl.when(is_usable)
        def _(j=j):
            exps = jnp.exp2(scores[1 + j] - top)
            weight_ref[0, 1 + j] = exps.astype(jnp.bfloat16)
            inverse_ref[0] = inverse_ref[0] + jnp.sum(exps, axis=0, keepdims=True)

        @pl.when(jnp.logical_not(is_usable))
        def _(j=j):
            weight_ref[0, 1 + j] = jnp.zeros((BLK, BLK), jnp.bfloat16)

    inverse_ref[0] = 1.0 / inverse_ref[0]


def make_weights(tables, vq_all, own_keys, got_keys):
    owner, rank, usable = tables

    def pick(j):
        def index(r, owner, rank, usable):
            return (owner[r * TOPK + j], rank[r * TOPK + j], 0, 0)

        return pl.BlockSpec((1, 1, BLK, DH), index)

    blocks = ROWS * (1 + TOPK)
    return pl.pallas_call(
        weights_kernel,
        grid_spec=pltpu.PrefetchScalarGridSpec(
            num_scalar_prefetch=3,
            grid=(ROWS,),
            in_specs=[
                pl.BlockSpec((1, 1, DH, BLK), lambda r, *_: (r, 1, 0, 0)),
                pl.BlockSpec((1, BLK, DH), lambda r, *_: (r, 0, 0)),
            ]
            + [pick(j) for j in range(TOPK)],
            out_specs=[
                pl.BlockSpec((1, 1 + TOPK, BLK, BLK), lambda r, *_: (r, 0, 0, 0)),
                pl.BlockSpec((1, 1, BLK), lambda r, *_: (r, 0, 0)),
            ],
            scratch_shapes=[pltpu.VMEM((1 + TOPK, BLK, BLK), jnp.float32)],
        ),
        out_shape=[
            jax.ShapeDtypeStruct((ROWS, 1 + TOPK, BLK, BLK), jnp.bfloat16),
            jax.ShapeDtypeStruct((ROWS, 1, BLK), jnp.float32),
        ],
        compiler_params=params(),
        cost_estimate=cost(
            2 * blocks * BLK * BLK * DH, 2 * blocks * (BLK * BLK + BLK * DH), blocks * BLK * BLK
        ),
        name="make_weights",
    )(
        owner,
        rank,
        usable,
        vq_all.reshape(ROWS, 2, DH, BLK),
        own_keys,
        *([got_keys.reshape(ROWS, CAP, BLK, DH)] * TOPK),
    )


def outputs_kernel(start, rows, steps, owner_ref, rank_ref, row_ref, weight_ref, inverse_ref, *rest):
    own_ref, picks, out_refs = rest[0], rest[1 : 1 + TOPK], rest[1 + TOPK :]
    total = jnp.dot(
        own_ref[0, pl.ds(start, rows), :], weight_ref[0, 0], preferred_element_type=jnp.float32
    )
    for j in range(TOPK):
        total += jnp.dot(picks[j][0, 0], weight_ref[0, 1 + j], preferred_element_type=jnp.float32)
    out = (total * inverse_ref[0]).astype(jnp.bfloat16)
    if len(out_refs) == 1:
        out_refs[0][0] = out
        return
    for step in range(steps):

        @pl.when(pl.program_id(0) == step)
        def _(step=step):
            out_refs[step][...] = out


def make_outputs(
    tables, rows_at, weights, inverse, values, got, start, rows, first, steps, whole=False
):
    owner, rank, _ = tables

    def pick(j):
        def index(step, owner, rank, row_at):
            at = row_at[first + step] * TOPK + j
            return (owner[at], rank[at], 0, 0)

        return pl.BlockSpec((1, 1, rows, BLK), index)

    if whole:
        out_specs = [pl.BlockSpec((1, rows, BLK), lambda i, *_: (i, 0, 0))]
        out_shape = [jax.ShapeDtypeStruct((steps, rows, BLK), jnp.bfloat16)]
    else:
        out_specs = [pl.BlockSpec((rows, BLK), lambda i, *_: (0, 0))] * steps
        out_shape = [jax.ShapeDtypeStruct((rows, BLK), jnp.bfloat16)] * steps
    blocks = steps * (1 + TOPK)
    return pl.pallas_call(
        functools.partial(outputs_kernel, start, rows, steps),
        grid_spec=pltpu.PrefetchScalarGridSpec(
            num_scalar_prefetch=3,
            grid=(steps,),
            in_specs=[
                pl.BlockSpec(
                    (1, 1 + TOPK, BLK, BLK), lambda i, o, r, at: (at[first + i], 0, 0, 0)
                ),
                pl.BlockSpec((1, 1, BLK), lambda i, o, r, at: (at[first + i], 0, 0)),
                pl.BlockSpec((1, DH, BLK), lambda i, o, r, at: (at[first + i], 0, 0)),
            ]
            + [pick(j) for j in range(TOPK)],
            out_specs=out_specs,
        ),
        out_shape=out_shape,
        compiler_params=params(),
        cost_estimate=cost(2 * blocks * BLK * BLK * 128, 2 * blocks * BLK * (BLK + rows)),
        name="make_outputs",
    )(owner, rank, rows_at, weights, inverse, values, *([got.reshape(ROWS, CAP, rows, BLK)] * TOPK))


def finish_kernel(parts, seq_ref, *rest):
    count = (len(parts) - 1) * ROWS
    pieces, (last_ref, out_ref, held, sem) = rest[:count], rest[count:]
    seq = seq_ref[0]
    copies = []
    start = 0
    for part, rows in enumerate(parts[:-1]):
        for shift in range(ROWS):
            head = lax.rem(seq + ROWS - shift, ROWS)
            at = part * ROWS + shift
            copies.append(
                pltpu.make_async_copy(pieces[at], held.at[head, pl.ds(start, rows)], sem.at[at])
            )
        start += rows
    for head in range(HEADS):
        copies.append(
            pltpu.make_async_copy(
                last_ref.at[head], held.at[head, pl.ds(start, parts[-1])], sem.at[count + head]
            )
        )
    for copy in copies:
        copy.start()
    for copy in copies:
        copy.wait()
    for head in range(HEADS):
        out_ref[:, pl.ds(head * DH, DH)] = held[head].T


def finish(seq, pieces, last, parts):
    count = (len(parts) - 1) * ROWS
    return pl.pallas_call(
        functools.partial(finish_kernel, parts),
        in_specs=[smem_spec()] + [any_spec()] * (count + 1),
        out_specs=vmem_spec(),
        out_shape=jax.ShapeDtypeStruct((BLK, HEADS * DH), jnp.bfloat16),
        scratch_shapes=[
            pltpu.VMEM((HEADS, DH, BLK), jnp.bfloat16),
            pltpu.SemaphoreType.DMA((count + HEADS,)),
        ],
        compiler_params=params(),
        cost_estimate=cost(0, 4 * BLK * HEADS * DH),
        name="finish",
    )(seq, *pieces, last)


def shift_pairs(shift):
    seq_count, grp_count = lax.axis_size("seq"), lax.axis_size("grp")
    return [
        (s * grp_count + g, (s + shift) % seq_count * grp_count + g)
        for s in range(seq_count)
        for g in range(grp_count)
    ]


def along_seq(pieces):
    moved = dict(pieces)
    for shift in SHIFT_ORDER:
        if shift and shift in pieces:
            moved[shift] = lax.ppermute(pieces[shift], AXES, shift_pairs(shift))
    return moved


def in_order(moved):
    return [moved[shift] for shift in range(ROWS)]


def exchange(array, axis):
    return lax.all_to_all(array, axis, split_axis=0, concat_axis=0, tiled=True)


def routes(pick_column, pick_back):
    seq, grp = lax.axis_index("seq"), lax.axis_index("grp")
    requests = ROWS * TOPK
    target = lax.dynamic_index_in_dim(pick_column, seq, 1, keepdims=False).reshape(-1, requests)
    back = lax.dynamic_index_in_dim(pick_back, seq, 1, keepdims=False).reshape(-1, requests)
    column = jnp.arange(target.shape[0], dtype=jnp.int32)[:, None]
    row = (jnp.arange(requests, dtype=jnp.int32) // TOPK)[None, :]
    local_row = row - back - (target >= column).astype(jnp.int32)
    at = jnp.arange(requests, dtype=jnp.int32)
    earlier = at[:, None] > at[None, :]
    hits = target == grp
    place = jnp.sum(hits[:, None, :] & earlier[None], axis=2, dtype=jnp.int32)
    chosen = hits[:, None, :] & (
        place[:, None, :] == jnp.arange(CAP, dtype=jnp.int32)[None, :, None]
    )
    send_block = jnp.sum(
        jnp.where(chosen, jnp.maximum(local_row, 0)[:, None, :], 0), axis=2, dtype=jnp.int32
    ).reshape(-1)
    owner = lax.dynamic_index_in_dim(target, grp, 0, keepdims=False)
    rank = jnp.sum((owner[:, None] == owner[None, :]) & earlier, axis=1, dtype=jnp.int32)
    usable = (lax.dynamic_index_in_dim(local_row, grp, 0, keepdims=False) >= 0).astype(jnp.int32)
    return send_block, (owner, rank, usable)


def body(query_rows, key_rows, value_rows, pick_column, pick_back):
    seq = lax.axis_index("seq").astype(jnp.int32).reshape(1)
    own_keys = exchange(split_heads(key_rows), "seq")
    pieces = turn(seq, value_rows, query_rows)
    send_block, tables = routes(pick_column, pick_back)
    (send_keys,) = gather(
        seq, send_block, [own_keys], (BLK,), "gather_keys", earlier=[pieces[0]]
    )
    got_keys = exchange(send_keys, "grp")

    pieces = along_seq(dict(enumerate(after(pieces, [send_keys]))))
    vq_all, *sends = gather(seq, send_block, in_order(pieces), V_PARTS, "gather_values")
    weights, inverse = make_weights(tables, vq_all, own_keys, got_keys)

    rows_at = (seq + jnp.asarray(SHIFT_ORDER, jnp.int32)) % ROWS
    straight = jnp.arange(ROWS, dtype=jnp.int32)
    ended, start, earlier = [], 0, [got_keys]
    for part, rows in enumerate(V_PARTS):
        (send,) = after([sends[part]], earlier)
        got = exchange(send, "grp")
        earlier = [got, inverse]
        common = (weights, inverse, vq_all, got, start, rows)
        if part == len(V_PARTS) - 1:
            (outs,) = make_outputs(tables, straight, *common, 0, ROWS, whole=True)
            last = exchange(outs, "seq")
        else:
            moved = {}
            for first in range(0, ROWS, GROUP):
                outs = make_outputs(tables, rows_at, *common, first, GROUP)
                moved.update(along_seq(dict(zip(SHIFT_ORDER[first : first + GROUP], outs))))
            ended += in_order(moved)
        start += rows
    return finish(seq, ended, last, V_PARTS)


def solution(mesh):
    return jax.shard_map(
        body,
        mesh=mesh,
        in_specs=(P(AXES, None), P(AXES, None), P(AXES, None), P(), P()),
        out_specs=P(AXES, None),
        check_vma=False,
    )
```

```python
import functools

import jax
import jax.numpy as jnp
from jax import lax
from jax.experimental import pallas as pl
from jax.experimental.pallas import tpu as pltpu
from jax.sharding import PartitionSpec as P

HEADS = 16
DH = 128
BLK = 512
TOPK = 3
CAP = 4
ROWS = 16
CHIPS = ROWS // 2
K_FIRST = 192
V_PARTS = (64, 64)
CHIP_ORDER = (4, 3, 5, 2, 6, 1, 7)
EXP2_SCALE = DH ** (-0.5) * 1.4426950408889634
VMEM_BYTES = 56 * 1024 * 1024
AXES = ("seq", "grp")


def any_spec():
    return pl.BlockSpec(memory_space=pl.ANY)


def vmem_spec():
    return pl.BlockSpec(memory_space=pltpu.VMEM)


def smem_spec():
    return pl.BlockSpec(memory_space=pltpu.SMEM)


def params():
    return pltpu.CompilerParams(vmem_limit_bytes=VMEM_BYTES)


def cost(flops, moved, exps=0):
    return pl.CostEstimate(flops=flops, bytes_accessed=moved, transcendentals=exps)


def split_first_kernel(key_ref, first_ref):
    for head in range(HEADS):
        first_ref[head] = key_ref[:, pl.ds(head * DH, DH)]


def split_first(key_rows):
    return pl.pallas_call(
        split_first_kernel,
        grid=(1,),
        in_specs=[pl.BlockSpec((K_FIRST, HEADS * DH), lambda i: (0, 0))],
        out_specs=pl.BlockSpec((HEADS, K_FIRST, DH), lambda i: (0, 0, 0)),
        out_shape=jax.ShapeDtypeStruct((HEADS, K_FIRST, DH), jnp.bfloat16),
        compiler_params=params(),
        cost_estimate=cost(0, 4 * K_FIRST * HEADS * DH),
        name="split_first",
    )(key_rows)


def run_copies(copies):
    for copy in copies:
        copy.start()
    for copy in copies:
        copy.wait()


def same_core(seq, chip_shift):
    core = lax.rem(seq, 2)
    at = lax.rem(seq + 2 * chip_shift + ROWS, ROWS)
    return at, at + 1 - 2 * core


def put_heads(seq, held, mine_ref, other_ref, sem):
    copies = []
    for chip in range(CHIPS):
        mine, other = same_core(seq, chip)
        copies.append(pltpu.make_async_copy(held.at[mine], mine_ref.at[chip], sem.at[2 * chip]))
        copies.append(
            pltpu.make_async_copy(held.at[other], other_ref.at[chip], sem.at[2 * chip + 1])
        )
    run_copies(copies)


def split_rest_kernel(seq_ref, key_ref, earlier_ref, mine_ref, other_ref, held, sem):
    for head in range(HEADS):
        held[head] = key_ref[pl.ds(K_FIRST, BLK - K_FIRST), pl.ds(head * DH, DH)]
    put_heads(seq_ref[0], held, mine_ref, other_ref, sem)


def turn_kernel(seq_ref, row_ref, earlier_ref, mine_ref, other_ref, held, sem):
    for head in range(HEADS):
        held[head] = row_ref[:, pl.ds(head * DH, DH)].T
    put_heads(seq_ref[0], held, mine_ref, other_ref, sem)


def by_core(kernel, seq, array, earlier, shape, name):
    return pl.pallas_call(
        kernel,
        in_specs=[smem_spec(), vmem_spec(), any_spec()],
        out_specs=[any_spec()] * 2,
        out_shape=[jax.ShapeDtypeStruct((CHIPS,) + shape, jnp.bfloat16)] * 2,
        scratch_shapes=[
            pltpu.VMEM((ROWS,) + shape, jnp.bfloat16),
            pltpu.SemaphoreType.DMA((ROWS,)),
        ],
        compiler_params=params(),
        cost_estimate=cost(0, 4 * ROWS * shape[0] * shape[1]),
        name=name,
    )(seq, array, earlier)


def pack_kernel(mine_ref, other_ref, *rest):
    piece_refs, sem = rest[:CHIPS], rest[CHIPS]
    copies = []
    for chip in range(CHIPS):
        copies.append(
            pltpu.make_async_copy(mine_ref.at[chip], piece_refs[chip].at[0], sem.at[2 * chip])
        )
        copies.append(
            pltpu.make_async_copy(other_ref.at[chip], piece_refs[chip].at[1], sem.at[2 * chip + 1])
        )
    run_copies(copies)


def pack(mine, other, name):
    shape = mine.shape[1:]
    return pl.pallas_call(
        pack_kernel,
        in_specs=[any_spec()] * 2,
        out_specs=[any_spec()] * CHIPS,
        out_shape=[jax.ShapeDtypeStruct((2,) + shape, jnp.bfloat16)] * CHIPS,
        scratch_shapes=[pltpu.SemaphoreType.DMA((ROWS,))],
        compiler_params=params(),
        cost_estimate=cost(0, 8 * CHIPS * shape[0] * shape[1]),
        name=name,
    )(mine, other)


def to_rows(seq, piece_refs, held, sem, start=0, rows=None):
    copies = []
    for chip in range(CHIPS):
        for which, row in enumerate(same_core(seq, -chip)):
            place = held.at[row] if rows is None else held.at[row, pl.ds(start, rows)]
            copies.append(
                pltpu.make_async_copy(piece_refs[chip].at[which], place, sem.at[2 * chip + which])
            )
    return copies


def nothing_kernel(*refs):
    pass


def after(arrays, earlier):
    count = len(arrays)
    return pl.pallas_call(
        nothing_kernel,
        in_specs=[any_spec()] * (count + len(earlier)),
        out_specs=[any_spec()] * count,
        out_shape=[jax.ShapeDtypeStruct(a.shape, a.dtype) for a in arrays],
        input_output_aliases={i: i for i in range(count)},
        cost_estimate=cost(0, 0),
        name="after",
    )(*arrays, *earlier)


def gather_kernel(parts, pieces, extra, seq_ref, block_ref, *rest):
    in_refs, rest = rest[: max(pieces, 1)], rest[max(pieces, 1) + extra :]
    if pieces:
        all_ref, rest = rest[0], rest[1:]
    send_refs, rest = rest[: len(parts)], rest[len(parts) :]
    if pieces:
        held, in_sem, out_sem = rest
        run_copies(to_rows(seq_ref[0], in_refs, held, in_sem))
        whole = pltpu.make_async_copy(held, all_ref, in_sem.at[0])
        whole.start()
    else:
        held, out_sem, whole = in_refs[0], rest[0], None

    start = 0
    for part, (rows, send_ref) in enumerate(zip(parts, send_refs)):

        def send(slot, carry, start=start, rows=rows, send_ref=send_ref, part=part):
            pltpu.make_async_copy(
                held.at[block_ref[slot], pl.ds(start, rows)], send_ref.at[slot], out_sem.at[part]
            ).start()
            return carry

        lax.fori_loop(0, ROWS * CAP, send, 0)
        start += rows
    for part, send_ref in enumerate(send_refs):
        pltpu.make_async_copy(send_ref, send_ref, out_sem.at[part]).wait()
    if whole is not None:
        whole.wait()


def gather(seq, send_block, arrays, parts, name, earlier=()):
    pieces = len(arrays) if len(arrays) > 1 else 0
    rows, columns = arrays[0].shape[-2:]
    out_shape = [jax.ShapeDtypeStruct((ROWS * CAP, part, columns), jnp.bfloat16) for part in parts]
    scratch = [pltpu.SemaphoreType.DMA((len(parts),))]
    in_specs = [vmem_spec()]
    if pieces:
        out_shape = [jax.ShapeDtypeStruct((ROWS, rows, columns), jnp.bfloat16)] + out_shape
        scratch = [
            pltpu.VMEM((ROWS, rows, columns), jnp.bfloat16),
            pltpu.SemaphoreType.DMA((ROWS,)),
        ] + scratch
        in_specs = [any_spec()] * pieces
    return pl.pallas_call(
        functools.partial(gather_kernel, parts, pieces, len(earlier)),
        in_specs=[smem_spec(), smem_spec()] + in_specs + [any_spec()] * len(earlier),
        out_specs=[any_spec()] * len(out_shape),
        out_shape=out_shape,
        scratch_shapes=scratch,
        compiler_params=params(),
        cost_estimate=cost(0, 2 * ROWS * (CAP + 1) * sum(parts) * columns),
        name=name,
    )(seq, send_block, *arrays, *earlier)


def weights_kernel(owner_ref, rank_ref, usable_ref, seq_ref, own_a, own_b, *rest):
    picks, rest = rest[: 2 * TOPK], rest[2 * TOPK :]
    pieces, (weight_ref, inverse_ref, queries, scores, sem) = rest[:CHIPS], rest[CHIPS:]
    row = pl.program_id(0)

    @pl.when(row == 0)
    def _():
        run_copies(to_rows(seq_ref[0], pieces, queries, sem))

    query = queries[row]
    key_pairs = [(own_a[0], own_b[0])] + [
        (picks[2 * j][0, 0], picks[2 * j + 1][0, 0]) for j in range(TOPK)
    ]

    def raw(pair):
        upper = jnp.dot(pair[0], query, preferred_element_type=jnp.float32)
        lower = jnp.dot(pair[1], query, preferred_element_type=jnp.float32)
        return upper * EXP2_SCALE, lower * EXP2_SCALE

    key_at = lax.broadcasted_iota(jnp.int32, (BLK, BLK), 0)
    query_at = lax.broadcasted_iota(jnp.int32, (BLK, BLK), 1)
    upper, lower = raw(key_pairs[0])
    own = jnp.where(query_at >= key_at, jnp.concatenate([upper, lower], axis=0), -jnp.inf)
    scores[0] = own
    top = jnp.max(own, axis=0, keepdims=True)
    inverse_ref[0] = top

    for j in range(TOPK):

        @pl.when(usable_ref[row * TOPK + j] > 0)
        def _(j=j):
            upper, lower = raw(key_pairs[1 + j])
            scores[1 + j, pl.ds(0, K_FIRST), :] = upper
            scores[1 + j, pl.ds(K_FIRST, BLK - K_FIRST), :] = lower
            inverse_ref[0] = jnp.maximum(
                inverse_ref[0],
                jnp.maximum(
                    jnp.max(upper, axis=0, keepdims=True), jnp.max(lower, axis=0, keepdims=True)
                ),
            )

    top = inverse_ref[0]
    exps = jnp.exp2(scores[0] - top)
    weight_ref[0, 0] = exps.astype(jnp.bfloat16)
    inverse_ref[0] = jnp.sum(exps, axis=0, keepdims=True)
    for j in range(TOPK):
        is_usable = usable_ref[row * TOPK + j] > 0

        @pl.when(is_usable)
        def _(j=j):
            exps = jnp.exp2(scores[1 + j] - top)
            weight_ref[0, 1 + j] = exps.astype(jnp.bfloat16)
            inverse_ref[0] = inverse_ref[0] + jnp.sum(exps, axis=0, keepdims=True)

        @pl.when(jnp.logical_not(is_usable))
        def _(j=j):
            weight_ref[0, 1 + j] = jnp.zeros((BLK, BLK), jnp.bfloat16)

    inverse_ref[0] = 1.0 / inverse_ref[0]


def make_weights(tables, seq, query_pieces, own_a, own_b, got_a, got_b):
    owner, rank, usable = tables
    rest = BLK - K_FIRST

    def pick(j, rows):
        return pl.BlockSpec(
            (1, 1, rows, DH),
            lambda r, owner, rank, usable, seq, j=j: (
                owner[r * TOPK + j],
                rank[r * TOPK + j],
                0,
                0,
            ),
        )

    in_specs = [
        pl.BlockSpec((1, K_FIRST, DH), lambda r, *_: (r, 0, 0)),
        pl.BlockSpec((1, rest, DH), lambda r, *_: (r, 0, 0)),
    ]
    args = [own_a, own_b]
    for j in range(TOPK):
        in_specs += [pick(j, K_FIRST), pick(j, rest)]
        args += [got_a.reshape(ROWS, CAP, K_FIRST, DH), got_b.reshape(ROWS, CAP, rest, DH)]
    in_specs += [any_spec()] * CHIPS
    blocks = ROWS * (1 + TOPK)
    return pl.pallas_call(
        weights_kernel,
        grid_spec=pltpu.PrefetchScalarGridSpec(
            num_scalar_prefetch=4,
            grid=(ROWS,),
            in_specs=in_specs,
            out_specs=[
                pl.BlockSpec((1, 1 + TOPK, BLK, BLK), lambda r, *_: (r, 0, 0, 0)),
                pl.BlockSpec((1, 1, BLK), lambda r, *_: (r, 0, 0)),
            ],
            scratch_shapes=[
                pltpu.VMEM((ROWS, DH, BLK), jnp.bfloat16),
                pltpu.VMEM((1 + TOPK, BLK, BLK), jnp.float32),
                pltpu.SemaphoreType.DMA((ROWS,)),
            ],
        ),
        out_shape=[
            jax.ShapeDtypeStruct((ROWS, 1 + TOPK, BLK, BLK), jnp.bfloat16),
            jax.ShapeDtypeStruct((ROWS, 1, BLK), jnp.float32),
        ],
        compiler_params=params(),
        cost_estimate=cost(
            2 * blocks * BLK * BLK * DH, 2 * blocks * (BLK * BLK + BLK * DH), blocks * BLK * BLK
        ),
        name="make_weights",
    )(owner, rank, usable, seq, *args, *query_pieces)


def outputs_kernel(start, rows, owner_ref, rank_ref, row_ref, weight_ref, inverse_ref, *rest):
    own_ref, picks, out_ref = rest[0], rest[1 : 1 + TOPK], rest[1 + TOPK]
    total = jnp.dot(
        own_ref[0, pl.ds(start, rows), :], weight_ref[0, 0], preferred_element_type=jnp.float32
    )
    for j in range(TOPK):
        total += jnp.dot(picks[j][0, 0], weight_ref[0, 1 + j], preferred_element_type=jnp.float32)
    out_ref[0] = (total * inverse_ref[0]).astype(jnp.bfloat16)


def make_outputs(tables, rows_at, weights, inverse, values, got, start, rows):
    owner, rank, _ = tables
    steps = rows_at.shape[0]

    def pick(j):
        def index(step, owner, rank, row_at):
            at = row_at[step] * TOPK + j
            return (owner[at], rank[at], 0, 0)

        return pl.BlockSpec((1, 1, rows, BLK), index)

    blocks = steps * (1 + TOPK)
    return pl.pallas_call(
        functools.partial(outputs_kernel, start, rows),
        grid_spec=pltpu.PrefetchScalarGridSpec(
            num_scalar_prefetch=3,
            grid=(steps,),
            in_specs=[
                pl.BlockSpec((1, 1 + TOPK, BLK, BLK), lambda i, o, r, at: (at[i], 0, 0, 0)),
                pl.BlockSpec((1, 1, BLK), lambda i, o, r, at: (at[i], 0, 0)),
                pl.BlockSpec((1, DH, BLK), lambda i, o, r, at: (at[i], 0, 0)),
            ]
            + [pick(j) for j in range(TOPK)],
            out_specs=pl.BlockSpec((1, rows, BLK), lambda i, *_: (i, 0, 0)),
        ),
        out_shape=jax.ShapeDtypeStruct((steps, rows, BLK), jnp.bfloat16),
        compiler_params=params(),
        cost_estimate=cost(2 * blocks * BLK * BLK * 128, 2 * blocks * BLK * (BLK + rows)),
        name="make_outputs",
    )(owner, rank, rows_at, weights, inverse, values, *([got.reshape(ROWS, CAP, rows, BLK)] * TOPK))


def finish_kernel(parts, seq_ref, *rest):
    pieces, (last_ref, out_ref, held, sem) = rest[:CHIPS], rest[CHIPS:]
    copies = to_rows(seq_ref[0], pieces, held, sem, 0, parts[0])
    for head in range(HEADS):
        copies.append(
            pltpu.make_async_copy(
                last_ref.at[head], held.at[head, pl.ds(parts[0], parts[1])], sem.at[ROWS + head]
            )
        )
    run_copies(copies)
    for head in range(HEADS):
        out_ref[:, pl.ds(head * DH, DH)] = held[head].T


def finish(seq, pieces, last, parts):
    return pl.pallas_call(
        functools.partial(finish_kernel, parts),
        in_specs=[smem_spec()] + [any_spec()] * (CHIPS + 1),
        out_specs=vmem_spec(),
        out_shape=jax.ShapeDtypeStruct((BLK, HEADS * DH), jnp.bfloat16),
        scratch_shapes=[
            pltpu.VMEM((HEADS, DH, BLK), jnp.bfloat16),
            pltpu.SemaphoreType.DMA((ROWS + HEADS,)),
        ],
        compiler_params=params(),
        cost_estimate=cost(0, 4 * BLK * HEADS * DH),
        name="finish",
    )(seq, *pieces, last)


def permute_seq(array, place):
    seq_count, grp_count = lax.axis_size("seq"), lax.axis_size("grp")
    pairs = [
        (s * grp_count + g, place(s) % seq_count * grp_count + g)
        for s in range(seq_count)
        for g in range(grp_count)
    ]
    return lax.ppermute(array, AXES, pairs)


def swap_cores(array):
    return permute_seq(array, lambda s: s ^ 1)


def along_chips(pieces):
    moved = {0: pieces[0]}
    for chip in CHIP_ORDER:
        moved[chip] = permute_seq(pieces[chip], lambda s, chip=chip: s + 2 * chip)
    return [moved[chip] for chip in range(CHIPS)]


def exchange(array, axis):
    return lax.all_to_all(array, axis, split_axis=0, concat_axis=0, tiled=True)


def routes(pick_column, pick_back):
    seq, grp = lax.axis_index("seq"), lax.axis_index("grp")
    requests = ROWS * TOPK
    target = lax.dynamic_index_in_dim(pick_column, seq, 1, keepdims=False).reshape(-1, requests)
    back = lax.dynamic_index_in_dim(pick_back, seq, 1, keepdims=False).reshape(-1, requests)
    column = jnp.arange(target.shape[0], dtype=jnp.int32)[:, None]
    row = (jnp.arange(requests, dtype=jnp.int32) // TOPK)[None, :]
    local_row = row - back - (target >= column).astype(jnp.int32)
    at = jnp.arange(requests, dtype=jnp.int32)
    earlier = at[:, None] > at[None, :]
    hits = target == grp
    place = jnp.sum(hits[:, None, :] & earlier[None], axis=2, dtype=jnp.int32)
    chosen = hits[:, None, :] & (
        place[:, None, :] == jnp.arange(CAP, dtype=jnp.int32)[None, :, None]
    )
    send_block = jnp.sum(
        jnp.where(chosen, jnp.maximum(local_row, 0)[:, None, :], 0), axis=2, dtype=jnp.int32
    ).reshape(-1)
    owner = lax.dynamic_index_in_dim(target, grp, 0, keepdims=False)
    rank = jnp.sum((owner[:, None] == owner[None, :]) & earlier, axis=1, dtype=jnp.int32)
    usable = (lax.dynamic_index_in_dim(local_row, grp, 0, keepdims=False) >= 0).astype(jnp.int32)
    return send_block, (owner, rank, usable)


def body(query_rows, key_rows, value_rows, pick_column, pick_back):
    seq = lax.axis_index("seq").astype(jnp.int32).reshape(1)
    rest = BLK - K_FIRST
    key_first = split_first(key_rows)
    own_a = exchange(key_first, "seq")
    mine, other = by_core(split_rest_kernel, seq, key_rows, key_first, (rest, DH), "split_rest")
    key_pieces = pack(mine, swap_cores(other), "pack_keys")
    mine, other = by_core(turn_kernel, seq, value_rows, key_first, (DH, BLK), "turn_values")
    value_pieces = pack(mine, swap_cores(other), "pack_values")
    mine, other = by_core(turn_kernel, seq, query_rows, key_first, (DH, BLK), "turn_queries")
    query_pieces = pack(mine, swap_cores(other), "pack_queries")

    send_block, tables = routes(pick_column, pick_back)
    ready = [key_pieces[0], value_pieces[0]]
    (send_a,) = gather(seq, send_block, [own_a], (K_FIRST,), "gather_a", earlier=ready)
    got_a = exchange(send_a, "grp")

    key_pieces = along_chips(after(key_pieces, [send_a]))
    own_b, send_b = gather(seq, send_block, key_pieces, (rest,), "gather_b")
    (send_b,) = after([send_b], [got_a])
    got_b = exchange(send_b, "grp")

    value_pieces = along_chips(after(value_pieces, [key_pieces[CHIP_ORDER[4]]]))
    values, *sends = gather(seq, send_block, value_pieces, V_PARTS, "gather_values")
    query_pieces = along_chips(after(query_pieces, [value_pieces[CHIP_ORDER[4]]]))
    weights, inverse = make_weights(tables, seq, query_pieces, own_a, own_b, got_a, got_b)

    (send,) = after(sends[:1], [got_b] + [query_pieces[chip] for chip in CHIP_ORDER[:2]])
    got = exchange(send, "grp")
    (send,) = after(sends[1:], [got, inverse])
    chips = jnp.arange(CHIPS, dtype=jnp.int32)
    same = (seq + 2 * chips) % ROWS
    opposite = same ^ 1
    first = (weights, inverse, values, got, 0, V_PARTS[0])
    other = swap_cores(make_outputs(tables, opposite, *first))
    mine = make_outputs(tables, same, *first)
    pieces = along_chips(pack(mine, other, "pack_outputs"))

    (got,) = after([exchange(send, "grp")], pieces[1:])
    second = (weights, inverse, values, got, V_PARTS[0], V_PARTS[1])
    outs = make_outputs(tables, jnp.arange(ROWS, dtype=jnp.int32), *second)
    return finish(seq, pieces, exchange(outs, "seq"), V_PARTS)


def solution(mesh):
    return jax.shard_map(
        body,
        mesh=mesh,
        in_specs=(P(AXES, None), P(AXES, None), P(AXES, None), P(), P()),
        out_specs=P(AXES, None),
        check_vma=False,
    )
```

```python
import functools

import jax
import jax.numpy as jnp
from jax import lax
from jax.experimental import pallas as pl
from jax.experimental.pallas import tpu as pltpu
from jax.sharding import PartitionSpec as P

HEADS = 16
DH = 128
BLK = 512
TOPK = 3
CAP = 4
ROWS = 16
CHIPS = ROWS // 2
K_FIRST = 192
V_PARTS = (80, 48)
CHIP_ORDER = (4, 3, 5, 2, 6, 1, 7)
EXP2_SCALE = DH ** (-0.5) * 1.4426950408889634
VMEM_BYTES = 56 * 1024 * 1024
AXES = ("seq", "grp")


def any_spec():
    return pl.BlockSpec(memory_space=pl.ANY)


def vmem_spec():
    return pl.BlockSpec(memory_space=pltpu.VMEM)


def smem_spec():
    return pl.BlockSpec(memory_space=pltpu.SMEM)


def params():
    return pltpu.CompilerParams(vmem_limit_bytes=VMEM_BYTES)


def cost(flops, moved, exps=0):
    return pl.CostEstimate(flops=flops, bytes_accessed=moved, transcendentals=exps)


def split_first_kernel(key_ref, first_ref):
    for head in range(HEADS):
        first_ref[head] = key_ref[:, pl.ds(head * DH, DH)]


def split_first(key_rows):
    return pl.pallas_call(
        split_first_kernel,
        grid=(1,),
        in_specs=[pl.BlockSpec((K_FIRST, HEADS * DH), lambda i: (0, 0))],
        out_specs=pl.BlockSpec((HEADS, K_FIRST, DH), lambda i: (0, 0, 0)),
        out_shape=jax.ShapeDtypeStruct((HEADS, K_FIRST, DH), jnp.bfloat16),
        compiler_params=params(),
        cost_estimate=cost(0, 4 * K_FIRST * HEADS * DH),
        name="split_first",
    )(key_rows)


def run_copies(copies):
    for copy in copies:
        copy.start()
    for copy in copies:
        copy.wait()


def same_core(seq, chip_shift):
    core = lax.rem(seq, 2)
    at = lax.rem(seq + 2 * chip_shift + ROWS, ROWS)
    return at, at + 1 - 2 * core


def put_heads(seq, held, mine_ref, other_ref, sem):
    copies = []
    for chip in range(CHIPS):
        mine, other = same_core(seq, chip)
        copies.append(pltpu.make_async_copy(held.at[mine], mine_ref.at[chip], sem.at[2 * chip]))
        copies.append(
            pltpu.make_async_copy(held.at[other], other_ref.at[chip], sem.at[2 * chip + 1])
        )
    run_copies(copies)


def split_rest_kernel(seq_ref, key_ref, earlier_ref, mine_ref, other_ref, held, sem):
    for head in range(HEADS):
        held[head] = key_ref[pl.ds(K_FIRST, BLK - K_FIRST), pl.ds(head * DH, DH)]
    put_heads(seq_ref[0], held, mine_ref, other_ref, sem)


def turn_kernel(seq_ref, row_ref, earlier_ref, mine_ref, other_ref, held, sem):
    for head in range(HEADS):
        held[head] = row_ref[:, pl.ds(head * DH, DH)].T
    put_heads(seq_ref[0], held, mine_ref, other_ref, sem)


def by_core(kernel, seq, array, earlier, shape, name):
    return pl.pallas_call(
        kernel,
        in_specs=[smem_spec(), vmem_spec(), any_spec()],
        out_specs=[any_spec()] * 2,
        out_shape=[jax.ShapeDtypeStruct((CHIPS,) + shape, jnp.bfloat16)] * 2,
        scratch_shapes=[
            pltpu.VMEM((ROWS,) + shape, jnp.bfloat16),
            pltpu.SemaphoreType.DMA((ROWS,)),
        ],
        compiler_params=params(),
        cost_estimate=cost(0, 4 * ROWS * shape[0] * shape[1]),
        name=name,
    )(seq, array, earlier)


def pack_kernel(mine_ref, other_ref, *rest):
    piece_refs, sem = rest[:CHIPS], rest[CHIPS]
    copies = []
    for chip in range(CHIPS):
        copies.append(
            pltpu.make_async_copy(mine_ref.at[chip], piece_refs[chip].at[0], sem.at[2 * chip])
        )
        copies.append(
            pltpu.make_async_copy(other_ref.at[chip], piece_refs[chip].at[1], sem.at[2 * chip + 1])
        )
    run_copies(copies)


def pack(mine, other, name):
    shape = mine.shape[1:]
    return pl.pallas_call(
        pack_kernel,
        in_specs=[vmem_spec()] * 2,
        out_specs=[any_spec()] * CHIPS,
        out_shape=[jax.ShapeDtypeStruct((2,) + shape, jnp.bfloat16)] * CHIPS,
        scratch_shapes=[pltpu.SemaphoreType.DMA((ROWS,))],
        compiler_params=params(),
        cost_estimate=cost(0, 8 * CHIPS * shape[0] * shape[1]),
        name=name,
    )(mine, other)


def to_rows(seq, piece_refs, held, sem, start=0, rows=None):
    copies = []
    for chip in range(CHIPS):
        for which, row in enumerate(same_core(seq, -chip)):
            place = held.at[row] if rows is None else held.at[row, pl.ds(start, rows)]
            copies.append(
                pltpu.make_async_copy(piece_refs[chip].at[which], place, sem.at[2 * chip + which])
            )
    return copies


def nothing_kernel(*refs):
    pass


def after(arrays, earlier):
    count = len(arrays)
    return pl.pallas_call(
        nothing_kernel,
        in_specs=[any_spec()] * (count + len(earlier)),
        out_specs=[any_spec()] * count,
        out_shape=[jax.ShapeDtypeStruct(a.shape, a.dtype) for a in arrays],
        input_output_aliases={i: i for i in range(count)},
        cost_estimate=cost(0, 0),
        name="after",
    )(*arrays, *earlier)


def gather_kernel(parts, pieces, extra, seq_ref, block_ref, *rest):
    in_refs, rest = rest[: max(pieces, 1)], rest[max(pieces, 1) + extra :]
    if pieces:
        all_ref, rest = rest[0], rest[1:]
    send_refs, rest = rest[: len(parts)], rest[len(parts) :]
    if pieces:
        held, in_sem, out_sem = rest
        run_copies(to_rows(seq_ref[0], in_refs, held, in_sem))
        whole = pltpu.make_async_copy(held, all_ref, in_sem.at[0])
        whole.start()
    else:
        held, out_sem, whole = in_refs[0], rest[0], None

    start = 0
    for part, (rows, send_ref) in enumerate(zip(parts, send_refs)):

        def send(slot, carry, start=start, rows=rows, send_ref=send_ref, part=part):
            pltpu.make_async_copy(
                held.at[block_ref[slot], pl.ds(start, rows)], send_ref.at[slot], out_sem.at[part]
            ).start()
            return carry

        lax.fori_loop(0, ROWS * CAP, send, 0)
        start += rows
    for part, send_ref in enumerate(send_refs):
        pltpu.make_async_copy(send_ref, send_ref, out_sem.at[part]).wait()
    if whole is not None:
        whole.wait()


def gather(seq, send_block, arrays, parts, name, earlier=()):
    pieces = len(arrays) if len(arrays) > 1 else 0
    rows, columns = arrays[0].shape[-2:]
    out_shape = [jax.ShapeDtypeStruct((ROWS * CAP, part, columns), jnp.bfloat16) for part in parts]
    scratch = [pltpu.SemaphoreType.DMA((len(parts),))]
    in_specs = [vmem_spec()]
    if pieces:
        out_shape = [jax.ShapeDtypeStruct((ROWS, rows, columns), jnp.bfloat16)] + out_shape
        scratch = [
            pltpu.VMEM((ROWS, rows, columns), jnp.bfloat16),
            pltpu.SemaphoreType.DMA((ROWS,)),
        ] + scratch
        in_specs = [any_spec()] * pieces
    return pl.pallas_call(
        functools.partial(gather_kernel, parts, pieces, len(earlier)),
        in_specs=[smem_spec(), smem_spec()] + in_specs + [any_spec()] * len(earlier),
        out_specs=[any_spec()] * len(out_shape),
        out_shape=out_shape,
        scratch_shapes=scratch,
        compiler_params=params(),
        cost_estimate=cost(0, 2 * ROWS * (CAP + 1) * sum(parts) * columns),
        name=name,
    )(seq, send_block, *arrays, *earlier)


def weights_kernel(held_count, owner_ref, rank_ref, usable_ref, row_ref, seq_ref, own_a, own_b, *rest):
    picks, rest = rest[: 2 * TOPK], rest[2 * TOPK :]
    pieces, rest = rest[:CHIPS], rest[CHIPS + held_count :]
    weight_ref, inverse_ref, queries, scores, sem = rest
    row = row_ref[pl.program_id(0)]

    @pl.when(pl.program_id(0) == 0)
    def _():
        run_copies(to_rows(seq_ref[0], pieces, queries, sem))

    query = queries[row]
    key_pairs = [(own_a[0], own_b[0])] + [
        (picks[2 * j][0, 0], picks[2 * j + 1][0, 0]) for j in range(TOPK)
    ]

    def raw(pair):
        upper = jnp.dot(pair[0], query, preferred_element_type=jnp.float32)
        lower = jnp.dot(pair[1], query, preferred_element_type=jnp.float32)
        return upper * EXP2_SCALE, lower * EXP2_SCALE

    key_at = lax.broadcasted_iota(jnp.int32, (BLK, BLK), 0)
    query_at = lax.broadcasted_iota(jnp.int32, (BLK, BLK), 1)
    upper, lower = raw(key_pairs[0])
    own = jnp.where(query_at >= key_at, jnp.concatenate([upper, lower], axis=0), -jnp.inf)
    scores[0] = own
    top = jnp.max(own, axis=0, keepdims=True)
    inverse_ref[0] = top

    for j in range(TOPK):

        @pl.when(usable_ref[row * TOPK + j] > 0)
        def _(j=j):
            upper, lower = raw(key_pairs[1 + j])
            scores[1 + j, pl.ds(0, K_FIRST), :] = upper
            scores[1 + j, pl.ds(K_FIRST, BLK - K_FIRST), :] = lower
            inverse_ref[0] = jnp.maximum(
                inverse_ref[0],
                jnp.maximum(
                    jnp.max(upper, axis=0, keepdims=True), jnp.max(lower, axis=0, keepdims=True)
                ),
            )

    top = inverse_ref[0]
    exps = jnp.exp2(scores[0] - top)
    weight_ref[0, 0] = exps.astype(jnp.bfloat16)
    inverse_ref[0] = jnp.sum(exps, axis=0, keepdims=True)
    for j in range(TOPK):
        is_usable = usable_ref[row * TOPK + j] > 0

        @pl.when(is_usable)
        def _(j=j):
            exps = jnp.exp2(scores[1 + j] - top)
            weight_ref[0, 1 + j] = exps.astype(jnp.bfloat16)
            inverse_ref[0] = inverse_ref[0] + jnp.sum(exps, axis=0, keepdims=True)

        @pl.when(jnp.logical_not(is_usable))
        def _(j=j):
            weight_ref[0, 1 + j] = jnp.zeros((BLK, BLK), jnp.bfloat16)

    inverse_ref[0] = 1.0 / inverse_ref[0]


def make_weights(tables, seq, rows_at, query_pieces, own_a, own_b, got_a, got_b, held=()):
    owner, rank, usable = tables
    rest = BLK - K_FIRST
    steps = rows_at.shape[0]

    def pick(j, rows):
        def index(i, owner, rank, usable, at, seq):
            return (owner[at[i] * TOPK + j], rank[at[i] * TOPK + j], 0, 0)

        return pl.BlockSpec((1, 1, rows, DH), index)

    in_specs = [
        pl.BlockSpec((1, K_FIRST, DH), lambda i, o, r, u, at, s: (at[i], 0, 0)),
        pl.BlockSpec((1, rest, DH), lambda i, o, r, u, at, s: (at[i], 0, 0)),
    ]
    args = [own_a, own_b]
    for j in range(TOPK):
        in_specs += [pick(j, K_FIRST), pick(j, rest)]
        args += [got_a.reshape(ROWS, CAP, K_FIRST, DH), got_b.reshape(ROWS, CAP, rest, DH)]
    args += [*query_pieces, *held]
    in_specs += [any_spec()] * (CHIPS + len(held))
    blocks = steps * (1 + TOPK)
    prefetched = (owner, rank, usable, rows_at, seq)
    first_held = len(prefetched) + len(args) - len(held)
    return pl.pallas_call(
        functools.partial(weights_kernel, len(held)),
        grid_spec=pltpu.PrefetchScalarGridSpec(
            num_scalar_prefetch=len(prefetched),
            grid=(steps,),
            in_specs=in_specs,
            out_specs=[
                pl.BlockSpec(
                    (1, 1 + TOPK, BLK, BLK), lambda i, o, r, u, at, s: (at[i], 0, 0, 0)
                ),
                pl.BlockSpec((1, 1, BLK), lambda i, o, r, u, at, s: (at[i], 0, 0)),
            ],
            scratch_shapes=[
                pltpu.VMEM((ROWS, DH, BLK), jnp.bfloat16),
                pltpu.VMEM((1 + TOPK, BLK, BLK), jnp.float32),
                pltpu.SemaphoreType.DMA((ROWS,)),
            ],
        ),
        out_shape=[
            jax.ShapeDtypeStruct((ROWS, 1 + TOPK, BLK, BLK), jnp.bfloat16),
            jax.ShapeDtypeStruct((ROWS, 1, BLK), jnp.float32),
        ],
        input_output_aliases={first_held + i: i for i in range(len(held))},
        compiler_params=params(),
        cost_estimate=cost(
            2 * blocks * BLK * BLK * DH, 2 * blocks * (BLK * BLK + BLK * DH), blocks * BLK * BLK
        ),
        name="make_weights",
    )(*prefetched, *args)


def outputs_kernel(start, rows, owner_ref, rank_ref, row_ref, weight_ref, inverse_ref, *rest):
    own_ref, picks, out_ref = rest[0], rest[1 : 1 + TOPK], rest[1 + TOPK]
    total = jnp.dot(
        own_ref[0, pl.ds(start, rows), :], weight_ref[0, 0], preferred_element_type=jnp.float32
    )
    for j in range(TOPK):
        total += jnp.dot(picks[j][0, 0], weight_ref[0, 1 + j], preferred_element_type=jnp.float32)
    out_ref[0] = (total * inverse_ref[0]).astype(jnp.bfloat16)


def make_outputs(tables, rows_at, weights, inverse, values, got, start, rows):
    owner, rank, _ = tables
    steps = rows_at.shape[0]

    def pick(j):
        def index(step, owner, rank, row_at):
            at = row_at[step] * TOPK + j
            return (owner[at], rank[at], 0, 0)

        return pl.BlockSpec((1, 1, rows, BLK), index)

    blocks = steps * (1 + TOPK)
    return pl.pallas_call(
        functools.partial(outputs_kernel, start, rows),
        grid_spec=pltpu.PrefetchScalarGridSpec(
            num_scalar_prefetch=3,
            grid=(steps,),
            in_specs=[
                pl.BlockSpec((1, 1 + TOPK, BLK, BLK), lambda i, o, r, at: (at[i], 0, 0, 0)),
                pl.BlockSpec((1, 1, BLK), lambda i, o, r, at: (at[i], 0, 0)),
                pl.BlockSpec((1, DH, BLK), lambda i, o, r, at: (at[i], 0, 0)),
            ]
            + [pick(j) for j in range(TOPK)],
            out_specs=pl.BlockSpec((1, rows, BLK), lambda i, *_: (i, 0, 0)),
        ),
        out_shape=jax.ShapeDtypeStruct((steps, rows, BLK), jnp.bfloat16),
        compiler_params=params(),
        cost_estimate=cost(2 * blocks * BLK * BLK * 128, 2 * blocks * BLK * (BLK + rows)),
        name="make_outputs",
    )(owner, rank, rows_at, weights, inverse, values, *([got.reshape(ROWS, CAP, rows, BLK)] * TOPK))


def finish_kernel(parts, seq_ref, *rest):
    pieces, (last_ref, out_ref, held, sem) = rest[:CHIPS], rest[CHIPS:]
    copies = to_rows(seq_ref[0], pieces, held, sem, 0, parts[0])
    for head in range(HEADS):
        copies.append(
            pltpu.make_async_copy(
                last_ref.at[head], held.at[head, pl.ds(parts[0], parts[1])], sem.at[ROWS + head]
            )
        )
    run_copies(copies)
    for head in range(HEADS):
        out_ref[:, pl.ds(head * DH, DH)] = held[head].T


def finish(seq, pieces, last, parts):
    return pl.pallas_call(
        functools.partial(finish_kernel, parts),
        in_specs=[smem_spec()] + [any_spec()] * (CHIPS + 1),
        out_specs=vmem_spec(),
        out_shape=jax.ShapeDtypeStruct((BLK, HEADS * DH), jnp.bfloat16),
        scratch_shapes=[
            pltpu.VMEM((HEADS, DH, BLK), jnp.bfloat16),
            pltpu.SemaphoreType.DMA((ROWS + HEADS,)),
        ],
        compiler_params=params(),
        cost_estimate=cost(0, 4 * BLK * HEADS * DH),
        name="finish",
    )(seq, *pieces, last)


def permute_seq(array, place):
    seq_count, grp_count = lax.axis_size("seq"), lax.axis_size("grp")
    pairs = [
        (s * grp_count + g, place(s) % seq_count * grp_count + g)
        for s in range(seq_count)
        for g in range(grp_count)
    ]
    return lax.ppermute(array, AXES, pairs)


def swap_cores(array):
    return permute_seq(array, lambda s: s ^ 1)


def along_chips(pieces):
    moved = {0: pieces[0]}
    for chip in CHIP_ORDER:
        moved[chip] = permute_seq(pieces[chip], lambda s, chip=chip: s + 2 * chip)
    return [moved[chip] for chip in range(CHIPS)]


def exchange(array, axis):
    return lax.all_to_all(array, axis, split_axis=0, concat_axis=0, tiled=True)


def routes(pick_column, pick_back):
    seq, grp = lax.axis_index("seq"), lax.axis_index("grp")
    requests = ROWS * TOPK
    target = lax.dynamic_index_in_dim(pick_column, seq, 1, keepdims=False).reshape(-1, requests)
    back = lax.dynamic_index_in_dim(pick_back, seq, 1, keepdims=False).reshape(-1, requests)
    column = jnp.arange(target.shape[0], dtype=jnp.int32)[:, None]
    row = (jnp.arange(requests, dtype=jnp.int32) // TOPK)[None, :]
    local_row = row - back - (target >= column).astype(jnp.int32)
    at = jnp.arange(requests, dtype=jnp.int32)
    earlier = at[:, None] > at[None, :]
    hits = target == grp
    place = jnp.sum(hits[:, None, :] & earlier[None], axis=2, dtype=jnp.int32)
    chosen = hits[:, None, :] & (
        place[:, None, :] == jnp.arange(CAP, dtype=jnp.int32)[None, :, None]
    )
    send_block = jnp.sum(
        jnp.where(chosen, jnp.maximum(local_row, 0)[:, None, :], 0), axis=2, dtype=jnp.int32
    ).reshape(-1)
    owner = lax.dynamic_index_in_dim(target, grp, 0, keepdims=False)
    rank = jnp.sum((owner[:, None] == owner[None, :]) & earlier, axis=1, dtype=jnp.int32)
    usable = (lax.dynamic_index_in_dim(local_row, grp, 0, keepdims=False) >= 0).astype(jnp.int32)
    return send_block, (owner, rank, usable)


def body(query_rows, key_rows, value_rows, pick_column, pick_back):
    seq = lax.axis_index("seq").astype(jnp.int32).reshape(1)
    rest = BLK - K_FIRST
    key_first = split_first(key_rows)
    own_a = exchange(key_first, "seq")
    mine, other = by_core(split_rest_kernel, seq, key_rows, key_first, (rest, DH), "split_rest")
    key_pieces = pack(mine, swap_cores(other), "pack_keys")
    mine, other = by_core(turn_kernel, seq, value_rows, key_first, (DH, BLK), "turn_values")
    value_pieces = pack(mine, swap_cores(other), "pack_values")
    mine, other = by_core(turn_kernel, seq, query_rows, key_first, (DH, BLK), "turn_queries")
    query_pieces = pack(mine, swap_cores(other), "pack_queries")

    send_block, tables = routes(pick_column, pick_back)
    ready = [key_pieces[0], value_pieces[0]]
    (send_a,) = gather(seq, send_block, [own_a], (K_FIRST,), "gather_a", earlier=ready)
    got_a = exchange(send_a, "grp")

    key_pieces = along_chips(after(key_pieces, [send_a]))
    own_b, send_b = gather(seq, send_block, key_pieces, (rest,), "gather_b")
    (send_b,) = after([send_b], [got_a])
    got_b = exchange(send_b, "grp")

    value_pieces = along_chips(after(value_pieces, [key_pieces[CHIP_ORDER[4]]]))
    values, *sends = gather(seq, send_block, value_pieces, V_PARTS, "gather_values")
    query_pieces = along_chips(after(query_pieces, [value_pieces[CHIP_ORDER[4]]]))
    chips = jnp.arange(CHIPS, dtype=jnp.int32)
    same = (seq + 2 * chips) % ROWS
    opposite = same ^ 1
    inputs = (query_pieces, own_a, own_b, got_a, got_b)
    held = make_weights(tables, seq, opposite, *inputs)

    (send,) = after(sends[:1], [got_b] + [query_pieces[chip] for chip in CHIP_ORDER[:2]])
    got = exchange(send, "grp")
    (send,) = after(sends[1:], [got, held[1]])
    weights, inverse = make_weights(tables, seq, same, *inputs, held=held)
    first = (weights, inverse, values, got, 0, V_PARTS[0])
    other = swap_cores(make_outputs(tables, opposite, *first))
    mine = make_outputs(tables, same, *first)
    pieces = along_chips(pack(mine, other, "pack_outputs"))

    (got,) = after([exchange(send, "grp")], [pieces[chip] for chip in CHIP_ORDER[:2]])
    second = (weights, inverse, values, got, V_PARTS[0], V_PARTS[1])
    outs = make_outputs(tables, jnp.arange(ROWS, dtype=jnp.int32), *second)
    return finish(seq, pieces, exchange(outs, "seq"), V_PARTS)


def solution(mesh):
    return jax.shard_map(
        body,
        mesh=mesh,
        in_specs=(P(AXES, None), P(AXES, None), P(AXES, None), P(), P()),
        out_specs=P(AXES, None),
        check_vma=False,
    )
```

```python
import functools

import jax
import jax.numpy as jnp
from jax import lax
from jax.experimental import pallas as pl
from jax.experimental.pallas import tpu as pltpu
from jax.sharding import PartitionSpec as P

HEADS = 16
DH = 128
BLK = 512
TOPK = 3
CAP = 4
ROWS = 16
CHIPS = ROWS // 2
K_FIRST = 192
V_PARTS = (64, 64)
CHIP_ORDER = (4, 3, 5, 2, 6, 1, 7)
EXP2_SCALE = DH ** (-0.5) * 1.4426950408889634
VMEM_BYTES = 56 * 1024 * 1024
AXES = ("seq", "grp")


def any_spec():
    return pl.BlockSpec(memory_space=pl.ANY)


def vmem_spec():
    return pl.BlockSpec(memory_space=pltpu.VMEM)


def smem_spec():
    return pl.BlockSpec(memory_space=pltpu.SMEM)


def params():
    return pltpu.CompilerParams(vmem_limit_bytes=VMEM_BYTES)


def cost(flops, moved, exps=0):
    return pl.CostEstimate(flops=flops, bytes_accessed=moved, transcendentals=exps)


def split_first_kernel(key_ref, first_ref):
    for head in range(HEADS):
        first_ref[head] = key_ref[:, pl.ds(head * DH, DH)]


def split_first(key_rows):
    return pl.pallas_call(
        split_first_kernel,
        grid=(1,),
        in_specs=[pl.BlockSpec((K_FIRST, HEADS * DH), lambda i: (0, 0))],
        out_specs=pl.BlockSpec((HEADS, K_FIRST, DH), lambda i: (0, 0, 0)),
        out_shape=jax.ShapeDtypeStruct((HEADS, K_FIRST, DH), jnp.bfloat16),
        compiler_params=params(),
        cost_estimate=cost(0, 4 * K_FIRST * HEADS * DH),
        name="split_first",
    )(key_rows)


def run_copies(copies):
    for copy in copies:
        copy.start()
    for copy in copies:
        copy.wait()


def same_core(seq, chip_shift):
    core = lax.rem(seq, 2)
    at = lax.rem(seq + 2 * chip_shift + ROWS, ROWS)
    return at, at + 1 - 2 * core


def put_heads(seq, held, mine_ref, other_ref, sem):
    copies = []
    for chip in range(CHIPS):
        mine, other = same_core(seq, chip)
        copies.append(pltpu.make_async_copy(held.at[mine], mine_ref.at[chip], sem.at[2 * chip]))
        copies.append(
            pltpu.make_async_copy(held.at[other], other_ref.at[chip], sem.at[2 * chip + 1])
        )
    run_copies(copies)


def split_rest_kernel(seq_ref, key_ref, earlier_ref, mine_ref, other_ref, held, sem):
    for head in range(HEADS):
        held[head] = key_ref[pl.ds(K_FIRST, BLK - K_FIRST), pl.ds(head * DH, DH)]
    put_heads(seq_ref[0], held, mine_ref, other_ref, sem)


def turn_kernel(seq_ref, row_ref, earlier_ref, mine_ref, other_ref, held, sem):
    for head in range(HEADS):
        held[head] = row_ref[:, pl.ds(head * DH, DH)].T
    put_heads(seq_ref[0], held, mine_ref, other_ref, sem)


def by_core(kernel, seq, array, earlier, shape, name):
    return pl.pallas_call(
        kernel,
        in_specs=[smem_spec(), vmem_spec(), any_spec()],
        out_specs=[any_spec()] * 2,
        out_shape=[jax.ShapeDtypeStruct((CHIPS,) + shape, jnp.bfloat16)] * 2,
        scratch_shapes=[
            pltpu.VMEM((ROWS,) + shape, jnp.bfloat16),
            pltpu.SemaphoreType.DMA((ROWS,)),
        ],
        compiler_params=params(),
        cost_estimate=cost(0, 4 * ROWS * shape[0] * shape[1]),
        name=name,
    )(seq, array, earlier)


def pack_kernel(mine_ref, other_ref, *rest):
    piece_refs, sem = rest[:CHIPS], rest[CHIPS]
    copies = []
    for chip in range(CHIPS):
        copies.append(
            pltpu.make_async_copy(mine_ref.at[chip], piece_refs[chip].at[0], sem.at[2 * chip])
        )
        copies.append(
            pltpu.make_async_copy(other_ref.at[chip], piece_refs[chip].at[1], sem.at[2 * chip + 1])
        )
    run_copies(copies)


def pack(mine, other, name):
    shape = mine.shape[1:]
    return pl.pallas_call(
        pack_kernel,
        in_specs=[vmem_spec()] * 2,
        out_specs=[any_spec()] * CHIPS,
        out_shape=[jax.ShapeDtypeStruct((2,) + shape, jnp.bfloat16)] * CHIPS,
        scratch_shapes=[pltpu.SemaphoreType.DMA((ROWS,))],
        compiler_params=params(),
        cost_estimate=cost(0, 8 * CHIPS * shape[0] * shape[1]),
        name=name,
    )(mine, other)


def to_rows(seq, piece_refs, held, sem, start=0, rows=None):
    copies = []
    for chip in range(CHIPS):
        for which, row in enumerate(same_core(seq, -chip)):
            place = held.at[row] if rows is None else held.at[row, pl.ds(start, rows)]
            copies.append(
                pltpu.make_async_copy(piece_refs[chip].at[which], place, sem.at[2 * chip + which])
            )
    return copies


def nothing_kernel(*refs):
    pass


def after(arrays, earlier):
    count = len(arrays)
    return pl.pallas_call(
        nothing_kernel,
        in_specs=[any_spec()] * (count + len(earlier)),
        out_specs=[any_spec()] * count,
        out_shape=[jax.ShapeDtypeStruct(a.shape, a.dtype) for a in arrays],
        input_output_aliases={i: i for i in range(count)},
        cost_estimate=cost(0, 0),
        name="after",
    )(*arrays, *earlier)


def gather_kernel(parts, pieces, extra, seq_ref, block_ref, *rest):
    in_refs, rest = rest[: max(pieces, 1)], rest[max(pieces, 1) + extra :]
    if pieces:
        all_ref, rest = rest[0], rest[1:]
    send_refs, rest = rest[: len(parts)], rest[len(parts) :]
    if pieces:
        held, in_sem, out_sem = rest
        run_copies(to_rows(seq_ref[0], in_refs, held, in_sem))
        whole = pltpu.make_async_copy(held, all_ref, in_sem.at[0])
        whole.start()
    else:
        held, out_sem, whole = in_refs[0], rest[0], None

    start = 0
    for part, (rows, send_ref) in enumerate(zip(parts, send_refs)):

        def send(slot, carry, start=start, rows=rows, send_ref=send_ref, part=part):
            pltpu.make_async_copy(
                held.at[block_ref[slot], pl.ds(start, rows)], send_ref.at[slot], out_sem.at[part]
            ).start()
            return carry

        lax.fori_loop(0, ROWS * CAP, send, 0)
        start += rows
    for part, send_ref in enumerate(send_refs):
        pltpu.make_async_copy(send_ref, send_ref, out_sem.at[part]).wait()
    if whole is not None:
        whole.wait()


def gather(seq, send_block, arrays, parts, name, earlier=()):
    pieces = len(arrays) if len(arrays) > 1 else 0
    rows, columns = arrays[0].shape[-2:]
    out_shape = [jax.ShapeDtypeStruct((ROWS * CAP, part, columns), jnp.bfloat16) for part in parts]
    scratch = [pltpu.SemaphoreType.DMA((len(parts),))]
    in_specs = [vmem_spec()]
    if pieces:
        out_shape = [jax.ShapeDtypeStruct((ROWS, rows, columns), jnp.bfloat16)] + out_shape
        scratch = [
            pltpu.VMEM((ROWS, rows, columns), jnp.bfloat16),
            pltpu.SemaphoreType.DMA((ROWS,)),
        ] + scratch
        in_specs = [any_spec()] * pieces
    return pl.pallas_call(
        functools.partial(gather_kernel, parts, pieces, len(earlier)),
        in_specs=[smem_spec(), smem_spec()] + in_specs + [any_spec()] * len(earlier),
        out_specs=[any_spec()] * len(out_shape),
        out_shape=out_shape,
        scratch_shapes=scratch,
        compiler_params=params(),
        cost_estimate=cost(0, 2 * ROWS * (CAP + 1) * sum(parts) * columns),
        name=name,
    )(seq, send_block, *arrays, *earlier)


def weights_kernel(held_count, owner_ref, rank_ref, usable_ref, row_ref, seq_ref, own_a, own_b, *rest):
    picks, rest = rest[: 2 * TOPK], rest[2 * TOPK :]
    pieces, rest = rest[:CHIPS], rest[CHIPS + held_count :]
    weight_ref, inverse_ref, queries, scores, sem = rest
    row = row_ref[pl.program_id(0)]

    @pl.when(pl.program_id(0) == 0)
    def _():
        run_copies(to_rows(seq_ref[0], pieces, queries, sem))

    query = queries[row]
    key_pairs = [(own_a[0], own_b[0])] + [
        (picks[2 * j][0, 0], picks[2 * j + 1][0, 0]) for j in range(TOPK)
    ]

    def raw(pair):
        upper = jnp.dot(pair[0], query, preferred_element_type=jnp.float32)
        lower = jnp.dot(pair[1], query, preferred_element_type=jnp.float32)
        return upper * EXP2_SCALE, lower * EXP2_SCALE

    key_at = lax.broadcasted_iota(jnp.int32, (BLK, BLK), 0)
    query_at = lax.broadcasted_iota(jnp.int32, (BLK, BLK), 1)
    upper, lower = raw(key_pairs[0])
    own = jnp.where(query_at >= key_at, jnp.concatenate([upper, lower], axis=0), -jnp.inf)
    scores[0] = own
    top = jnp.max(own, axis=0, keepdims=True)
    inverse_ref[0] = top

    for j in range(TOPK):

        @pl.when(usable_ref[row * TOPK + j] > 0)
        def _(j=j):
            upper, lower = raw(key_pairs[1 + j])
            scores[1 + j, pl.ds(0, K_FIRST), :] = upper
            scores[1 + j, pl.ds(K_FIRST, BLK - K_FIRST), :] = lower
            inverse_ref[0] = jnp.maximum(
                inverse_ref[0],
                jnp.maximum(
                    jnp.max(upper, axis=0, keepdims=True), jnp.max(lower, axis=0, keepdims=True)
                ),
            )

    top = inverse_ref[0]
    exps = jnp.exp2(scores[0] - top)
    weight_ref[0, 0] = exps.astype(jnp.bfloat16)
    inverse_ref[0] = jnp.sum(exps, axis=0, keepdims=True)
    for j in range(TOPK):
        is_usable = usable_ref[row * TOPK + j] > 0

        @pl.when(is_usable)
        def _(j=j):
            exps = jnp.exp2(scores[1 + j] - top)
            weight_ref[0, 1 + j] = exps.astype(jnp.bfloat16)
            inverse_ref[0] = inverse_ref[0] + jnp.sum(exps, axis=0, keepdims=True)

        @pl.when(jnp.logical_not(is_usable))
        def _(j=j):
            weight_ref[0, 1 + j] = jnp.zeros((BLK, BLK), jnp.bfloat16)

    inverse_ref[0] = 1.0 / inverse_ref[0]


def make_weights(tables, seq, rows_at, query_pieces, own_a, own_b, got_a, got_b, held=()):
    owner, rank, usable = tables
    rest = BLK - K_FIRST
    steps = rows_at.shape[0]

    def pick(j, rows):
        def index(i, owner, rank, usable, at, seq):
            return (owner[at[i] * TOPK + j], rank[at[i] * TOPK + j], 0, 0)

        return pl.BlockSpec((1, 1, rows, DH), index)

    in_specs = [
        pl.BlockSpec((1, K_FIRST, DH), lambda i, o, r, u, at, s: (at[i], 0, 0)),
        pl.BlockSpec((1, rest, DH), lambda i, o, r, u, at, s: (at[i], 0, 0)),
    ]
    args = [own_a, own_b]
    for j in range(TOPK):
        in_specs += [pick(j, K_FIRST), pick(j, rest)]
        args += [got_a.reshape(ROWS, CAP, K_FIRST, DH), got_b.reshape(ROWS, CAP, rest, DH)]
    args += [*query_pieces, *held]
    in_specs += [any_spec()] * (CHIPS + len(held))
    blocks = steps * (1 + TOPK)
    prefetched = (owner, rank, usable, rows_at, seq)
    first_held = len(prefetched) + len(args) - len(held)
    return pl.pallas_call(
        functools.partial(weights_kernel, len(held)),
        grid_spec=pltpu.PrefetchScalarGridSpec(
            num_scalar_prefetch=len(prefetched),
            grid=(steps,),
            in_specs=in_specs,
            out_specs=[
                pl.BlockSpec(
                    (1, 1 + TOPK, BLK, BLK), lambda i, o, r, u, at, s: (at[i], 0, 0, 0)
                ),
                pl.BlockSpec((1, 1, BLK), lambda i, o, r, u, at, s: (at[i], 0, 0)),
            ],
            scratch_shapes=[
                pltpu.VMEM((ROWS, DH, BLK), jnp.bfloat16),
                pltpu.VMEM((1 + TOPK, BLK, BLK), jnp.float32),
                pltpu.SemaphoreType.DMA((ROWS,)),
            ],
        ),
        out_shape=[
            jax.ShapeDtypeStruct((ROWS, 1 + TOPK, BLK, BLK), jnp.bfloat16),
            jax.ShapeDtypeStruct((ROWS, 1, BLK), jnp.float32),
        ],
        input_output_aliases={first_held + i: i for i in range(len(held))},
        compiler_params=params(),
        cost_estimate=cost(
            2 * blocks * BLK * BLK * DH, 2 * blocks * (BLK * BLK + BLK * DH), blocks * BLK * BLK
        ),
        name="make_weights",
    )(*prefetched, *args)


def outputs_kernel(start, rows, owner_ref, rank_ref, row_ref, inverse_ref, *rest):
    weight_refs, rest = rest[: 1 + TOPK], rest[1 + TOPK :]
    own_ref, picks, out_ref = rest[0], rest[1 : 1 + TOPK], rest[1 + TOPK]
    total = jnp.dot(
        own_ref[0, pl.ds(start, rows), :], weight_refs[0][0, 0], preferred_element_type=jnp.float32
    )
    for j in range(TOPK):
        total += jnp.dot(
            picks[j][0, 0], weight_refs[1 + j][0, 0], preferred_element_type=jnp.float32
        )
    out_ref[0] = (total * inverse_ref[0]).astype(jnp.bfloat16)


def make_outputs(tables, rows_at, weights, inverse, values, got, start, rows):
    owner, rank, _ = tables
    steps = rows_at.shape[0]

    def pick(j):
        def index(step, owner, rank, row_at):
            at = row_at[step] * TOPK + j
            return (owner[at], rank[at], 0, 0)

        return pl.BlockSpec((1, 1, rows, BLK), index)

    blocks = steps * (1 + TOPK)
    return pl.pallas_call(
        functools.partial(outputs_kernel, start, rows),
        grid_spec=pltpu.PrefetchScalarGridSpec(
            num_scalar_prefetch=3,
            grid=(steps,),
            in_specs=[pl.BlockSpec((1, 1, BLK), lambda i, o, r, at: (at[i], 0, 0))]
            + [
                pl.BlockSpec((1, 1, BLK, BLK), lambda i, o, r, at, j=j: (at[i], j, 0, 0))
                for j in range(1 + TOPK)
            ]
            + [pl.BlockSpec((1, DH, BLK), lambda i, o, r, at: (at[i], 0, 0))]
            + [pick(j) for j in range(TOPK)],
            out_specs=pl.BlockSpec((1, rows, BLK), lambda i, *_: (i, 0, 0)),
        ),
        out_shape=jax.ShapeDtypeStruct((steps, rows, BLK), jnp.bfloat16),
        compiler_params=params(),
        cost_estimate=cost(2 * blocks * BLK * BLK * 128, 2 * blocks * BLK * (BLK + rows)),
        name="make_outputs",
    )(
        owner,
        rank,
        rows_at,
        inverse,
        *([weights] * (1 + TOPK)),
        values,
        *([got.reshape(ROWS, CAP, rows, BLK)] * TOPK),
    )


def finish_kernel(parts, seq_ref, *rest):
    pieces, (last_ref, out_ref, held, sem) = rest[:CHIPS], rest[CHIPS:]
    copies = to_rows(seq_ref[0], pieces, held, sem, 0, parts[0])
    for head in range(HEADS):
        copies.append(
            pltpu.make_async_copy(
                last_ref.at[head], held.at[head, pl.ds(parts[0], parts[1])], sem.at[ROWS + head]
            )
        )
    run_copies(copies)
    for head in range(HEADS):
        out_ref[:, pl.ds(head * DH, DH)] = held[head].T


def finish(seq, pieces, last, parts):
    return pl.pallas_call(
        functools.partial(finish_kernel, parts),
        in_specs=[smem_spec()] + [any_spec()] * (CHIPS + 1),
        out_specs=vmem_spec(),
        out_shape=jax.ShapeDtypeStruct((BLK, HEADS * DH), jnp.bfloat16),
        scratch_shapes=[
            pltpu.VMEM((HEADS, DH, BLK), jnp.bfloat16),
            pltpu.SemaphoreType.DMA((ROWS + HEADS,)),
        ],
        compiler_params=params(),
        cost_estimate=cost(0, 4 * BLK * HEADS * DH),
        name="finish",
    )(seq, *pieces, last)


def permute_seq(array, place):
    seq_count, grp_count = lax.axis_size("seq"), lax.axis_size("grp")
    pairs = [
        (s * grp_count + g, place(s) % seq_count * grp_count + g)
        for s in range(seq_count)
        for g in range(grp_count)
    ]
    return lax.ppermute(array, AXES, pairs)


def swap_cores(array):
    return permute_seq(array, lambda s: s ^ 1)


def along_chips(pieces):
    moved = {0: pieces[0]}
    for chip in CHIP_ORDER:
        moved[chip] = permute_seq(pieces[chip], lambda s, chip=chip: s + 2 * chip)
    return [moved[chip] for chip in range(CHIPS)]


def exchange(array, axis):
    return lax.all_to_all(array, axis, split_axis=0, concat_axis=0, tiled=True)


def routes(pick_column, pick_back):
    seq, grp = lax.axis_index("seq"), lax.axis_index("grp")
    requests = ROWS * TOPK
    target = lax.dynamic_index_in_dim(pick_column, seq, 1, keepdims=False).reshape(-1, requests)
    back = lax.dynamic_index_in_dim(pick_back, seq, 1, keepdims=False).reshape(-1, requests)
    column = jnp.arange(target.shape[0], dtype=jnp.int32)[:, None]
    row = (jnp.arange(requests, dtype=jnp.int32) // TOPK)[None, :]
    local_row = row - back - (target >= column).astype(jnp.int32)
    at = jnp.arange(requests, dtype=jnp.int32)
    earlier = at[:, None] > at[None, :]
    hits = target == grp
    place = jnp.sum(hits[:, None, :] & earlier[None], axis=2, dtype=jnp.int32)
    chosen = hits[:, None, :] & (
        place[:, None, :] == jnp.arange(CAP, dtype=jnp.int32)[None, :, None]
    )
    send_block = jnp.sum(
        jnp.where(chosen, jnp.maximum(local_row, 0)[:, None, :], 0), axis=2, dtype=jnp.int32
    ).reshape(-1)
    owner = lax.dynamic_index_in_dim(target, grp, 0, keepdims=False)
    rank = jnp.sum((owner[:, None] == owner[None, :]) & earlier, axis=1, dtype=jnp.int32)
    usable = (lax.dynamic_index_in_dim(local_row, grp, 0, keepdims=False) >= 0).astype(jnp.int32)
    return send_block, (owner, rank, usable)


def body(query_rows, key_rows, value_rows, pick_column, pick_back):
    seq = lax.axis_index("seq").astype(jnp.int32).reshape(1)
    rest = BLK - K_FIRST
    key_first = split_first(key_rows)
    own_a = exchange(key_first, "seq")
    mine, other = by_core(split_rest_kernel, seq, key_rows, key_first, (rest, DH), "split_rest")
    key_pieces = pack(mine, swap_cores(other), "pack_keys")
    mine, other = by_core(turn_kernel, seq, value_rows, key_first, (DH, BLK), "turn_values")
    value_pieces = pack(mine, swap_cores(other), "pack_values")
    mine, other = by_core(turn_kernel, seq, query_rows, key_first, (DH, BLK), "turn_queries")
    query_pieces = pack(mine, swap_cores(other), "pack_queries")

    send_block, tables = routes(pick_column, pick_back)
    ready = [key_pieces[0], value_pieces[0]]
    (send_a,) = gather(seq, send_block, [own_a], (K_FIRST,), "gather_a", earlier=ready)
    got_a = exchange(send_a, "grp")

    key_pieces = along_chips(after(key_pieces, [send_a]))
    own_b, send_b = gather(
        seq, send_block, key_pieces, (rest,), "gather_b", earlier=[query_pieces[0]]
    )
    (send_b,) = after([send_b], [got_a])
    got_b = exchange(send_b, "grp")

    value_pieces = along_chips(after(value_pieces, [key_pieces[CHIP_ORDER[2]]]))
    values, *sends = gather(seq, send_block, value_pieces, V_PARTS, "gather_values")
    query_pieces = along_chips(after(query_pieces, [value_pieces[CHIP_ORDER[2]]]))
    chips = jnp.arange(CHIPS, dtype=jnp.int32)
    same = (seq + 2 * chips) % ROWS
    opposite = same ^ 1
    inputs = (query_pieces, own_a, own_b, got_a, got_b)
    held = make_weights(tables, seq, opposite, *inputs)

    (send,) = after(sends[:1], [got_b] + [query_pieces[chip] for chip in CHIP_ORDER[:2]])
    got = exchange(send, "grp")
    (send,) = after(sends[1:], [got, held[1]])
    weights, inverse = make_weights(tables, seq, same, *inputs, held=held)
    first = (weights, inverse, values, got, 0, V_PARTS[0])
    other = swap_cores(make_outputs(tables, opposite, *first))
    mine = make_outputs(tables, same, *first)
    pieces = along_chips(pack(mine, other, "pack_outputs"))

    (got,) = after([exchange(send, "grp")], pieces[1:])
    second = (weights, inverse, values, got, V_PARTS[0], V_PARTS[1])
    outs = make_outputs(tables, jnp.arange(ROWS, dtype=jnp.int32), *second)
    return finish(seq, pieces, exchange(outs, "seq"), V_PARTS)


def solution(mesh):
    return jax.shard_map(
        body,
        mesh=mesh,
        in_specs=(P(AXES, None), P(AXES, None), P(AXES, None), P(), P()),
        out_specs=P(AXES, None),
        check_vma=False,
    )
```

```python
import functools

import jax
import jax.numpy as jnp
from jax import lax
from jax.experimental import pallas as pl
from jax.experimental.pallas import tpu as pltpu
from jax.sharding import PartitionSpec as P

HEADS = 16
DH = 128
BLK = 512
TOPK = 3
CAP = 4
ROWS = 16
CHIPS = ROWS // 2
K_FIRST = 320
V_PARTS = (64, 64)
FAR_FIRST = (4, 3, 5, 2, 6, 1, 7)
NEAR_FIRST = (1, 7, 2, 6, 3, 5, 4)
EXP2_SCALE = DH ** (-0.5) * 1.4426950408889634
VMEM_BYTES = 56 * 1024 * 1024
AXES = ("seq", "grp")


def any_spec():
    return pl.BlockSpec(memory_space=pl.ANY)


def vmem_spec():
    return pl.BlockSpec(memory_space=pltpu.VMEM)


def smem_spec():
    return pl.BlockSpec(memory_space=pltpu.SMEM)


def params():
    return pltpu.CompilerParams(vmem_limit_bytes=VMEM_BYTES)


def cost(flops, moved, exps=0):
    return pl.CostEstimate(flops=flops, bytes_accessed=moved, transcendentals=exps)


def split_first_kernel(key_ref, first_ref):
    for head in range(HEADS):
        first_ref[head] = key_ref[:, pl.ds(head * DH, DH)]


def split_first(key_rows):
    return pl.pallas_call(
        split_first_kernel,
        grid=(1,),
        in_specs=[pl.BlockSpec((K_FIRST, HEADS * DH), lambda i: (0, 0))],
        out_specs=pl.BlockSpec((HEADS, K_FIRST, DH), lambda i: (0, 0, 0)),
        out_shape=jax.ShapeDtypeStruct((HEADS, K_FIRST, DH), jnp.bfloat16),
        compiler_params=params(),
        cost_estimate=cost(0, 4 * K_FIRST * HEADS * DH),
        name="split_first",
    )(key_rows)


def run_copies(copies):
    for copy in copies:
        copy.start()
    for copy in copies:
        copy.wait()


def same_core(seq, chip_shift):
    core = lax.rem(seq, 2)
    at = lax.rem(seq + 2 * chip_shift + ROWS, ROWS)
    return at, at + 1 - 2 * core


def put_heads(seq, held, mine_ref, other_ref, sem):
    copies = []
    for chip in range(CHIPS):
        mine, other = same_core(seq, chip)
        copies.append(pltpu.make_async_copy(held.at[mine], mine_ref.at[chip], sem.at[2 * chip]))
        copies.append(
            pltpu.make_async_copy(held.at[other], other_ref.at[chip], sem.at[2 * chip + 1])
        )
    run_copies(copies)


def split_rest_kernel(seq_ref, key_ref, earlier_ref, mine_ref, other_ref, held, sem):
    for head in range(HEADS):
        held[head] = key_ref[pl.ds(K_FIRST, BLK - K_FIRST), pl.ds(head * DH, DH)]
    put_heads(seq_ref[0], held, mine_ref, other_ref, sem)


def turn_kernel(seq_ref, row_ref, earlier_ref, mine_ref, other_ref, held, sem):
    for head in range(HEADS):
        held[head] = row_ref[:, pl.ds(head * DH, DH)].T
    put_heads(seq_ref[0], held, mine_ref, other_ref, sem)


def by_core(kernel, seq, array, earlier, shape, name):
    return pl.pallas_call(
        kernel,
        in_specs=[smem_spec(), vmem_spec(), any_spec()],
        out_specs=[any_spec()] * 2,
        out_shape=[jax.ShapeDtypeStruct((CHIPS,) + shape, jnp.bfloat16)] * 2,
        scratch_shapes=[
            pltpu.VMEM((ROWS,) + shape, jnp.bfloat16),
            pltpu.SemaphoreType.DMA((ROWS,)),
        ],
        compiler_params=params(),
        cost_estimate=cost(0, 4 * ROWS * shape[0] * shape[1]),
        name=name,
    )(seq, array, earlier)


def pack_kernel(mine_ref, other_ref, *rest):
    piece_refs, sem = rest[:CHIPS], rest[CHIPS]
    copies = []
    for chip in range(CHIPS):
        copies.append(
            pltpu.make_async_copy(mine_ref.at[chip], piece_refs[chip].at[0], sem.at[2 * chip])
        )
        copies.append(
            pltpu.make_async_copy(other_ref.at[chip], piece_refs[chip].at[1], sem.at[2 * chip + 1])
        )
    run_copies(copies)


def pack(mine, other, name):
    shape = mine.shape[1:]
    return pl.pallas_call(
        pack_kernel,
        in_specs=[vmem_spec()] * 2,
        out_specs=[any_spec()] * CHIPS,
        out_shape=[jax.ShapeDtypeStruct((2,) + shape, jnp.bfloat16)] * CHIPS,
        scratch_shapes=[pltpu.SemaphoreType.DMA((ROWS,))],
        compiler_params=params(),
        cost_estimate=cost(0, 8 * CHIPS * shape[0] * shape[1]),
        name=name,
    )(mine, other)


def to_rows(seq, piece_refs, held, sem, start=0, rows=None):
    copies = []
    for chip in range(CHIPS):
        for which, row in enumerate(same_core(seq, -chip)):
            place = held.at[row] if rows is None else held.at[row, pl.ds(start, rows)]
            copies.append(
                pltpu.make_async_copy(piece_refs[chip].at[which], place, sem.at[2 * chip + which])
            )
    return copies


def nothing_kernel(*refs):
    pass


def after(arrays, earlier):
    count = len(arrays)
    return pl.pallas_call(
        nothing_kernel,
        in_specs=[any_spec()] * (count + len(earlier)),
        out_specs=[any_spec()] * count,
        out_shape=[jax.ShapeDtypeStruct(a.shape, a.dtype) for a in arrays],
        input_output_aliases={i: i for i in range(count)},
        cost_estimate=cost(0, 0),
        name="after",
    )(*arrays, *earlier)


def gather_kernel(parts, pieces, extra, seq_ref, block_ref, *rest):
    in_refs, rest = rest[: max(pieces, 1)], rest[max(pieces, 1) + extra :]
    if pieces:
        all_ref, rest = rest[0], rest[1:]
    send_refs, rest = rest[: len(parts)], rest[len(parts) :]
    if pieces:
        held, in_sem, out_sem = rest
        run_copies(to_rows(seq_ref[0], in_refs, held, in_sem))
        whole = pltpu.make_async_copy(held, all_ref, in_sem.at[0])
        whole.start()
    else:
        held, out_sem, whole = in_refs[0], rest[0], None

    start = 0
    for part, (rows, send_ref) in enumerate(zip(parts, send_refs)):

        def send(slot, carry, start=start, rows=rows, send_ref=send_ref, part=part):
            pltpu.make_async_copy(
                held.at[block_ref[slot], pl.ds(start, rows)], send_ref.at[slot], out_sem.at[part]
            ).start()
            return carry

        lax.fori_loop(0, ROWS * CAP, send, 0)
        start += rows
    for part, send_ref in enumerate(send_refs):
        pltpu.make_async_copy(send_ref, send_ref, out_sem.at[part]).wait()
    if whole is not None:
        whole.wait()


def gather(seq, send_block, arrays, parts, name, earlier=()):
    pieces = len(arrays) if len(arrays) > 1 else 0
    rows, columns = arrays[0].shape[-2:]
    out_shape = [jax.ShapeDtypeStruct((ROWS * CAP, part, columns), jnp.bfloat16) for part in parts]
    scratch = [pltpu.SemaphoreType.DMA((len(parts),))]
    in_specs = [vmem_spec()]
    if pieces:
        out_shape = [jax.ShapeDtypeStruct((ROWS, rows, columns), jnp.bfloat16)] + out_shape
        scratch = [
            pltpu.VMEM((ROWS, rows, columns), jnp.bfloat16),
            pltpu.SemaphoreType.DMA((ROWS,)),
        ] + scratch
        in_specs = [any_spec()] * pieces
    return pl.pallas_call(
        functools.partial(gather_kernel, parts, pieces, len(earlier)),
        in_specs=[smem_spec(), smem_spec()] + in_specs + [any_spec()] * len(earlier),
        out_specs=[any_spec()] * len(out_shape),
        out_shape=out_shape,
        scratch_shapes=scratch,
        compiler_params=params(),
        cost_estimate=cost(0, 2 * ROWS * (CAP + 1) * sum(parts) * columns),
        name=name,
    )(seq, send_block, *arrays, *earlier)


def weights_kernel(held_count, owner_ref, rank_ref, usable_ref, row_ref, seq_ref, own_a, own_b, *rest):
    picks, rest = rest[: 2 * TOPK], rest[2 * TOPK :]
    pieces, rest = rest[:CHIPS], rest[CHIPS + held_count :]
    weight_ref, inverse_ref, queries, scores, sem = rest
    row = row_ref[pl.program_id(0)]

    @pl.when(pl.program_id(0) == 0)
    def _():
        run_copies(to_rows(seq_ref[0], pieces, queries, sem))

    query = queries[row]
    key_pairs = [(own_a[0], own_b[0])] + [
        (picks[2 * j][0, 0], picks[2 * j + 1][0, 0]) for j in range(TOPK)
    ]

    def raw(pair):
        upper = jnp.dot(pair[0], query, preferred_element_type=jnp.float32)
        lower = jnp.dot(pair[1], query, preferred_element_type=jnp.float32)
        return upper * EXP2_SCALE, lower * EXP2_SCALE

    key_at = lax.broadcasted_iota(jnp.int32, (BLK, BLK), 0)
    query_at = lax.broadcasted_iota(jnp.int32, (BLK, BLK), 1)
    upper, lower = raw(key_pairs[0])
    own = jnp.where(query_at >= key_at, jnp.concatenate([upper, lower], axis=0), -jnp.inf)
    scores[0] = own
    top = jnp.max(own, axis=0, keepdims=True)
    inverse_ref[0] = top

    for j in range(TOPK):

        @pl.when(usable_ref[row * TOPK + j] > 0)
        def _(j=j):
            upper, lower = raw(key_pairs[1 + j])
            scores[1 + j, pl.ds(0, K_FIRST), :] = upper
            scores[1 + j, pl.ds(K_FIRST, BLK - K_FIRST), :] = lower
            inverse_ref[0] = jnp.maximum(
                inverse_ref[0],
                jnp.maximum(
                    jnp.max(upper, axis=0, keepdims=True), jnp.max(lower, axis=0, keepdims=True)
                ),
            )

    top = inverse_ref[0]
    exps = jnp.exp2(scores[0] - top)
    weight_ref[0, 0] = exps.astype(jnp.bfloat16)
    inverse_ref[0] = jnp.sum(exps, axis=0, keepdims=True)
    for j in range(TOPK):
        is_usable = usable_ref[row * TOPK + j] > 0

        @pl.when(is_usable)
        def _(j=j):
            exps = jnp.exp2(scores[1 + j] - top)
            weight_ref[0, 1 + j] = exps.astype(jnp.bfloat16)
            inverse_ref[0] = inverse_ref[0] + jnp.sum(exps, axis=0, keepdims=True)

        @pl.when(jnp.logical_not(is_usable))
        def _(j=j):
            weight_ref[0, 1 + j] = jnp.zeros((BLK, BLK), jnp.bfloat16)

    inverse_ref[0] = 1.0 / inverse_ref[0]


def make_weights(tables, seq, rows_at, query_pieces, own_a, own_b, got_a, got_b, held=()):
    owner, rank, usable = tables
    rest = BLK - K_FIRST
    steps = rows_at.shape[0]

    def pick(j, rows):
        def index(i, owner, rank, usable, at, seq):
            return (owner[at[i] * TOPK + j], rank[at[i] * TOPK + j], 0, 0)

        return pl.BlockSpec((1, 1, rows, DH), index)

    in_specs = [
        pl.BlockSpec((1, K_FIRST, DH), lambda i, o, r, u, at, s: (at[i], 0, 0)),
        pl.BlockSpec((1, rest, DH), lambda i, o, r, u, at, s: (at[i], 0, 0)),
    ]
    args = [own_a, own_b]
    for j in range(TOPK):
        in_specs += [pick(j, K_FIRST), pick(j, rest)]
        args += [got_a.reshape(ROWS, CAP, K_FIRST, DH), got_b.reshape(ROWS, CAP, rest, DH)]
    args += [*query_pieces, *held]
    in_specs += [any_spec()] * (CHIPS + len(held))
    blocks = steps * (1 + TOPK)
    prefetched = (owner, rank, usable, rows_at, seq)
    first_held = len(prefetched) + len(args) - len(held)
    return pl.pallas_call(
        functools.partial(weights_kernel, len(held)),
        grid_spec=pltpu.PrefetchScalarGridSpec(
            num_scalar_prefetch=len(prefetched),
            grid=(steps,),
            in_specs=in_specs,
            out_specs=[
                pl.BlockSpec(
                    (1, 1 + TOPK, BLK, BLK), lambda i, o, r, u, at, s: (at[i], 0, 0, 0)
                ),
                pl.BlockSpec((1, 1, BLK), lambda i, o, r, u, at, s: (at[i], 0, 0)),
            ],
            scratch_shapes=[
                pltpu.VMEM((ROWS, DH, BLK), jnp.bfloat16),
                pltpu.VMEM((1 + TOPK, BLK, BLK), jnp.float32),
                pltpu.SemaphoreType.DMA((ROWS,)),
            ],
        ),
        out_shape=[
            jax.ShapeDtypeStruct((ROWS, 1 + TOPK, BLK, BLK), jnp.bfloat16),
            jax.ShapeDtypeStruct((ROWS, 1, BLK), jnp.float32),
        ],
        input_output_aliases={first_held + i: i for i in range(len(held))},
        compiler_params=params(),
        cost_estimate=cost(
            2 * blocks * BLK * BLK * DH, 2 * blocks * (BLK * BLK + BLK * DH), blocks * BLK * BLK
        ),
        name="make_weights",
    )(*prefetched, *args)


def outputs_kernel(start, rows, owner_ref, rank_ref, row_ref, inverse_ref, *rest):
    weight_refs, rest = rest[: 1 + TOPK], rest[1 + TOPK :]
    own_ref, picks, out_ref = rest[0], rest[1 : 1 + TOPK], rest[1 + TOPK]
    total = jnp.dot(
        own_ref[0, pl.ds(start, rows), :], weight_refs[0][0, 0], preferred_element_type=jnp.float32
    )
    for j in range(TOPK):
        total += jnp.dot(
            picks[j][0, 0], weight_refs[1 + j][0, 0], preferred_element_type=jnp.float32
        )
    out_ref[0] = (total * inverse_ref[0]).astype(jnp.bfloat16)


def make_outputs(tables, rows_at, weights, inverse, values, got, start, rows):
    owner, rank, _ = tables
    steps = rows_at.shape[0]

    def pick(j):
        def index(step, owner, rank, row_at):
            at = row_at[step] * TOPK + j
            return (owner[at], rank[at], 0, 0)

        return pl.BlockSpec((1, 1, rows, BLK), index)

    blocks = steps * (1 + TOPK)
    return pl.pallas_call(
        functools.partial(outputs_kernel, start, rows),
        grid_spec=pltpu.PrefetchScalarGridSpec(
            num_scalar_prefetch=3,
            grid=(steps,),
            in_specs=[pl.BlockSpec((1, 1, BLK), lambda i, o, r, at: (at[i], 0, 0))]
            + [
                pl.BlockSpec((1, 1, BLK, BLK), lambda i, o, r, at, j=j: (at[i], j, 0, 0))
                for j in range(1 + TOPK)
            ]
            + [pl.BlockSpec((1, DH, BLK), lambda i, o, r, at: (at[i], 0, 0))]
            + [pick(j) for j in range(TOPK)],
            out_specs=pl.BlockSpec((1, rows, BLK), lambda i, *_: (i, 0, 0)),
        ),
        out_shape=jax.ShapeDtypeStruct((steps, rows, BLK), jnp.bfloat16),
        compiler_params=params(),
        cost_estimate=cost(2 * blocks * BLK * BLK * 128, 2 * blocks * BLK * (BLK + rows)),
        name="make_outputs",
    )(
        owner,
        rank,
        rows_at,
        inverse,
        *([weights] * (1 + TOPK)),
        values,
        *([got.reshape(ROWS, CAP, rows, BLK)] * TOPK),
    )


def finish_kernel(parts, seq_ref, *rest):
    pieces, (last_ref, out_ref, held, sem) = rest[:CHIPS], rest[CHIPS:]
    copies = to_rows(seq_ref[0], pieces, held, sem, 0, parts[0])
    for head in range(HEADS):
        copies.append(
            pltpu.make_async_copy(
                last_ref.at[head], held.at[head, pl.ds(parts[0], parts[1])], sem.at[ROWS + head]
            )
        )
    run_copies(copies)
    for head in range(HEADS):
        out_ref[:, pl.ds(head * DH, DH)] = held[head].T


def finish(seq, pieces, last, parts):
    return pl.pallas_call(
        functools.partial(finish_kernel, parts),
        in_specs=[smem_spec()] + [any_spec()] * (CHIPS + 1),
        out_specs=vmem_spec(),
        out_shape=jax.ShapeDtypeStruct((BLK, HEADS * DH), jnp.bfloat16),
        scratch_shapes=[
            pltpu.VMEM((HEADS, DH, BLK), jnp.bfloat16),
            pltpu.SemaphoreType.DMA((ROWS + HEADS,)),
        ],
        compiler_params=params(),
        cost_estimate=cost(0, 4 * BLK * HEADS * DH),
        name="finish",
    )(seq, *pieces, last)


def permute_seq(array, place):
    seq_count, grp_count = lax.axis_size("seq"), lax.axis_size("grp")
    pairs = [
        (s * grp_count + g, place(s) % seq_count * grp_count + g)
        for s in range(seq_count)
        for g in range(grp_count)
    ]
    return lax.ppermute(array, AXES, pairs)


def swap_cores(array):
    return permute_seq(array, lambda s: s ^ 1)


def along_chips(pieces, order):
    moved = {0: pieces[0]}
    for chip in order:
        moved[chip] = permute_seq(pieces[chip], lambda s, chip=chip: s + 2 * chip)
    return [moved[chip] for chip in range(CHIPS)]


def exchange(array, axis):
    return lax.all_to_all(array, axis, split_axis=0, concat_axis=0, tiled=True)


def routes(pick_column, pick_back):
    seq, grp = lax.axis_index("seq"), lax.axis_index("grp")
    requests = ROWS * TOPK
    target = lax.dynamic_index_in_dim(pick_column, seq, 1, keepdims=False).reshape(-1, requests)
    back = lax.dynamic_index_in_dim(pick_back, seq, 1, keepdims=False).reshape(-1, requests)
    column = jnp.arange(target.shape[0], dtype=jnp.int32)[:, None]
    row = (jnp.arange(requests, dtype=jnp.int32) // TOPK)[None, :]
    local_row = row - back - (target >= column).astype(jnp.int32)
    at = jnp.arange(requests, dtype=jnp.int32)
    earlier = at[:, None] > at[None, :]
    hits = target == grp
    place = jnp.sum(hits[:, None, :] & earlier[None], axis=2, dtype=jnp.int32)
    chosen = hits[:, None, :] & (
        place[:, None, :] == jnp.arange(CAP, dtype=jnp.int32)[None, :, None]
    )
    send_block = jnp.sum(
        jnp.where(chosen, jnp.maximum(local_row, 0)[:, None, :], 0), axis=2, dtype=jnp.int32
    ).reshape(-1)
    owner = lax.dynamic_index_in_dim(target, grp, 0, keepdims=False)
    rank = jnp.sum((owner[:, None] == owner[None, :]) & earlier, axis=1, dtype=jnp.int32)
    usable = (lax.dynamic_index_in_dim(local_row, grp, 0, keepdims=False) >= 0).astype(jnp.int32)
    return send_block, (owner, rank, usable)


def body(query_rows, key_rows, value_rows, pick_column, pick_back):
    seq = lax.axis_index("seq").astype(jnp.int32).reshape(1)
    rest = BLK - K_FIRST
    key_first = split_first(key_rows)
    own_a = exchange(key_first, "seq")
    mine, other = by_core(split_rest_kernel, seq, key_rows, key_first, (rest, DH), "split_rest")
    key_pieces = pack(mine, swap_cores(other), "pack_keys")
    mine, other = by_core(turn_kernel, seq, value_rows, key_first, (DH, BLK), "turn_values")
    value_pieces = pack(mine, swap_cores(other), "pack_values")
    mine, other = by_core(turn_kernel, seq, query_rows, key_first, (DH, BLK), "turn_queries")
    query_pieces = pack(mine, swap_cores(other), "pack_queries")

    send_block, tables = routes(pick_column, pick_back)
    ready = [key_pieces[0], value_pieces[0]]
    (send_a,) = gather(seq, send_block, [own_a], (K_FIRST,), "gather_a", earlier=ready)
    got_a = exchange(send_a, "grp")

    key_pieces = along_chips(after(key_pieces, [send_a]), FAR_FIRST)
    value_pieces = along_chips(after(value_pieces, [key_pieces[FAR_FIRST[2]]]), NEAR_FIRST)
    ready = [query_pieces[0]] + [value_pieces[chip] for chip in NEAR_FIRST[:2]]
    own_b, send_b = gather(seq, send_block, key_pieces, (rest,), "gather_b", earlier=ready)
    (send_b,) = after([send_b], [got_a])
    got_b = exchange(send_b, "grp")

    query_pieces = along_chips(after(query_pieces, [value_pieces[NEAR_FIRST[3]]]), NEAR_FIRST)
    ready = [query_pieces[chip] for chip in NEAR_FIRST[:2]]
    values, *sends = gather(
        seq, send_block, value_pieces, V_PARTS, "gather_values", earlier=ready
    )
    chips = jnp.arange(CHIPS, dtype=jnp.int32)
    same = (seq + 2 * chips) % ROWS
    opposite = same ^ 1
    inputs = (query_pieces, own_a, own_b, got_a, got_b)
    held = make_weights(tables, seq, opposite, *inputs)

    (send,) = after(sends[:1], [got_b] + [query_pieces[chip] for chip in NEAR_FIRST[2:6]])
    got = exchange(send, "grp")
    (send,) = after(sends[1:], [got, held[1]])
    weights, inverse = make_weights(tables, seq, same, *inputs, held=held)
    first = (weights, inverse, values, got, 0, V_PARTS[0])
    other = swap_cores(make_outputs(tables, opposite, *first))
    mine = make_outputs(tables, same, *first)
    pieces = along_chips(pack(mine, other, "pack_outputs"), FAR_FIRST)

    (got,) = after([exchange(send, "grp")], pieces[1:])
    second = (weights, inverse, values, got, V_PARTS[0], V_PARTS[1])
    outs = make_outputs(tables, jnp.arange(ROWS, dtype=jnp.int32), *second)
    return finish(seq, pieces, exchange(outs, "seq"), V_PARTS)


def solution(mesh):
    return jax.shard_map(
        body,
        mesh=mesh,
        in_specs=(P(AXES, None), P(AXES, None), P(AXES, None), P(), P()),
        out_specs=P(AXES, None),
        check_vma=False,
    )
```

```python
import functools

import jax
import jax.numpy as jnp
from jax import lax
from jax.experimental import pallas as pl
from jax.experimental.pallas import tpu as pltpu
from jax.sharding import PartitionSpec as P

HEADS = 16
DH = 128
BLK = 512
TOPK = 3
CAP = 4
ROWS = 16
CHIPS = ROWS // 2
V_PARTS = (64, 64)
CHIP_ORDER = (4, 3, 5, 2, 6, 1, 7)
EXP2_SCALE = DH ** (-0.5) * 1.4426950408889634
VMEM_BYTES = 56 * 1024 * 1024
AXES = ("seq", "grp")


def any_spec():
    return pl.BlockSpec(memory_space=pl.ANY)


def vmem_spec():
    return pl.BlockSpec(memory_space=pltpu.VMEM)


def smem_spec():
    return pl.BlockSpec(memory_space=pltpu.SMEM)


def params():
    return pltpu.CompilerParams(vmem_limit_bytes=VMEM_BYTES)


def cost(flops, moved, exps=0):
    return pl.CostEstimate(flops=flops, bytes_accessed=moved, transcendentals=exps)


def split_heads_kernel(row_ref, head_ref):
    for head in range(HEADS):
        head_ref[head] = row_ref[:, pl.ds(head * DH, DH)]


def split_heads(rows):
    return pl.pallas_call(
        split_heads_kernel,
        grid=(4,),
        in_specs=[pl.BlockSpec((BLK // 4, HEADS * DH), lambda i: (i, 0))],
        out_specs=pl.BlockSpec((HEADS, BLK // 4, DH), lambda i: (0, i, 0)),
        out_shape=jax.ShapeDtypeStruct((HEADS, BLK, DH), jnp.bfloat16),
        compiler_params=params(),
        cost_estimate=cost(0, 4 * BLK * HEADS * DH),
        name="split_heads",
    )(rows)


def run_copies(copies):
    for copy in copies:
        copy.start()
    for copy in copies:
        copy.wait()


def same_core(seq, chip_shift):
    core = lax.rem(seq, 2)
    at = lax.rem(seq + 2 * chip_shift + ROWS, ROWS)
    return at, at + 1 - 2 * core


def put_heads(seq, held, mine_ref, other_ref, sem):
    copies = []
    for chip in range(CHIPS):
        mine, other = same_core(seq, chip)
        copies.append(pltpu.make_async_copy(held.at[mine], mine_ref.at[chip], sem.at[2 * chip]))
        copies.append(
            pltpu.make_async_copy(held.at[other], other_ref.at[chip], sem.at[2 * chip + 1])
        )
    run_copies(copies)


def turn_kernel(seq_ref, value_ref, query_ref, earlier_ref, mine_ref, other_ref, held, sem):
    for head in range(HEADS):
        columns = pl.ds(head * DH, DH)
        held[head, pl.ds(0, DH), :] = value_ref[:, columns].T
        held[head, pl.ds(DH, DH), :] = query_ref[:, columns].T
    put_heads(seq_ref[0], held, mine_ref, other_ref, sem)


def turn(seq, value_rows, query_rows, earlier):
    shape = (2 * DH, BLK)
    return pl.pallas_call(
        turn_kernel,
        in_specs=[smem_spec(), vmem_spec(), vmem_spec(), any_spec()],
        out_specs=[any_spec()] * 2,
        out_shape=[jax.ShapeDtypeStruct((CHIPS,) + shape, jnp.bfloat16)] * 2,
        scratch_shapes=[
            pltpu.VMEM((ROWS,) + shape, jnp.bfloat16),
            pltpu.SemaphoreType.DMA((ROWS,)),
        ],
        compiler_params=params(),
        cost_estimate=cost(0, 4 * ROWS * shape[0] * shape[1]),
        name="turn",
    )(seq, value_rows, query_rows, earlier)


def pack_kernel(mine_ref, other_ref, *rest):
    piece_refs, sem = rest[:CHIPS], rest[CHIPS]
    copies = []
    for chip in range(CHIPS):
        copies.append(
            pltpu.make_async_copy(mine_ref.at[chip], piece_refs[chip].at[0], sem.at[2 * chip])
        )
        copies.append(
            pltpu.make_async_copy(other_ref.at[chip], piece_refs[chip].at[1], sem.at[2 * chip + 1])
        )
    run_copies(copies)


def pack(mine, other, name):
    shape = mine.shape[1:]
    return pl.pallas_call(
        pack_kernel,
        in_specs=[vmem_spec()] * 2,
        out_specs=[any_spec()] * CHIPS,
        out_shape=[jax.ShapeDtypeStruct((2,) + shape, jnp.bfloat16)] * CHIPS,
        scratch_shapes=[pltpu.SemaphoreType.DMA((ROWS,))],
        compiler_params=params(),
        cost_estimate=cost(0, 8 * CHIPS * shape[0] * shape[1]),
        name=name,
    )(mine, other)


def to_rows(seq, piece_refs, held, sem, start=0, rows=None):
    copies = []
    for chip in range(CHIPS):
        for which, row in enumerate(same_core(seq, -chip)):
            place = held.at[row] if rows is None else held.at[row, pl.ds(start, rows)]
            copies.append(
                pltpu.make_async_copy(piece_refs[chip].at[which], place, sem.at[2 * chip + which])
            )
    return copies


def nothing_kernel(*refs):
    pass


def after(arrays, earlier):
    count = len(arrays)
    return pl.pallas_call(
        nothing_kernel,
        in_specs=[any_spec()] * (count + len(earlier)),
        out_specs=[any_spec()] * count,
        out_shape=[jax.ShapeDtypeStruct(a.shape, a.dtype) for a in arrays],
        input_output_aliases={i: i for i in range(count)},
        cost_estimate=cost(0, 0),
        name="after",
    )(*arrays, *earlier)


def gather_kernel(parts, pieces, extra, seq_ref, block_ref, *rest):
    in_refs, rest = rest[: max(pieces, 1)], rest[max(pieces, 1) + extra :]
    if pieces:
        all_ref, rest = rest[0], rest[1:]
    send_refs, rest = rest[: len(parts)], rest[len(parts) :]
    if pieces:
        held, in_sem, out_sem = rest
        run_copies(to_rows(seq_ref[0], in_refs, held, in_sem))
        whole = pltpu.make_async_copy(held, all_ref, in_sem.at[0])
        whole.start()
    else:
        held, out_sem, whole = in_refs[0], rest[0], None

    start = 0
    for part, (rows, send_ref) in enumerate(zip(parts, send_refs)):

        def send(slot, carry, start=start, rows=rows, send_ref=send_ref, part=part):
            pltpu.make_async_copy(
                held.at[block_ref[slot], pl.ds(start, rows)], send_ref.at[slot], out_sem.at[part]
            ).start()
            return carry

        lax.fori_loop(0, ROWS * CAP, send, 0)
        start += rows
    for part, send_ref in enumerate(send_refs):
        pltpu.make_async_copy(send_ref, send_ref, out_sem.at[part]).wait()
    if whole is not None:
        whole.wait()


def gather(seq, send_block, arrays, parts, name, earlier=()):
    pieces = len(arrays) if len(arrays) > 1 else 0
    rows, columns = arrays[0].shape[-2:]
    out_shape = [jax.ShapeDtypeStruct((ROWS * CAP, part, columns), jnp.bfloat16) for part in parts]
    scratch = [pltpu.SemaphoreType.DMA((len(parts),))]
    in_specs = [vmem_spec()]
    if pieces:
        out_shape = [jax.ShapeDtypeStruct((ROWS, rows, columns), jnp.bfloat16)] + out_shape
        scratch = [
            pltpu.VMEM((ROWS, rows, columns), jnp.bfloat16),
            pltpu.SemaphoreType.DMA((ROWS,)),
        ] + scratch
        in_specs = [any_spec()] * pieces
    return pl.pallas_call(
        functools.partial(gather_kernel, parts, pieces, len(earlier)),
        in_specs=[smem_spec(), smem_spec()] + in_specs + [any_spec()] * len(earlier),
        out_specs=[any_spec()] * len(out_shape),
        out_shape=out_shape,
        scratch_shapes=scratch,
        compiler_params=params(),
        cost_estimate=cost(0, 2 * ROWS * (CAP + 1) * sum(parts) * columns),
        name=name,
    )(seq, send_block, *arrays, *earlier)


def weights_kernel(owner_ref, rank_ref, usable_ref, query_ref, own_ref, *rest):
    picks, (weight_ref, inverse_ref, scores) = rest[:TOPK], rest[TOPK:]
    row = pl.program_id(0)
    query = query_ref[0, 0]

    key_at = lax.broadcasted_iota(jnp.int32, (BLK, BLK), 0)
    query_at = lax.broadcasted_iota(jnp.int32, (BLK, BLK), 1)
    own = jnp.dot(own_ref[0], query, preferred_element_type=jnp.float32) * EXP2_SCALE
    own = jnp.where(query_at >= key_at, own, -jnp.inf)
    scores[0] = own
    inverse_ref[0] = jnp.max(own, axis=0, keepdims=True)

    for j in range(TOPK):

        @pl.when(usable_ref[row * TOPK + j] > 0)
        def _(j=j):
            picked = jnp.dot(picks[j][0, 0], query, preferred_element_type=jnp.float32)
            picked = picked * EXP2_SCALE
            scores[1 + j] = picked
            inverse_ref[0] = jnp.maximum(inverse_ref[0], jnp.max(picked, axis=0, keepdims=True))

    top = inverse_ref[0]
    exps = jnp.exp2(scores[0] - top)
    weight_ref[0, 0] = exps.astype(jnp.bfloat16)
    inverse_ref[0] = jnp.sum(exps, axis=0, keepdims=True)
    for j in range(TOPK):
        is_usable = usable_ref[row * TOPK + j] > 0

        @pl.when(is_usable)
        def _(j=j):
            exps = jnp.exp2(scores[1 + j] - top)
            weight_ref[0, 1 + j] = exps.astype(jnp.bfloat16)
            inverse_ref[0] = inverse_ref[0] + jnp.sum(exps, axis=0, keepdims=True)

        @pl.when(jnp.logical_not(is_usable))
        def _(j=j):
            weight_ref[0, 1 + j] = jnp.zeros((BLK, BLK), jnp.bfloat16)

    inverse_ref[0] = 1.0 / inverse_ref[0]


def make_weights(tables, vq_all, own_keys, got_keys):
    owner, rank, usable = tables

    def pick(j):
        def index(r, owner, rank, usable):
            return (owner[r * TOPK + j], rank[r * TOPK + j], 0, 0)

        return pl.BlockSpec((1, 1, BLK, DH), index)

    blocks = ROWS * (1 + TOPK)
    return pl.pallas_call(
        weights_kernel,
        grid_spec=pltpu.PrefetchScalarGridSpec(
            num_scalar_prefetch=3,
            grid=(ROWS,),
            in_specs=[
                pl.BlockSpec((1, 1, DH, BLK), lambda r, *_: (r, 1, 0, 0)),
                pl.BlockSpec((1, BLK, DH), lambda r, *_: (r, 0, 0)),
            ]
            + [pick(j) for j in range(TOPK)],
            out_specs=[
                pl.BlockSpec((1, 1 + TOPK, BLK, BLK), lambda r, *_: (r, 0, 0, 0)),
                pl.BlockSpec((1, 1, BLK), lambda r, *_: (r, 0, 0)),
            ],
            scratch_shapes=[pltpu.VMEM((1 + TOPK, BLK, BLK), jnp.float32)],
        ),
        out_shape=[
            jax.ShapeDtypeStruct((ROWS, 1 + TOPK, BLK, BLK), jnp.bfloat16),
            jax.ShapeDtypeStruct((ROWS, 1, BLK), jnp.float32),
        ],
        compiler_params=params(),
        cost_estimate=cost(
            2 * blocks * BLK * BLK * DH, 2 * blocks * (BLK * BLK + BLK * DH), blocks * BLK * BLK
        ),
        name="make_weights",
    )(
        owner,
        rank,
        usable,
        vq_all.reshape(ROWS, 2, DH, BLK),
        own_keys,
        *([got_keys.reshape(ROWS, CAP, BLK, DH)] * TOPK),
    )


def outputs_kernel(
    start, rows, owner_ref, rank_ref, usable_ref, row_ref, kept_ref, inverse_ref, *rest
):
    weight_refs, rest = rest[: 1 + TOPK], rest[1 + TOPK :]
    own_ref, picks, (out_ref, total) = rest[0], rest[1 : 1 + TOPK], rest[1 + TOPK :]
    row = row_ref[pl.program_id(0)]
    total[...] = jnp.dot(
        own_ref[0, pl.ds(start, rows), :], weight_refs[0][0, 0], preferred_element_type=jnp.float32
    )
    for j in range(TOPK):

        @pl.when(usable_ref[row * TOPK + j] > 0)
        def _(j=j):
            total[...] += jnp.dot(
                picks[j][0, 0], weight_refs[1 + j][0, 0], preferred_element_type=jnp.float32
            )

    out_ref[0] = (total[...] * inverse_ref[0]).astype(jnp.bfloat16)


def kept_rows(usable, rows_at):
    step = jnp.arange(rows_at.shape[0], dtype=jnp.int32)
    row = jnp.arange(ROWS, dtype=jnp.int32)
    table = usable.reshape(1, ROWS, TOPK)
    is_row = (rows_at[:, None] == row[None, :])[:, :, None]
    used = jnp.sum(jnp.where(is_row, table, 0), axis=1, dtype=jnp.int32)
    so_far = (step[None, :] <= step[:, None])[:, :, None] & (used > 0)[None]
    last = jnp.max(jnp.where(so_far, step[None, :, None], 0), axis=1)
    is_last = last[:, :, None] == step[None, None, :]
    return jnp.sum(jnp.where(is_last, rows_at[None, None, :], 0), axis=2, dtype=jnp.int32).reshape(-1)


def make_outputs(tables, rows_at, weights, inverse, values, got, start, rows):
    owner, rank, usable = tables
    steps = rows_at.shape[0]

    def pick(j):
        def index(i, owner, rank, usable, at, kept):
            place = kept[i * TOPK + j] * TOPK + j
            return (owner[place], rank[place], 0, 0)

        return pl.BlockSpec((1, 1, rows, BLK), index)

    def weight(j):
        def index(i, owner, rank, usable, at, kept):
            return (kept[i * TOPK + j], 1 + j, 0, 0)

        return pl.BlockSpec((1, 1, BLK, BLK), index)

    blocks = steps * (1 + TOPK)
    return pl.pallas_call(
        functools.partial(outputs_kernel, start, rows),
        grid_spec=pltpu.PrefetchScalarGridSpec(
            num_scalar_prefetch=5,
            grid=(steps,),
            in_specs=[
                pl.BlockSpec((1, 1, BLK), lambda i, o, r, u, at, k: (at[i], 0, 0)),
                pl.BlockSpec((1, 1, BLK, BLK), lambda i, o, r, u, at, k: (at[i], 0, 0, 0)),
            ]
            + [weight(j) for j in range(TOPK)]
            + [pl.BlockSpec((1, DH, BLK), lambda i, o, r, u, at, k: (at[i], 0, 0))]
            + [pick(j) for j in range(TOPK)],
            out_specs=pl.BlockSpec((1, rows, BLK), lambda i, *_: (i, 0, 0)),
            scratch_shapes=[pltpu.VMEM((rows, BLK), jnp.float32)],
        ),
        out_shape=jax.ShapeDtypeStruct((steps, rows, BLK), jnp.bfloat16),
        compiler_params=params(),
        cost_estimate=cost(2 * blocks * BLK * BLK * 128, 2 * blocks * BLK * (BLK + rows)),
        name="make_outputs",
    )(
        owner,
        rank,
        usable,
        rows_at,
        kept_rows(usable, rows_at),
        inverse,
        *([weights] * (1 + TOPK)),
        values,
        *([got.reshape(ROWS, CAP, rows, BLK)] * TOPK),
    )


def finish_kernel(parts, seq_ref, *rest):
    pieces, (last_ref, out_ref, held, sem) = rest[:CHIPS], rest[CHIPS:]
    copies = to_rows(seq_ref[0], pieces, held, sem, 0, parts[0])
    for head in range(HEADS):
        copies.append(
            pltpu.make_async_copy(
                last_ref.at[head], held.at[head, pl.ds(parts[0], parts[1])], sem.at[ROWS + head]
            )
        )
    run_copies(copies)
    for head in range(HEADS):
        out_ref[:, pl.ds(head * DH, DH)] = held[head].T


def finish(seq, pieces, last, parts):
    return pl.pallas_call(
        functools.partial(finish_kernel, parts),
        in_specs=[smem_spec()] + [any_spec()] * (CHIPS + 1),
        out_specs=vmem_spec(),
        out_shape=jax.ShapeDtypeStruct((BLK, HEADS * DH), jnp.bfloat16),
        scratch_shapes=[
            pltpu.VMEM((HEADS, DH, BLK), jnp.bfloat16),
            pltpu.SemaphoreType.DMA((ROWS + HEADS,)),
        ],
        compiler_params=params(),
        cost_estimate=cost(0, 4 * BLK * HEADS * DH),
        name="finish",
    )(seq, *pieces, last)


def permute_seq(array, place):
    seq_count, grp_count = lax.axis_size("seq"), lax.axis_size("grp")
    pairs = [
        (s * grp_count + g, place(s) % seq_count * grp_count + g)
        for s in range(seq_count)
        for g in range(grp_count)
    ]
    return lax.ppermute(array, AXES, pairs)


def swap_cores(array):
    return permute_seq(array, lambda s: s ^ 1)


def along_chips(pieces):
    moved = {0: pieces[0]}
    for chip in CHIP_ORDER:
        moved[chip] = permute_seq(pieces[chip], lambda s, chip=chip: s + 2 * chip)
    return [moved[chip] for chip in range(CHIPS)]


def exchange(array, axis):
    return lax.all_to_all(array, axis, split_axis=0, concat_axis=0, tiled=True)


def routes(pick_column, pick_back):
    seq, grp = lax.axis_index("seq"), lax.axis_index("grp")
    requests = ROWS * TOPK
    target = lax.dynamic_index_in_dim(pick_column, seq, 1, keepdims=False).reshape(-1, requests)
    back = lax.dynamic_index_in_dim(pick_back, seq, 1, keepdims=False).reshape(-1, requests)
    column = jnp.arange(target.shape[0], dtype=jnp.int32)[:, None]
    row = (jnp.arange(requests, dtype=jnp.int32) // TOPK)[None, :]
    local_row = row - back - (target >= column).astype(jnp.int32)
    at = jnp.arange(requests, dtype=jnp.int32)
    earlier = at[:, None] > at[None, :]
    hits = target == grp
    place = jnp.sum(hits[:, None, :] & earlier[None], axis=2, dtype=jnp.int32)
    chosen = hits[:, None, :] & (
        place[:, None, :] == jnp.arange(CAP, dtype=jnp.int32)[None, :, None]
    )
    send_block = jnp.sum(
        jnp.where(chosen, jnp.maximum(local_row, 0)[:, None, :], 0), axis=2, dtype=jnp.int32
    ).reshape(-1)
    owner = lax.dynamic_index_in_dim(target, grp, 0, keepdims=False)
    rank = jnp.sum((owner[:, None] == owner[None, :]) & earlier, axis=1, dtype=jnp.int32)
    usable = (lax.dynamic_index_in_dim(local_row, grp, 0, keepdims=False) >= 0).astype(jnp.int32)
    return send_block, (owner, rank, usable)


def body(query_rows, key_rows, value_rows, pick_column, pick_back):
    seq = lax.axis_index("seq").astype(jnp.int32).reshape(1)
    key_heads = split_heads(key_rows)
    own_keys = exchange(key_heads, "seq")
    mine, other = turn(seq, value_rows, query_rows, key_heads)
    pieces = pack(mine, swap_cores(other), "pack_inputs")
    send_block, tables = routes(pick_column, pick_back)
    (send_keys,) = gather(
        seq, send_block, [own_keys], (BLK,), "gather_keys", earlier=[pieces[0]]
    )
    got_keys = exchange(send_keys, "grp")

    pieces = along_chips(after(pieces, [send_keys]))
    vq_all, *sends = gather(seq, send_block, pieces, V_PARTS, "gather_values")
    weights, inverse = make_weights(tables, vq_all, own_keys, got_keys)
    (send,) = after(sends[:1], [got_keys])
    got = exchange(send, "grp")
    (send,) = after(sends[1:], [got, inverse])

    chips = jnp.arange(CHIPS, dtype=jnp.int32)
    same = (seq + 2 * chips) % ROWS
    first = (weights, inverse, vq_all, got, 0, V_PARTS[0])
    other = swap_cores(make_outputs(tables, same ^ 1, *first))
    mine = make_outputs(tables, same, *first)
    pieces = along_chips(pack(mine, other, "pack_outputs"))

    (got,) = after([exchange(send, "grp")], pieces[1:])
    second = (weights, inverse, vq_all, got, V_PARTS[0], V_PARTS[1])
    outs = make_outputs(tables, jnp.arange(ROWS, dtype=jnp.int32), *second)
    return finish(seq, pieces, exchange(outs, "seq"), V_PARTS)


def solution(mesh):
    return jax.shard_map(
        body,
        mesh=mesh,
        in_specs=(P(AXES, None), P(AXES, None), P(AXES, None), P(), P()),
        out_specs=P(AXES, None),
        check_vma=False,
    )
```

```python
import functools

import jax
import jax.numpy as jnp
from jax import lax
from jax.experimental import pallas as pl
from jax.experimental.pallas import tpu as pltpu
from jax.sharding import PartitionSpec as P

HEADS = 16
DH = 128
BLK = 512
TOPK = 3
CAP = 4
ROWS = 16
CHIPS = ROWS // 2
K_FIRST = 192
V_PARTS = (64, 64)
CHIP_ORDER = (4, 3, 5, 2, 6, 1, 7)
EXP2_SCALE = DH ** (-0.5) * 1.4426950408889634
VMEM_BYTES = 56 * 1024 * 1024
AXES = ("seq", "grp")


def any_spec():
    return pl.BlockSpec(memory_space=pl.ANY)


def vmem_spec():
    return pl.BlockSpec(memory_space=pltpu.VMEM)


def smem_spec():
    return pl.BlockSpec(memory_space=pltpu.SMEM)


def params():
    return pltpu.CompilerParams(vmem_limit_bytes=VMEM_BYTES)


def cost(flops, moved, exps=0):
    return pl.CostEstimate(flops=flops, bytes_accessed=moved, transcendentals=exps)


def split_first_kernel(key_ref, first_ref):
    for head in range(HEADS):
        first_ref[head] = key_ref[:, pl.ds(head * DH, DH)]


def split_first(key_rows):
    return pl.pallas_call(
        split_first_kernel,
        grid=(1,),
        in_specs=[pl.BlockSpec((K_FIRST, HEADS * DH), lambda i: (0, 0))],
        out_specs=pl.BlockSpec((HEADS, K_FIRST, DH), lambda i: (0, 0, 0)),
        out_shape=jax.ShapeDtypeStruct((HEADS, K_FIRST, DH), jnp.bfloat16),
        compiler_params=params(),
        cost_estimate=cost(0, 4 * K_FIRST * HEADS * DH),
        name="split_first",
    )(key_rows)


def run_copies(copies):
    for copy in copies:
        copy.start()
    for copy in copies:
        copy.wait()


def same_core(seq, chip_shift):
    core = lax.rem(seq, 2)
    at = lax.rem(seq + 2 * chip_shift + ROWS, ROWS)
    return at, at + 1 - 2 * core


def put_heads(seq, held, mine_ref, other_ref, sem):
    copies = []
    for chip in range(CHIPS):
        mine, other = same_core(seq, chip)
        copies.append(pltpu.make_async_copy(held.at[mine], mine_ref.at[chip], sem.at[2 * chip]))
        copies.append(
            pltpu.make_async_copy(held.at[other], other_ref.at[chip], sem.at[2 * chip + 1])
        )
    run_copies(copies)


def split_rest_kernel(seq_ref, key_ref, earlier_ref, mine_ref, other_ref, held, sem):
    for head in range(HEADS):
        held[head] = key_ref[pl.ds(K_FIRST, BLK - K_FIRST), pl.ds(head * DH, DH)]
    put_heads(seq_ref[0], held, mine_ref, other_ref, sem)


def turn_kernel(seq_ref, value_ref, query_ref, earlier_ref, *rest):
    outs, (early, late, sem) = rest[:4], rest[4:]
    rows = V_PARTS[0]
    for head in range(HEADS):
        columns = pl.ds(head * DH, DH)
        values = value_ref[:, columns].T
        early[head, pl.ds(0, rows), :] = values[:rows]
        early[head, pl.ds(rows, DH), :] = query_ref[:, columns].T
        late[head] = values[rows:]
    put_heads(seq_ref[0], early, outs[0], outs[1], sem)
    put_heads(seq_ref[0], late, outs[2], outs[3], sem)


def turn(seq, value_rows, query_rows, earlier):
    shapes = [(V_PARTS[0] + DH, BLK), (V_PARTS[1], BLK)]
    return pl.pallas_call(
        turn_kernel,
        in_specs=[smem_spec(), vmem_spec(), vmem_spec(), any_spec()],
        out_specs=[any_spec()] * 4,
        out_shape=[
            jax.ShapeDtypeStruct((CHIPS,) + shape, jnp.bfloat16)
            for shape in shapes
            for _ in range(2)
        ],
        scratch_shapes=[pltpu.VMEM((ROWS,) + shape, jnp.bfloat16) for shape in shapes]
        + [pltpu.SemaphoreType.DMA((ROWS,))],
        compiler_params=params(),
        cost_estimate=cost(0, 8 * BLK * HEADS * DH),
        name="turn",
    )(seq, value_rows, query_rows, earlier)


def split_rest(seq, key_rows, earlier):
    shape = (BLK - K_FIRST, DH)
    return pl.pallas_call(
        split_rest_kernel,
        in_specs=[smem_spec(), vmem_spec(), any_spec()],
        out_specs=[any_spec()] * 2,
        out_shape=[jax.ShapeDtypeStruct((CHIPS,) + shape, jnp.bfloat16)] * 2,
        scratch_shapes=[
            pltpu.VMEM((ROWS,) + shape, jnp.bfloat16),
            pltpu.SemaphoreType.DMA((ROWS,)),
        ],
        compiler_params=params(),
        cost_estimate=cost(0, 4 * ROWS * shape[0] * shape[1]),
        name="split_rest",
    )(seq, key_rows, earlier)


def pack_kernel(mine_ref, other_ref, *rest):
    piece_refs, sem = rest[:CHIPS], rest[CHIPS]
    copies = []
    for chip in range(CHIPS):
        copies.append(
            pltpu.make_async_copy(mine_ref.at[chip], piece_refs[chip].at[0], sem.at[2 * chip])
        )
        copies.append(
            pltpu.make_async_copy(other_ref.at[chip], piece_refs[chip].at[1], sem.at[2 * chip + 1])
        )
    run_copies(copies)


def pack(mine, other, name):
    shape = mine.shape[1:]
    return pl.pallas_call(
        pack_kernel,
        in_specs=[vmem_spec()] * 2,
        out_specs=[any_spec()] * CHIPS,
        out_shape=[jax.ShapeDtypeStruct((2,) + shape, jnp.bfloat16)] * CHIPS,
        scratch_shapes=[pltpu.SemaphoreType.DMA((ROWS,))],
        compiler_params=params(),
        cost_estimate=cost(0, 8 * CHIPS * shape[0] * shape[1]),
        name=name,
    )(mine, other)


def to_rows(seq, piece_refs, held, sem, start=0, rows=None):
    copies = []
    for chip in range(CHIPS):
        for which, row in enumerate(same_core(seq, -chip)):
            place = held.at[row] if rows is None else held.at[row, pl.ds(start, rows)]
            copies.append(
                pltpu.make_async_copy(piece_refs[chip].at[which], place, sem.at[2 * chip + which])
            )
    return copies


def nothing_kernel(*refs):
    pass


def after(arrays, earlier):
    count = len(arrays)
    return pl.pallas_call(
        nothing_kernel,
        in_specs=[any_spec()] * (count + len(earlier)),
        out_specs=[any_spec()] * count,
        out_shape=[jax.ShapeDtypeStruct(a.shape, a.dtype) for a in arrays],
        input_output_aliases={i: i for i in range(count)},
        cost_estimate=cost(0, 0),
        name="after",
    )(*arrays, *earlier)


def gather_kernel(parts, pieces, extra, seq_ref, block_ref, *rest):
    in_refs, rest = rest[: max(pieces, 1)], rest[max(pieces, 1) + extra :]
    if pieces:
        all_ref, rest = rest[0], rest[1:]
    send_refs, rest = rest[: len(parts)], rest[len(parts) :]
    if pieces:
        held, in_sem, out_sem = rest
        run_copies(to_rows(seq_ref[0], in_refs, held, in_sem))
        whole = pltpu.make_async_copy(held, all_ref, in_sem.at[0])
        whole.start()
    else:
        held, out_sem, whole = in_refs[0], rest[0], None

    start = 0
    for part, (rows, send_ref) in enumerate(zip(parts, send_refs)):

        def send(slot, carry, start=start, rows=rows, send_ref=send_ref, part=part):
            pltpu.make_async_copy(
                held.at[block_ref[slot], pl.ds(start, rows)], send_ref.at[slot], out_sem.at[part]
            ).start()
            return carry

        lax.fori_loop(0, ROWS * CAP, send, 0)
        start += rows
    for part, send_ref in enumerate(send_refs):
        pltpu.make_async_copy(send_ref, send_ref, out_sem.at[part]).wait()
    if whole is not None:
        whole.wait()


def gather(seq, send_block, arrays, parts, name, earlier=()):
    pieces = len(arrays) if len(arrays) > 1 else 0
    rows, columns = arrays[0].shape[-2:]
    out_shape = [jax.ShapeDtypeStruct((ROWS * CAP, part, columns), jnp.bfloat16) for part in parts]
    scratch = [pltpu.SemaphoreType.DMA((len(parts),))]
    in_specs = [vmem_spec()]
    if pieces:
        out_shape = [jax.ShapeDtypeStruct((ROWS, rows, columns), jnp.bfloat16)] + out_shape
        scratch = [
            pltpu.VMEM((ROWS, rows, columns), jnp.bfloat16),
            pltpu.SemaphoreType.DMA((ROWS,)),
        ] + scratch
        in_specs = [any_spec()] * pieces
    return pl.pallas_call(
        functools.partial(gather_kernel, parts, pieces, len(earlier)),
        in_specs=[smem_spec(), smem_spec()] + in_specs + [any_spec()] * len(earlier),
        out_specs=[any_spec()] * len(out_shape),
        out_shape=out_shape,
        scratch_shapes=scratch,
        compiler_params=params(),
        cost_estimate=cost(0, 2 * ROWS * (CAP + 1) * sum(parts) * columns),
        name=name,
    )(seq, send_block, *arrays, *earlier)


def weights_kernel(owner_ref, rank_ref, usable_ref, query_ref, own_a, own_b, *rest):
    picks, (weight_ref, inverse_ref, scores) = rest[: 2 * TOPK], rest[2 * TOPK :]
    row = pl.program_id(0)
    query = query_ref[0, pl.ds(V_PARTS[0], DH), :]
    key_pairs = [(own_a[0], own_b[0])] + [
        (picks[2 * j][0, 0], picks[2 * j + 1][0, 0]) for j in range(TOPK)
    ]

    def raw(pair):
        upper = jnp.dot(pair[0], query, preferred_element_type=jnp.float32)
        lower = jnp.dot(pair[1], query, preferred_element_type=jnp.float32)
        return upper * EXP2_SCALE, lower * EXP2_SCALE

    key_at = lax.broadcasted_iota(jnp.int32, (BLK, BLK), 0)
    query_at = lax.broadcasted_iota(jnp.int32, (BLK, BLK), 1)
    upper, lower = raw(key_pairs[0])
    own = jnp.where(query_at >= key_at, jnp.concatenate([upper, lower], axis=0), -jnp.inf)
    scores[0] = own
    top = jnp.max(own, axis=0, keepdims=True)
    inverse_ref[0] = top

    for j in range(TOPK):

        @pl.when(usable_ref[row * TOPK + j] > 0)
        def _(j=j):
            upper, lower = raw(key_pairs[1 + j])
            scores[1 + j, pl.ds(0, K_FIRST), :] = upper
            scores[1 + j, pl.ds(K_FIRST, BLK - K_FIRST), :] = lower
            inverse_ref[0] = jnp.maximum(
                inverse_ref[0],
                jnp.maximum(
                    jnp.max(upper, axis=0, keepdims=True), jnp.max(lower, axis=0, keepdims=True)
                ),
            )

    top = inverse_ref[0]
    exps = jnp.exp2(scores[0] - top)
    weight_ref[0, 0] = exps.astype(jnp.bfloat16)
    inverse_ref[0] = jnp.sum(exps, axis=0, keepdims=True)
    for j in range(TOPK):
        is_usable = usable_ref[row * TOPK + j] > 0

        @pl.when(is_usable)
        def _(j=j):
            exps = jnp.exp2(scores[1 + j] - top)
            weight_ref[0, 1 + j] = exps.astype(jnp.bfloat16)
            inverse_ref[0] = inverse_ref[0] + jnp.sum(exps, axis=0, keepdims=True)

        @pl.when(jnp.logical_not(is_usable))
        def _(j=j):
            weight_ref[0, 1 + j] = jnp.zeros((BLK, BLK), jnp.bfloat16)

    inverse_ref[0] = 1.0 / inverse_ref[0]


def make_weights(tables, vq_all, own_a, own_b, got_a, got_b):
    owner, rank, usable = tables
    rest = BLK - K_FIRST

    def pick(j, rows):
        def index(r, owner, rank, usable):
            return (owner[r * TOPK + j], rank[r * TOPK + j], 0, 0)

        return pl.BlockSpec((1, 1, rows, DH), index)

    in_specs = [
        pl.BlockSpec((1, V_PARTS[0] + DH, BLK), lambda r, *_: (r, 0, 0)),
        pl.BlockSpec((1, K_FIRST, DH), lambda r, *_: (r, 0, 0)),
        pl.BlockSpec((1, rest, DH), lambda r, *_: (r, 0, 0)),
    ]
    args = [vq_all, own_a, own_b]
    for j in range(TOPK):
        in_specs += [pick(j, K_FIRST), pick(j, rest)]
        args += [got_a.reshape(ROWS, CAP, K_FIRST, DH), got_b.reshape(ROWS, CAP, rest, DH)]
    blocks = ROWS * (1 + TOPK)
    return pl.pallas_call(
        weights_kernel,
        grid_spec=pltpu.PrefetchScalarGridSpec(
            num_scalar_prefetch=3,
            grid=(ROWS,),
            in_specs=in_specs,
            out_specs=[
                pl.BlockSpec((1, 1 + TOPK, BLK, BLK), lambda r, *_: (r, 0, 0, 0)),
                pl.BlockSpec((1, 1, BLK), lambda r, *_: (r, 0, 0)),
            ],
            scratch_shapes=[pltpu.VMEM((1 + TOPK, BLK, BLK), jnp.float32)],
        ),
        out_shape=[
            jax.ShapeDtypeStruct((ROWS, 1 + TOPK, BLK, BLK), jnp.bfloat16),
            jax.ShapeDtypeStruct((ROWS, 1, BLK), jnp.float32),
        ],
        compiler_params=params(),
        cost_estimate=cost(
            2 * blocks * BLK * BLK * DH, 2 * blocks * (BLK * BLK + BLK * DH), blocks * BLK * BLK
        ),
        name="make_weights",
    )(owner, rank, usable, *args)


def outputs_kernel(rows, owner_ref, rank_ref, row_ref, inverse_ref, *rest):
    weight_refs, rest = rest[: 1 + TOPK], rest[1 + TOPK :]
    own_ref, picks, out_ref = rest[0], rest[1 : 1 + TOPK], rest[1 + TOPK]
    total = jnp.dot(
        own_ref[0, pl.ds(0, rows), :], weight_refs[0][0, 0], preferred_element_type=jnp.float32
    )
    for j in range(TOPK):
        total += jnp.dot(
            picks[j][0, 0], weight_refs[1 + j][0, 0], preferred_element_type=jnp.float32
        )
    out_ref[0] = (total * inverse_ref[0]).astype(jnp.bfloat16)


def make_outputs(tables, rows_at, weights, inverse, values, got, rows):
    owner, rank, _ = tables
    steps = rows_at.shape[0]

    def pick(j):
        def index(step, owner, rank, row_at):
            at = row_at[step] * TOPK + j
            return (owner[at], rank[at], 0, 0)

        return pl.BlockSpec((1, 1, rows, BLK), index)

    blocks = steps * (1 + TOPK)
    return pl.pallas_call(
        functools.partial(outputs_kernel, rows),
        grid_spec=pltpu.PrefetchScalarGridSpec(
            num_scalar_prefetch=3,
            grid=(steps,),
            in_specs=[pl.BlockSpec((1, 1, BLK), lambda i, o, r, at: (at[i], 0, 0))]
            + [
                pl.BlockSpec((1, 1, BLK, BLK), lambda i, o, r, at, j=j: (at[i], j, 0, 0))
                for j in range(1 + TOPK)
            ]
            + [pl.BlockSpec((1, values.shape[1], BLK), lambda i, o, r, at: (at[i], 0, 0))]
            + [pick(j) for j in range(TOPK)],
            out_specs=pl.BlockSpec((1, rows, BLK), lambda i, *_: (i, 0, 0)),
        ),
        out_shape=jax.ShapeDtypeStruct((steps, rows, BLK), jnp.bfloat16),
        compiler_params=params(),
        cost_estimate=cost(2 * blocks * BLK * BLK * 128, 2 * blocks * BLK * (BLK + rows)),
        name="make_outputs",
    )(
        owner,
        rank,
        rows_at,
        inverse,
        *([weights] * (1 + TOPK)),
        values,
        *([got.reshape(ROWS, CAP, rows, BLK)] * TOPK),
    )


def finish_kernel(parts, seq_ref, *rest):
    pieces, (last_ref, out_ref, held, sem) = rest[:CHIPS], rest[CHIPS:]
    copies = to_rows(seq_ref[0], pieces, held, sem, 0, parts[0])
    for head in range(HEADS):
        copies.append(
            pltpu.make_async_copy(
                last_ref.at[head], held.at[head, pl.ds(parts[0], parts[1])], sem.at[ROWS + head]
            )
        )
    run_copies(copies)
    for head in range(HEADS):
        out_ref[:, pl.ds(head * DH, DH)] = held[head].T


def finish(seq, pieces, last, parts):
    return pl.pallas_call(
        functools.partial(finish_kernel, parts),
        in_specs=[smem_spec()] + [any_spec()] * (CHIPS + 1),
        out_specs=vmem_spec(),
        out_shape=jax.ShapeDtypeStruct((BLK, HEADS * DH), jnp.bfloat16),
        scratch_shapes=[
            pltpu.VMEM((HEADS, DH, BLK), jnp.bfloat16),
            pltpu.SemaphoreType.DMA((ROWS + HEADS,)),
        ],
        compiler_params=params(),
        cost_estimate=cost(0, 4 * BLK * HEADS * DH),
        name="finish",
    )(seq, *pieces, last)


def permute_seq(array, place):
    seq_count, grp_count = lax.axis_size("seq"), lax.axis_size("grp")
    pairs = [
        (s * grp_count + g, place(s) % seq_count * grp_count + g)
        for s in range(seq_count)
        for g in range(grp_count)
    ]
    return lax.ppermute(array, AXES, pairs)


def swap_cores(array):
    return permute_seq(array, lambda s: s ^ 1)


def along_chips(pieces):
    moved = {0: pieces[0]}
    for chip in CHIP_ORDER:
        moved[chip] = permute_seq(pieces[chip], lambda s, chip=chip: s + 2 * chip)
    return [moved[chip] for chip in range(CHIPS)]


def exchange(array, axis):
    return lax.all_to_all(array, axis, split_axis=0, concat_axis=0, tiled=True)


def routes(pick_column, pick_back):
    seq, grp = lax.axis_index("seq"), lax.axis_index("grp")
    requests = ROWS * TOPK
    target = lax.dynamic_index_in_dim(pick_column, seq, 1, keepdims=False).reshape(-1, requests)
    back = lax.dynamic_index_in_dim(pick_back, seq, 1, keepdims=False).reshape(-1, requests)
    column = jnp.arange(target.shape[0], dtype=jnp.int32)[:, None]
    row = (jnp.arange(requests, dtype=jnp.int32) // TOPK)[None, :]
    local_row = row - back - (target >= column).astype(jnp.int32)
    at = jnp.arange(requests, dtype=jnp.int32)
    earlier = at[:, None] > at[None, :]
    hits = target == grp
    place = jnp.sum(hits[:, None, :] & earlier[None], axis=2, dtype=jnp.int32)
    chosen = hits[:, None, :] & (
        place[:, None, :] == jnp.arange(CAP, dtype=jnp.int32)[None, :, None]
    )
    send_block = jnp.sum(
        jnp.where(chosen, jnp.maximum(local_row, 0)[:, None, :], 0), axis=2, dtype=jnp.int32
    ).reshape(-1)
    owner = lax.dynamic_index_in_dim(target, grp, 0, keepdims=False)
    rank = jnp.sum((owner[:, None] == owner[None, :]) & earlier, axis=1, dtype=jnp.int32)
    usable = (lax.dynamic_index_in_dim(local_row, grp, 0, keepdims=False) >= 0).astype(jnp.int32)
    return send_block, (owner, rank, usable)


def body(query_rows, key_rows, value_rows, pick_column, pick_back):
    seq = lax.axis_index("seq").astype(jnp.int32).reshape(1)
    rest = BLK - K_FIRST
    key_first = split_first(key_rows)
    own_a = exchange(key_first, "seq")
    mine, other = split_rest(seq, key_rows, key_first)
    key_pieces = pack(mine, swap_cores(other), "pack_keys")
    mine, other, mine_late, other_late = turn(seq, value_rows, query_rows, key_first)
    early_pieces = pack(mine, swap_cores(other), "pack_early")
    late_pieces = pack(mine_late, swap_cores(other_late), "pack_late")

    send_block, tables = routes(pick_column, pick_back)
    ready = [key_pieces[0], early_pieces[0]]
    (send_a,) = gather(seq, send_block, [own_a], (K_FIRST,), "gather_a", earlier=ready)
    got_a = exchange(send_a, "grp")

    key_pieces = along_chips(after(key_pieces, [send_a]))
    own_b, send_b = gather(
        seq, send_block, key_pieces, (rest,), "gather_b", earlier=[late_pieces[0]]
    )
    (send_b,) = after([send_b], [got_a])
    got_b = exchange(send_b, "grp")

    early_pieces = along_chips(after(early_pieces, [key_pieces[CHIP_ORDER[2]]]))
    early, send = gather(seq, send_block, early_pieces, V_PARTS[:1], "gather_early")
    late_pieces = along_chips(after(late_pieces, [send]))
    (send,) = after([send], [got_b])
    got = exchange(send, "grp")
    late, send = gather(seq, send_block, late_pieces, V_PARTS[1:], "gather_late")
    weights, inverse = make_weights(tables, early, own_a, own_b, got_a, got_b)
    (send,) = after([send], [got, inverse])

    chips = jnp.arange(CHIPS, dtype=jnp.int32)
    same = (seq + 2 * chips) % ROWS
    first = (weights, inverse, early, got, V_PARTS[0])
    other = swap_cores(make_outputs(tables, same ^ 1, *first))
    mine = make_outputs(tables, same, *first)
    pieces = along_chips(pack(mine, other, "pack_outputs"))

    (got,) = after([exchange(send, "grp")], pieces[1:])
    second = (weights, inverse, late, got, V_PARTS[1])
    outs = make_outputs(tables, jnp.arange(ROWS, dtype=jnp.int32), *second)
    return finish(seq, pieces, exchange(outs, "seq"), V_PARTS)


def solution(mesh):
    return jax.shard_map(
        body,
        mesh=mesh,
        in_specs=(P(AXES, None), P(AXES, None), P(AXES, None), P(), P()),
        out_specs=P(AXES, None),
        check_vma=False,
    )
```

```python
import functools

import jax
import jax.numpy as jnp
from jax import lax
from jax.experimental import pallas as pl
from jax.experimental.pallas import tpu as pltpu
from jax.sharding import PartitionSpec as P

HEADS = 16
DH = 128
BLK = 512
TOPK = 3
CAP = 4
ROWS = 16
CHIPS = ROWS // 2
K_FIRST = 192
HALF = BLK // 2
CHIP_ORDER = (4, 3, 5, 2, 6, 1, 7)
EXP2_SCALE = DH ** (-0.5) * 1.4426950408889634
VMEM_BYTES = 56 * 1024 * 1024
AXES = ("seq", "grp")


def any_spec():
    return pl.BlockSpec(memory_space=pl.ANY)


def vmem_spec():
    return pl.BlockSpec(memory_space=pltpu.VMEM)


def smem_spec():
    return pl.BlockSpec(memory_space=pltpu.SMEM)


def params():
    return pltpu.CompilerParams(vmem_limit_bytes=VMEM_BYTES)


def cost(flops, moved, exps=0):
    return pl.CostEstimate(flops=flops, bytes_accessed=moved, transcendentals=exps)


def split_first_kernel(key_ref, first_ref):
    for head in range(HEADS):
        first_ref[head] = key_ref[:, pl.ds(head * DH, DH)]


def split_first(key_rows):
    return pl.pallas_call(
        split_first_kernel,
        grid=(1,),
        in_specs=[pl.BlockSpec((K_FIRST, HEADS * DH), lambda i: (0, 0))],
        out_specs=pl.BlockSpec((HEADS, K_FIRST, DH), lambda i: (0, 0, 0)),
        out_shape=jax.ShapeDtypeStruct((HEADS, K_FIRST, DH), jnp.bfloat16),
        compiler_params=params(),
        cost_estimate=cost(0, 4 * K_FIRST * HEADS * DH),
        name="split_first",
    )(key_rows)


def run_copies(copies):
    for copy in copies:
        copy.start()
    for copy in copies:
        copy.wait()


def same_core(seq, chip_shift):
    core = lax.rem(seq, 2)
    at = lax.rem(seq + 2 * chip_shift + ROWS, ROWS)
    return at, at + 1 - 2 * core


def put_heads(seq, held, mine_ref, other_ref, sem):
    copies = []
    for chip in range(CHIPS):
        mine, other = same_core(seq, chip)
        copies.append(pltpu.make_async_copy(held.at[mine], mine_ref.at[chip], sem.at[2 * chip]))
        copies.append(
            pltpu.make_async_copy(held.at[other], other_ref.at[chip], sem.at[2 * chip + 1])
        )
    run_copies(copies)


def split_rest_kernel(seq_ref, key_ref, earlier_ref, mine_ref, other_ref, held, sem):
    for head in range(HEADS):
        held[head] = key_ref[pl.ds(K_FIRST, BLK - K_FIRST), pl.ds(head * DH, DH)]
    put_heads(seq_ref[0], held, mine_ref, other_ref, sem)


def turn_kernel(seq_ref, row_ref, earlier_ref, mine_ref, other_ref, held, sem):
    for head in range(HEADS):
        held[head] = row_ref[:, pl.ds(head * DH, DH)].T
    put_heads(seq_ref[0], held, mine_ref, other_ref, sem)


def by_core(kernel, seq, array, earlier, shape, name):
    return pl.pallas_call(
        kernel,
        in_specs=[smem_spec(), vmem_spec(), any_spec()],
        out_specs=[any_spec()] * 2,
        out_shape=[jax.ShapeDtypeStruct((CHIPS,) + shape, jnp.bfloat16)] * 2,
        scratch_shapes=[
            pltpu.VMEM((ROWS,) + shape, jnp.bfloat16),
            pltpu.SemaphoreType.DMA((ROWS,)),
        ],
        compiler_params=params(),
        cost_estimate=cost(0, 4 * ROWS * shape[0] * shape[1]),
        name=name,
    )(seq, array, earlier)


def pack_kernel(mine_ref, other_ref, *rest):
    piece_refs, sem = rest[:CHIPS], rest[CHIPS]
    copies = []
    for chip in range(CHIPS):
        copies.append(
            pltpu.make_async_copy(mine_ref.at[chip], piece_refs[chip].at[0], sem.at[2 * chip])
        )
        copies.append(
            pltpu.make_async_copy(other_ref.at[chip], piece_refs[chip].at[1], sem.at[2 * chip + 1])
        )
    run_copies(copies)


def pack(mine, other, name):
    shape = mine.shape[1:]
    return pl.pallas_call(
        pack_kernel,
        in_specs=[vmem_spec()] * 2,
        out_specs=[any_spec()] * CHIPS,
        out_shape=[jax.ShapeDtypeStruct((2,) + shape, jnp.bfloat16)] * CHIPS,
        scratch_shapes=[pltpu.SemaphoreType.DMA((ROWS,))],
        compiler_params=params(),
        cost_estimate=cost(0, 8 * CHIPS * shape[0] * shape[1]),
        name=name,
    )(mine, other)


def to_rows(seq, piece_refs, held, sem, start=0, rows=None):
    copies = []
    for chip in range(CHIPS):
        for which, row in enumerate(same_core(seq, -chip)):
            place = held.at[row] if rows is None else held.at[row, pl.ds(start, rows)]
            copies.append(
                pltpu.make_async_copy(piece_refs[chip].at[which], place, sem.at[2 * chip + which])
            )
    return copies


def nothing_kernel(*refs):
    pass


def after(arrays, earlier):
    count = len(arrays)
    return pl.pallas_call(
        nothing_kernel,
        in_specs=[any_spec()] * (count + len(earlier)),
        out_specs=[any_spec()] * count,
        out_shape=[jax.ShapeDtypeStruct(a.shape, a.dtype) for a in arrays],
        input_output_aliases={i: i for i in range(count)},
        cost_estimate=cost(0, 0),
        name="after",
    )(*arrays, *earlier)


def gather_kernel(parts, pieces, extra, seq_ref, block_ref, *rest):
    in_refs, rest = rest[: max(pieces, 1)], rest[max(pieces, 1) + extra :]
    if pieces:
        all_ref, rest = rest[0], rest[1:]
    send_refs, rest = rest[: len(parts)], rest[len(parts) :]
    if pieces:
        held, in_sem, out_sem = rest
        run_copies(to_rows(seq_ref[0], in_refs, held, in_sem))
        whole = pltpu.make_async_copy(held, all_ref, in_sem.at[0])
        whole.start()
    else:
        held, out_sem, whole = in_refs[0], rest[0], None

    start = 0
    for part, (rows, send_ref) in enumerate(zip(parts, send_refs)):

        def send(slot, carry, start=start, rows=rows, send_ref=send_ref, part=part):
            pltpu.make_async_copy(
                held.at[block_ref[slot], pl.ds(start, rows)], send_ref.at[slot], out_sem.at[part]
            ).start()
            return carry

        lax.fori_loop(0, ROWS * CAP, send, 0)
        start += rows
    for part, send_ref in enumerate(send_refs):
        pltpu.make_async_copy(send_ref, send_ref, out_sem.at[part]).wait()
    if whole is not None:
        whole.wait()


def gather(seq, send_block, arrays, parts, name, earlier=()):
    pieces = len(arrays) if len(arrays) > 1 else 0
    rows, columns = arrays[0].shape[-2:]
    out_shape = [jax.ShapeDtypeStruct((ROWS * CAP, part, columns), jnp.bfloat16) for part in parts]
    scratch = [pltpu.SemaphoreType.DMA((len(parts),))]
    in_specs = [vmem_spec()]
    if pieces:
        out_shape = [jax.ShapeDtypeStruct((ROWS, rows, columns), jnp.bfloat16)] + out_shape
        scratch = [
            pltpu.VMEM((ROWS, rows, columns), jnp.bfloat16),
            pltpu.SemaphoreType.DMA((ROWS,)),
        ] + scratch
        in_specs = [any_spec()] * pieces
    return pl.pallas_call(
        functools.partial(gather_kernel, parts, pieces, len(earlier)),
        in_specs=[smem_spec(), smem_spec()] + in_specs + [any_spec()] * len(earlier),
        out_specs=[any_spec()] * len(out_shape),
        out_shape=out_shape,
        scratch_shapes=scratch,
        compiler_params=params(),
        cost_estimate=cost(0, 2 * ROWS * (CAP + 1) * sum(parts) * columns),
        name=name,
    )(seq, send_block, *arrays, *earlier)


def weights_kernel(held_count, owner_ref, rank_ref, usable_ref, row_ref, seq_ref, own_a, own_b, *rest):
    picks, rest = rest[: 2 * TOPK], rest[2 * TOPK :]
    pieces, rest = rest[:CHIPS], rest[CHIPS + held_count :]
    weight_ref, inverse_ref, queries, scores, sem = rest
    row = row_ref[pl.program_id(0)]

    @pl.when(pl.program_id(0) == 0)
    def _():
        run_copies(to_rows(seq_ref[0], pieces, queries, sem))

    query = queries[row]
    key_pairs = [(own_a[0], own_b[0])] + [
        (picks[2 * j][0, 0], picks[2 * j + 1][0, 0]) for j in range(TOPK)
    ]

    def raw(pair):
        upper = jnp.dot(pair[0], query, preferred_element_type=jnp.float32)
        lower = jnp.dot(pair[1], query, preferred_element_type=jnp.float32)
        return upper * EXP2_SCALE, lower * EXP2_SCALE

    key_at = lax.broadcasted_iota(jnp.int32, (BLK, BLK), 0)
    query_at = lax.broadcasted_iota(jnp.int32, (BLK, BLK), 1)
    upper, lower = raw(key_pairs[0])
    own = jnp.where(query_at >= key_at, jnp.concatenate([upper, lower], axis=0), -jnp.inf)
    scores[0] = own
    top = jnp.max(own, axis=0, keepdims=True)
    inverse_ref[0] = top

    for j in range(TOPK):

        @pl.when(usable_ref[row * TOPK + j] > 0)
        def _(j=j):
            upper, lower = raw(key_pairs[1 + j])
            scores[1 + j, pl.ds(0, K_FIRST), :] = upper
            scores[1 + j, pl.ds(K_FIRST, BLK - K_FIRST), :] = lower
            inverse_ref[0] = jnp.maximum(
                inverse_ref[0],
                jnp.maximum(
                    jnp.max(upper, axis=0, keepdims=True), jnp.max(lower, axis=0, keepdims=True)
                ),
            )

    top = inverse_ref[0]
    exps = jnp.exp2(scores[0] - top)
    weight_ref[0, 0] = exps.astype(jnp.bfloat16)
    inverse_ref[0] = jnp.sum(exps, axis=0, keepdims=True)
    for j in range(TOPK):
        is_usable = usable_ref[row * TOPK + j] > 0

        @pl.when(is_usable)
        def _(j=j):
            exps = jnp.exp2(scores[1 + j] - top)
            weight_ref[0, 1 + j] = exps.astype(jnp.bfloat16)
            inverse_ref[0] = inverse_ref[0] + jnp.sum(exps, axis=0, keepdims=True)

        @pl.when(jnp.logical_not(is_usable))
        def _(j=j):
            weight_ref[0, 1 + j] = jnp.zeros((BLK, BLK), jnp.bfloat16)

    inverse_ref[0] = 1.0 / inverse_ref[0]


def make_weights(tables, seq, rows_at, query_pieces, own_a, own_b, got_a, got_b, held=()):
    owner, rank, usable = tables
    rest = BLK - K_FIRST
    steps = rows_at.shape[0]

    def pick(j, rows):
        def index(i, owner, rank, usable, at, seq):
            return (owner[at[i] * TOPK + j], rank[at[i] * TOPK + j], 0, 0)

        return pl.BlockSpec((1, 1, rows, DH), index)

    in_specs = [
        pl.BlockSpec((1, K_FIRST, DH), lambda i, o, r, u, at, s: (at[i], 0, 0)),
        pl.BlockSpec((1, rest, DH), lambda i, o, r, u, at, s: (at[i], 0, 0)),
    ]
    args = [own_a, own_b]
    for j in range(TOPK):
        in_specs += [pick(j, K_FIRST), pick(j, rest)]
        args += [got_a.reshape(ROWS, CAP, K_FIRST, DH), got_b.reshape(ROWS, CAP, rest, DH)]
    args += [*query_pieces, *held]
    in_specs += [any_spec()] * (CHIPS + len(held))
    blocks = steps * (1 + TOPK)
    prefetched = (owner, rank, usable, rows_at, seq)
    first_held = len(prefetched) + len(args) - len(held)
    return pl.pallas_call(
        functools.partial(weights_kernel, len(held)),
        grid_spec=pltpu.PrefetchScalarGridSpec(
            num_scalar_prefetch=len(prefetched),
            grid=(steps,),
            in_specs=in_specs,
            out_specs=[
                pl.BlockSpec(
                    (1, 1 + TOPK, BLK, BLK), lambda i, o, r, u, at, s: (at[i], 0, 0, 0)
                ),
                pl.BlockSpec((1, 1, BLK), lambda i, o, r, u, at, s: (at[i], 0, 0)),
            ],
            scratch_shapes=[
                pltpu.VMEM((ROWS, DH, BLK), jnp.bfloat16),
                pltpu.VMEM((1 + TOPK, BLK, BLK), jnp.float32),
                pltpu.SemaphoreType.DMA((ROWS,)),
            ],
        ),
        out_shape=[
            jax.ShapeDtypeStruct((ROWS, 1 + TOPK, BLK, BLK), jnp.bfloat16),
            jax.ShapeDtypeStruct((ROWS, 1, BLK), jnp.float32),
        ],
        input_output_aliases={first_held + i: i for i in range(len(held))},
        compiler_params=params(),
        cost_estimate=cost(
            2 * blocks * BLK * BLK * DH, 2 * blocks * (BLK * BLK + BLK * DH), blocks * BLK * BLK
        ),
        name="make_weights",
    )(*prefetched, *args)


def outputs_kernel(owner_ref, rank_ref, inverse_ref, *rest):
    weight_refs, rest = rest[: 1 + TOPK], rest[1 + TOPK :]
    own_ref, picks, out_ref = rest[0], rest[1 : 1 + TOPK], rest[1 + TOPK]
    total = jnp.dot(own_ref[0], weight_refs[0][0, 0], preferred_element_type=jnp.float32)
    for j in range(TOPK):
        total += jnp.dot(
            picks[j][0, 0], weight_refs[1 + j][0, 0], preferred_element_type=jnp.float32
        )
    out_ref[0] = (total * inverse_ref[0]).astype(jnp.bfloat16)


def make_outputs(tables, weights, inverse, values, got, half):
    owner, rank, _ = tables

    def pick(j):
        def index(r, owner, rank):
            return (owner[r * TOPK + j], rank[r * TOPK + j], 0, 0)

        return pl.BlockSpec((1, 1, DH, BLK), index)

    blocks = ROWS * (1 + TOPK)
    return pl.pallas_call(
        outputs_kernel,
        grid_spec=pltpu.PrefetchScalarGridSpec(
            num_scalar_prefetch=2,
            grid=(ROWS,),
            in_specs=[pl.BlockSpec((1, 1, HALF), lambda r, *_: (r, 0, half))]
            + [
                pl.BlockSpec((1, 1, BLK, HALF), lambda r, *_, j=j: (r, j, 0, half))
                for j in range(1 + TOPK)
            ]
            + [pl.BlockSpec((1, DH, BLK), lambda r, *_: (r, 0, 0))]
            + [pick(j) for j in range(TOPK)],
            out_specs=pl.BlockSpec((1, DH, HALF), lambda r, *_: (r, 0, 0)),
        ),
        out_shape=jax.ShapeDtypeStruct((ROWS, DH, HALF), jnp.bfloat16),
        compiler_params=params(),
        cost_estimate=cost(2 * blocks * BLK * HALF * DH, 2 * blocks * BLK * (HALF + DH)),
        name="make_outputs",
    )(
        owner,
        rank,
        inverse,
        *([weights] * (1 + TOPK)),
        values,
        *([got.reshape(ROWS, CAP, DH, BLK)] * TOPK),
    )


def finish_kernel(head_ref, *rest):
    out_ref = rest[-1]
    for head in range(HEADS):
        out_ref[:, pl.ds(head * DH, DH)] = head_ref[head].T


def finish(heads, half, held=()):
    return pl.pallas_call(
        finish_kernel,
        grid=(1,),
        in_specs=[pl.BlockSpec((HEADS, DH, HALF), lambda i: (0, 0, 0))] + [any_spec()] * len(held),
        out_specs=pl.BlockSpec((HALF, HEADS * DH), lambda i: (half, 0)),
        out_shape=jax.ShapeDtypeStruct((BLK, HEADS * DH), jnp.bfloat16),
        input_output_aliases={1 + i: i for i in range(len(held))},
        compiler_params=params(),
        cost_estimate=cost(0, 4 * HALF * HEADS * DH),
        name="finish",
    )(heads, *held)


def permute_seq(array, place):
    seq_count, grp_count = lax.axis_size("seq"), lax.axis_size("grp")
    pairs = [
        (s * grp_count + g, place(s) % seq_count * grp_count + g)
        for s in range(seq_count)
        for g in range(grp_count)
    ]
    return lax.ppermute(array, AXES, pairs)


def swap_cores(array):
    return permute_seq(array, lambda s: s ^ 1)


def along_chips(pieces):
    moved = {0: pieces[0]}
    for chip in CHIP_ORDER:
        moved[chip] = permute_seq(pieces[chip], lambda s, chip=chip: s + 2 * chip)
    return [moved[chip] for chip in range(CHIPS)]


def exchange(array, axis):
    return lax.all_to_all(array, axis, split_axis=0, concat_axis=0, tiled=True)


def routes(pick_column, pick_back):
    seq, grp = lax.axis_index("seq"), lax.axis_index("grp")
    requests = ROWS * TOPK
    target = lax.dynamic_index_in_dim(pick_column, seq, 1, keepdims=False).reshape(-1, requests)
    back = lax.dynamic_index_in_dim(pick_back, seq, 1, keepdims=False).reshape(-1, requests)
    column = jnp.arange(target.shape[0], dtype=jnp.int32)[:, None]
    row = (jnp.arange(requests, dtype=jnp.int32) // TOPK)[None, :]
    local_row = row - back - (target >= column).astype(jnp.int32)
    at = jnp.arange(requests, dtype=jnp.int32)
    earlier = at[:, None] > at[None, :]
    hits = target == grp
    place = jnp.sum(hits[:, None, :] & earlier[None], axis=2, dtype=jnp.int32)
    chosen = hits[:, None, :] & (
        place[:, None, :] == jnp.arange(CAP, dtype=jnp.int32)[None, :, None]
    )
    send_block = jnp.sum(
        jnp.where(chosen, jnp.maximum(local_row, 0)[:, None, :], 0), axis=2, dtype=jnp.int32
    ).reshape(-1)
    owner = lax.dynamic_index_in_dim(target, grp, 0, keepdims=False)
    rank = jnp.sum((owner[:, None] == owner[None, :]) & earlier, axis=1, dtype=jnp.int32)
    usable = (lax.dynamic_index_in_dim(local_row, grp, 0, keepdims=False) >= 0).astype(jnp.int32)
    return send_block, (owner, rank, usable)


def body(query_rows, key_rows, value_rows, pick_column, pick_back):
    seq = lax.axis_index("seq").astype(jnp.int32).reshape(1)
    rest = BLK - K_FIRST
    key_first = split_first(key_rows)
    own_a = exchange(key_first, "seq")
    mine, other = by_core(split_rest_kernel, seq, key_rows, key_first, (rest, DH), "split_rest")
    key_pieces = pack(mine, swap_cores(other), "pack_keys")
    mine, other = by_core(turn_kernel, seq, value_rows, key_first, (DH, BLK), "turn_values")
    value_pieces = pack(mine, swap_cores(other), "pack_values")
    mine, other = by_core(turn_kernel, seq, query_rows, key_first, (DH, BLK), "turn_queries")
    query_pieces = pack(mine, swap_cores(other), "pack_queries")

    send_block, tables = routes(pick_column, pick_back)
    ready = [key_pieces[0], value_pieces[0]]
    (send_a,) = gather(seq, send_block, [own_a], (K_FIRST,), "gather_a", earlier=ready)
    got_a = exchange(send_a, "grp")

    key_pieces = along_chips(after(key_pieces, [send_a]))
    own_b, send_b = gather(
        seq, send_block, key_pieces, (rest,), "gather_b", earlier=[query_pieces[0]]
    )
    (send_b,) = after([send_b], [got_a])
    got_b = exchange(send_b, "grp")

    value_pieces = along_chips(after(value_pieces, [key_pieces[CHIP_ORDER[2]]]))
    values, send = gather(seq, send_block, value_pieces, (DH,), "gather_values")
    query_pieces = along_chips(after(query_pieces, [value_pieces[CHIP_ORDER[2]]]))
    (send,) = after([send], [got_b])
    got = exchange(send, "grp")
    straight = jnp.arange(ROWS, dtype=jnp.int32)
    weights, inverse = make_weights(
        tables, seq, straight, query_pieces, own_a, own_b, got_a, got_b
    )
    halves = [
        exchange(make_outputs(tables, weights, inverse, values, got, half), "seq")
        for half in range(2)
    ]
    out = finish(halves[0], 0)
    return finish(halves[1], 1, [out])


def solution(mesh):
    return jax.shard_map(
        body,
        mesh=mesh,
        in_specs=(P(AXES, None), P(AXES, None), P(AXES, None), P(), P()),
        out_specs=P(AXES, None),
        check_vma=False,
    )
```

```python
import functools

import jax
import jax.numpy as jnp
from jax import lax
from jax.experimental import pallas as pl
from jax.experimental.pallas import tpu as pltpu
from jax.sharding import PartitionSpec as P

HEADS = 16
DH = 128
BLK = 512
TOPK = 3
CAP = 4
ROWS = 16
CHIPS = ROWS // 2
K_FIRST = 224
V_PARTS = (96, 32)
CHIP_ORDER = (4, 3, 5, 2, 6, 1, 7)
EXP2_SCALE = DH ** (-0.5) * 1.4426950408889634
VMEM_BYTES = 56 * 1024 * 1024
AXES = ("seq", "grp")


def any_spec():
    return pl.BlockSpec(memory_space=pl.ANY)


def vmem_spec():
    return pl.BlockSpec(memory_space=pltpu.VMEM)


def smem_spec():
    return pl.BlockSpec(memory_space=pltpu.SMEM)


def params():
    return pltpu.CompilerParams(vmem_limit_bytes=VMEM_BYTES)


def cost(flops, moved, exps=0):
    return pl.CostEstimate(flops=flops, bytes_accessed=moved, transcendentals=exps)


def split_first_kernel(key_ref, first_ref):
    for head in range(HEADS):
        first_ref[head] = key_ref[:, pl.ds(head * DH, DH)]


def split_first(key_rows):
    return pl.pallas_call(
        split_first_kernel,
        grid=(1,),
        in_specs=[pl.BlockSpec((K_FIRST, HEADS * DH), lambda i: (0, 0))],
        out_specs=pl.BlockSpec((HEADS, K_FIRST, DH), lambda i: (0, 0, 0)),
        out_shape=jax.ShapeDtypeStruct((HEADS, K_FIRST, DH), jnp.bfloat16),
        compiler_params=params(),
        cost_estimate=cost(0, 4 * K_FIRST * HEADS * DH),
        name="split_first",
    )(key_rows)


def run_copies(copies):
    for copy in copies:
        copy.start()
    for copy in copies:
        copy.wait()


def same_core(seq, chip_shift):
    core = lax.rem(seq, 2)
    at = lax.rem(seq + 2 * chip_shift + ROWS, ROWS)
    return at, at + 1 - 2 * core


def put_heads(seq, held, mine_ref, other_ref, sem):
    copies = []
    for chip in range(CHIPS):
        mine, other = same_core(seq, chip)
        copies.append(pltpu.make_async_copy(held.at[mine], mine_ref.at[chip], sem.at[2 * chip]))
        copies.append(
            pltpu.make_async_copy(held.at[other], other_ref.at[chip], sem.at[2 * chip + 1])
        )
    run_copies(copies)


def split_rest_kernel(seq_ref, key_ref, earlier_ref, mine_ref, other_ref, held, sem):
    for head in range(HEADS):
        held[head] = key_ref[pl.ds(K_FIRST, BLK - K_FIRST), pl.ds(head * DH, DH)]
    put_heads(seq_ref[0], held, mine_ref, other_ref, sem)


def turn_kernel(seq_ref, row_ref, earlier_ref, mine_ref, other_ref, held, sem):
    for head in range(HEADS):
        held[head] = row_ref[:, pl.ds(head * DH, DH)].T
    put_heads(seq_ref[0], held, mine_ref, other_ref, sem)


def by_core(kernel, seq, array, earlier, shape, name):
    return pl.pallas_call(
        kernel,
        in_specs=[smem_spec(), vmem_spec(), any_spec()],
        out_specs=[any_spec()] * 2,
        out_shape=[jax.ShapeDtypeStruct((CHIPS,) + shape, jnp.bfloat16)] * 2,
        scratch_shapes=[
            pltpu.VMEM((ROWS,) + shape, jnp.bfloat16),
            pltpu.SemaphoreType.DMA((ROWS,)),
        ],
        compiler_params=params(),
        cost_estimate=cost(0, 4 * ROWS * shape[0] * shape[1]),
        name=name,
    )(seq, array, earlier)


def pack_kernel(mine_ref, other_ref, *rest):
    piece_refs, sem = rest[:CHIPS], rest[CHIPS]
    copies = []
    for chip in range(CHIPS):
        copies.append(
            pltpu.make_async_copy(mine_ref.at[chip], piece_refs[chip].at[0], sem.at[2 * chip])
        )
        copies.append(
            pltpu.make_async_copy(other_ref.at[chip], piece_refs[chip].at[1], sem.at[2 * chip + 1])
        )
    run_copies(copies)


def pack(mine, other, name):
    shape = mine.shape[1:]
    return pl.pallas_call(
        pack_kernel,
        in_specs=[vmem_spec()] * 2,
        out_specs=[any_spec()] * CHIPS,
        out_shape=[jax.ShapeDtypeStruct((2,) + shape, jnp.bfloat16)] * CHIPS,
        scratch_shapes=[pltpu.SemaphoreType.DMA((ROWS,))],
        compiler_params=params(),
        cost_estimate=cost(0, 8 * CHIPS * shape[0] * shape[1]),
        name=name,
    )(mine, other)


def to_rows(seq, piece_refs, held, sem, start=0, rows=None):
    copies = []
    for chip in range(CHIPS):
        for which, row in enumerate(same_core(seq, -chip)):
            place = held.at[row] if rows is None else held.at[row, pl.ds(start, rows)]
            copies.append(
                pltpu.make_async_copy(piece_refs[chip].at[which], place, sem.at[2 * chip + which])
            )
    return copies


def nothing_kernel(*refs):
    pass


def after(arrays, earlier):
    count = len(arrays)
    return pl.pallas_call(
        nothing_kernel,
        in_specs=[any_spec()] * (count + len(earlier)),
        out_specs=[any_spec()] * count,
        out_shape=[jax.ShapeDtypeStruct(a.shape, a.dtype) for a in arrays],
        input_output_aliases={i: i for i in range(count)},
        cost_estimate=cost(0, 0),
        name="after",
    )(*arrays, *earlier)


def gather_kernel(parts, pieces, extra, seq_ref, block_ref, *rest):
    in_refs, rest = rest[: max(pieces, 1)], rest[max(pieces, 1) + extra :]
    if pieces:
        all_ref, rest = rest[0], rest[1:]
    send_refs, rest = rest[: len(parts)], rest[len(parts) :]
    if pieces:
        held, in_sem, out_sem = rest
        run_copies(to_rows(seq_ref[0], in_refs, held, in_sem))
        whole = pltpu.make_async_copy(held, all_ref, in_sem.at[0])
        whole.start()
    else:
        held, out_sem, whole = in_refs[0], rest[0], None

    start = 0
    for part, (rows, send_ref) in enumerate(zip(parts, send_refs)):

        def send(slot, carry, start=start, rows=rows, send_ref=send_ref, part=part):
            pltpu.make_async_copy(
                held.at[block_ref[slot], pl.ds(start, rows)], send_ref.at[slot], out_sem.at[part]
            ).start()
            return carry

        lax.fori_loop(0, ROWS * CAP, send, 0)
        start += rows
    for part, send_ref in enumerate(send_refs):
        pltpu.make_async_copy(send_ref, send_ref, out_sem.at[part]).wait()
    if whole is not None:
        whole.wait()


def gather(seq, send_block, arrays, parts, name, earlier=()):
    pieces = len(arrays) if len(arrays) > 1 else 0
    rows, columns = arrays[0].shape[-2:]
    out_shape = [jax.ShapeDtypeStruct((ROWS * CAP, part, columns), jnp.bfloat16) for part in parts]
    scratch = [pltpu.SemaphoreType.DMA((len(parts),))]
    in_specs = [vmem_spec()]
    if pieces:
        out_shape = [jax.ShapeDtypeStruct((ROWS, rows, columns), jnp.bfloat16)] + out_shape
        scratch = [
            pltpu.VMEM((ROWS, rows, columns), jnp.bfloat16),
            pltpu.SemaphoreType.DMA((ROWS,)),
        ] + scratch
        in_specs = [any_spec()] * pieces
    return pl.pallas_call(
        functools.partial(gather_kernel, parts, pieces, len(earlier)),
        in_specs=[smem_spec(), smem_spec()] + in_specs + [any_spec()] * len(earlier),
        out_specs=[any_spec()] * len(out_shape),
        out_shape=out_shape,
        scratch_shapes=scratch,
        compiler_params=params(),
        cost_estimate=cost(0, 2 * ROWS * (CAP + 1) * sum(parts) * columns),
        name=name,
    )(seq, send_block, *arrays, *earlier)


def weights_kernel(held_count, owner_ref, rank_ref, usable_ref, row_ref, seq_ref, own_a, own_b, *rest):
    picks, rest = rest[: 2 * TOPK], rest[2 * TOPK :]
    pieces, rest = rest[:CHIPS], rest[CHIPS + held_count :]
    weight_ref, inverse_ref, queries, scores, sem = rest
    row = row_ref[pl.program_id(0)]

    @pl.when(pl.program_id(0) == 0)
    def _():
        run_copies(to_rows(seq_ref[0], pieces, queries, sem))

    query = queries[row]
    key_pairs = [(own_a[0], own_b[0])] + [
        (picks[2 * j][0, 0], picks[2 * j + 1][0, 0]) for j in range(TOPK)
    ]

    def raw(pair):
        upper = jnp.dot(pair[0], query, preferred_element_type=jnp.float32)
        lower = jnp.dot(pair[1], query, preferred_element_type=jnp.float32)
        return upper * EXP2_SCALE, lower * EXP2_SCALE

    key_at = lax.broadcasted_iota(jnp.int32, (BLK, BLK), 0)
    query_at = lax.broadcasted_iota(jnp.int32, (BLK, BLK), 1)
    upper, lower = raw(key_pairs[0])
    own = jnp.where(query_at >= key_at, jnp.concatenate([upper, lower], axis=0), -jnp.inf)
    scores[0] = own
    top = jnp.max(own, axis=0, keepdims=True)
    inverse_ref[0] = top

    for j in range(TOPK):

        @pl.when(usable_ref[row * TOPK + j] > 0)
        def _(j=j):
            upper, lower = raw(key_pairs[1 + j])
            scores[1 + j, pl.ds(0, K_FIRST), :] = upper
            scores[1 + j, pl.ds(K_FIRST, BLK - K_FIRST), :] = lower
            inverse_ref[0] = jnp.maximum(
                inverse_ref[0],
                jnp.maximum(
                    jnp.max(upper, axis=0, keepdims=True), jnp.max(lower, axis=0, keepdims=True)
                ),
            )

    top = inverse_ref[0]
    exps = jnp.exp2(scores[0] - top)
    weight_ref[0, 0] = exps.astype(jnp.bfloat16)
    inverse_ref[0] = jnp.sum(exps, axis=0, keepdims=True)
    for j in range(TOPK):
        is_usable = usable_ref[row * TOPK + j] > 0

        @pl.when(is_usable)
        def _(j=j):
            exps = jnp.exp2(scores[1 + j] - top)
            weight_ref[0, 1 + j] = exps.astype(jnp.bfloat16)
            inverse_ref[0] = inverse_ref[0] + jnp.sum(exps, axis=0, keepdims=True)

        @pl.when(jnp.logical_not(is_usable))
        def _(j=j):
            weight_ref[0, 1 + j] = jnp.zeros((BLK, BLK), jnp.bfloat16)

    inverse_ref[0] = 1.0 / inverse_ref[0]


def make_weights(tables, seq, rows_at, query_pieces, own_a, own_b, got_a, got_b, held=()):
    owner, rank, usable = tables
    rest = BLK - K_FIRST
    steps = rows_at.shape[0]

    def pick(j, rows):
        def index(i, owner, rank, usable, at, seq):
            return (owner[at[i] * TOPK + j], rank[at[i] * TOPK + j], 0, 0)

        return pl.BlockSpec((1, 1, rows, DH), index)

    in_specs = [
        pl.BlockSpec((1, K_FIRST, DH), lambda i, o, r, u, at, s: (at[i], 0, 0)),
        pl.BlockSpec((1, rest, DH), lambda i, o, r, u, at, s: (at[i], 0, 0)),
    ]
    args = [own_a, own_b]
    for j in range(TOPK):
        in_specs += [pick(j, K_FIRST), pick(j, rest)]
        args += [got_a.reshape(ROWS, CAP, K_FIRST, DH), got_b.reshape(ROWS, CAP, rest, DH)]
    args += [*query_pieces, *held]
    in_specs += [any_spec()] * (CHIPS + len(held))
    blocks = steps * (1 + TOPK)
    prefetched = (owner, rank, usable, rows_at, seq)
    first_held = len(prefetched) + len(args) - len(held)
    return pl.pallas_call(
        functools.partial(weights_kernel, len(held)),
        grid_spec=pltpu.PrefetchScalarGridSpec(
            num_scalar_prefetch=len(prefetched),
            grid=(steps,),
            in_specs=in_specs,
            out_specs=[
                pl.BlockSpec(
                    (1, 1 + TOPK, BLK, BLK), lambda i, o, r, u, at, s: (at[i], 0, 0, 0)
                ),
                pl.BlockSpec((1, 1, BLK), lambda i, o, r, u, at, s: (at[i], 0, 0)),
            ],
            scratch_shapes=[
                pltpu.VMEM((ROWS, DH, BLK), jnp.bfloat16),
                pltpu.VMEM((1 + TOPK, BLK, BLK), jnp.float32),
                pltpu.SemaphoreType.DMA((ROWS,)),
            ],
        ),
        out_shape=[
            jax.ShapeDtypeStruct((ROWS, 1 + TOPK, BLK, BLK), jnp.bfloat16),
            jax.ShapeDtypeStruct((ROWS, 1, BLK), jnp.float32),
        ],
        input_output_aliases={first_held + i: i for i in range(len(held))},
        compiler_params=params(),
        cost_estimate=cost(
            2 * blocks * BLK * BLK * DH, 2 * blocks * (BLK * BLK + BLK * DH), blocks * BLK * BLK
        ),
        name="make_weights",
    )(*prefetched, *args)


def outputs_kernel(start, rows, owner_ref, rank_ref, inverse_ref, *rest):
    weight_refs, rest = rest[: 1 + TOPK], rest[1 + TOPK :]
    own_ref, picks, out_ref = rest[0], rest[1 : 1 + TOPK], rest[1 + TOPK]
    total = jnp.dot(
        own_ref[0, pl.ds(start, rows), :], weight_refs[0][0, 0], preferred_element_type=jnp.float32
    )
    for j in range(TOPK):
        total += jnp.dot(
            picks[j][0, 0], weight_refs[1 + j][0, 0], preferred_element_type=jnp.float32
        )
    out_ref[0] = (total * inverse_ref[0]).astype(jnp.bfloat16)


def make_outputs(tables, weights, inverse, values, got, start, rows):
    owner, rank, _ = tables

    def pick(j):
        def index(r, owner, rank):
            return (owner[r * TOPK + j], rank[r * TOPK + j], 0, 0)

        return pl.BlockSpec((1, 1, rows, BLK), index)

    blocks = ROWS * (1 + TOPK)
    return pl.pallas_call(
        functools.partial(outputs_kernel, start, rows),
        grid_spec=pltpu.PrefetchScalarGridSpec(
            num_scalar_prefetch=2,
            grid=(ROWS,),
            in_specs=[pl.BlockSpec((1, 1, BLK), lambda r, *_: (r, 0, 0))]
            + [
                pl.BlockSpec((1, 1, BLK, BLK), lambda r, *_, j=j: (r, j, 0, 0))
                for j in range(1 + TOPK)
            ]
            + [pl.BlockSpec((1, DH, BLK), lambda r, *_: (r, 0, 0))]
            + [pick(j) for j in range(TOPK)],
            out_specs=pl.BlockSpec((1, rows, BLK), lambda r, *_: (r, 0, 0)),
        ),
        out_shape=jax.ShapeDtypeStruct((ROWS, rows, BLK), jnp.bfloat16),
        compiler_params=params(),
        cost_estimate=cost(2 * blocks * BLK * BLK * DH, 2 * blocks * BLK * (BLK + rows)),
        name="make_outputs",
    )(
        owner,
        rank,
        inverse,
        *([weights] * (1 + TOPK)),
        values,
        *([got.reshape(ROWS, CAP, rows, BLK)] * TOPK),
    )


def finish_kernel(first_ref, last_ref, out_ref):
    for head in range(HEADS):
        whole = jnp.concatenate([first_ref[head], last_ref[head]], axis=0)
        out_ref[:, pl.ds(head * DH, DH)] = whole.T


def finish(first, last):
    return pl.pallas_call(
        finish_kernel,
        in_specs=[vmem_spec()] * 2,
        out_specs=vmem_spec(),
        out_shape=jax.ShapeDtypeStruct((BLK, HEADS * DH), jnp.bfloat16),
        compiler_params=params(),
        cost_estimate=cost(0, 4 * BLK * HEADS * DH),
        name="finish",
    )(first, last)


def permute_seq(array, place):
    seq_count, grp_count = lax.axis_size("seq"), lax.axis_size("grp")
    pairs = [
        (s * grp_count + g, place(s) % seq_count * grp_count + g)
        for s in range(seq_count)
        for g in range(grp_count)
    ]
    return lax.ppermute(array, AXES, pairs)


def swap_cores(array):
    return permute_seq(array, lambda s: s ^ 1)


def along_chips(pieces):
    moved = {0: pieces[0]}
    for chip in CHIP_ORDER:
        moved[chip] = permute_seq(pieces[chip], lambda s, chip=chip: s + 2 * chip)
    return [moved[chip] for chip in range(CHIPS)]


def exchange(array, axis):
    return lax.all_to_all(array, axis, split_axis=0, concat_axis=0, tiled=True)


def routes(pick_column, pick_back):
    seq, grp = lax.axis_index("seq"), lax.axis_index("grp")
    requests = ROWS * TOPK
    target = lax.dynamic_index_in_dim(pick_column, seq, 1, keepdims=False).reshape(-1, requests)
    back = lax.dynamic_index_in_dim(pick_back, seq, 1, keepdims=False).reshape(-1, requests)
    column = jnp.arange(target.shape[0], dtype=jnp.int32)[:, None]
    row = (jnp.arange(requests, dtype=jnp.int32) // TOPK)[None, :]
    local_row = row - back - (target >= column).astype(jnp.int32)
    at = jnp.arange(requests, dtype=jnp.int32)
    earlier = at[:, None] > at[None, :]
    hits = target == grp
    place = jnp.sum(hits[:, None, :] & earlier[None], axis=2, dtype=jnp.int32)
    chosen = hits[:, None, :] & (
        place[:, None, :] == jnp.arange(CAP, dtype=jnp.int32)[None, :, None]
    )
    send_block = jnp.sum(
        jnp.where(chosen, jnp.maximum(local_row, 0)[:, None, :], 0), axis=2, dtype=jnp.int32
    ).reshape(-1)
    owner = lax.dynamic_index_in_dim(target, grp, 0, keepdims=False)
    rank = jnp.sum((owner[:, None] == owner[None, :]) & earlier, axis=1, dtype=jnp.int32)
    usable = (lax.dynamic_index_in_dim(local_row, grp, 0, keepdims=False) >= 0).astype(jnp.int32)
    return send_block, (owner, rank, usable)


def body(query_rows, key_rows, value_rows, pick_column, pick_back):
    seq = lax.axis_index("seq").astype(jnp.int32).reshape(1)
    rest = BLK - K_FIRST
    key_first = split_first(key_rows)
    own_a = exchange(key_first, "seq")
    mine, other = by_core(split_rest_kernel, seq, key_rows, key_first, (rest, DH), "split_rest")
    key_pieces = pack(mine, swap_cores(other), "pack_keys")
    mine, other = by_core(turn_kernel, seq, value_rows, key_first, (DH, BLK), "turn_values")
    value_pieces = pack(mine, swap_cores(other), "pack_values")
    mine, other = by_core(turn_kernel, seq, query_rows, key_first, (DH, BLK), "turn_queries")
    query_pieces = pack(mine, swap_cores(other), "pack_queries")

    send_block, tables = routes(pick_column, pick_back)
    ready = [key_pieces[0], value_pieces[0]]
    (send_a,) = gather(seq, send_block, [own_a], (K_FIRST,), "gather_a", earlier=ready)
    got_a = exchange(send_a, "grp")

    key_pieces = along_chips(after(key_pieces, [send_a]))
    own_b, send_b = gather(
        seq, send_block, key_pieces, (rest,), "gather_b", earlier=[query_pieces[0]]
    )
    (send_b,) = after([send_b], [got_a])
    got_b = exchange(send_b, "grp")

    value_pieces = along_chips(after(value_pieces, [key_pieces[CHIP_ORDER[2]]]))
    values, *sends = gather(seq, send_block, value_pieces, V_PARTS, "gather_values")
    query_pieces = along_chips(after(query_pieces, [value_pieces[CHIP_ORDER[2]]]))
    straight = jnp.arange(ROWS, dtype=jnp.int32)
    weights, inverse = make_weights(
        tables, seq, straight, query_pieces, own_a, own_b, got_a, got_b
    )
    (send,) = after(sends[:1], [got_b])
    got_first = exchange(send, "grp")
    first = make_outputs(tables, weights, inverse, values, got_first, 0, V_PARTS[0])
    (send,) = after(sends[1:], [got_first, inverse])
    got_last = exchange(send, "grp")
    last = make_outputs(tables, weights, inverse, values, got_last, *V_PARTS)

    (first,) = after([first], [got_last])
    first = exchange(first, "seq")
    (last,) = after([last], [first])
    return finish(first, exchange(last, "seq"))


def solution(mesh):
    return jax.shard_map(
        body,
        mesh=mesh,
        in_specs=(P(AXES, None), P(AXES, None), P(AXES, None), P(), P()),
        out_specs=P(AXES, None),
        check_vma=False,
    )
```

```python
import functools

import jax
import jax.numpy as jnp
from jax import lax
from jax.experimental import pallas as pl
from jax.experimental.pallas import tpu as pltpu
from jax.sharding import PartitionSpec as P

HEADS = 16
DH = 128
BLK = 512
TOPK = 3
CAP = 4
ROWS = 16
CHIPS = ROWS // 2
K_FIRST = 224
V_PARTS = (96, 32)
CHIP_ORDER = (4, 3, 5, 2, 6, 1, 7)
EXP2_SCALE = DH ** (-0.5) * 1.4426950408889634
VMEM_BYTES = 56 * 1024 * 1024
AXES = ("seq", "grp")


def any_spec():
    return pl.BlockSpec(memory_space=pl.ANY)


def vmem_spec():
    return pl.BlockSpec(memory_space=pltpu.VMEM)


def smem_spec():
    return pl.BlockSpec(memory_space=pltpu.SMEM)


def params():
    return pltpu.CompilerParams(vmem_limit_bytes=VMEM_BYTES)


def cost(flops, moved, exps=0):
    return pl.CostEstimate(flops=flops, bytes_accessed=moved, transcendentals=exps)


def split_first_kernel(key_ref, first_ref):
    for head in range(HEADS):
        first_ref[head] = key_ref[:, pl.ds(head * DH, DH)]


def split_first(key_rows):
    return pl.pallas_call(
        split_first_kernel,
        grid=(1,),
        in_specs=[pl.BlockSpec((K_FIRST, HEADS * DH), lambda i: (0, 0))],
        out_specs=pl.BlockSpec((HEADS, K_FIRST, DH), lambda i: (0, 0, 0)),
        out_shape=jax.ShapeDtypeStruct((HEADS, K_FIRST, DH), jnp.bfloat16),
        compiler_params=params(),
        cost_estimate=cost(0, 4 * K_FIRST * HEADS * DH),
        name="split_first",
    )(key_rows)


def run_copies(copies):
    for copy in copies:
        copy.start()
    for copy in copies:
        copy.wait()


def same_core(seq, chip_shift):
    core = lax.rem(seq, 2)
    at = lax.rem(seq + 2 * chip_shift + ROWS, ROWS)
    return at, at + 1 - 2 * core


def put_heads(seq, held, mine_ref, other_ref, sem):
    copies = []
    for chip in range(CHIPS):
        mine, other = same_core(seq, chip)
        copies.append(pltpu.make_async_copy(held.at[mine], mine_ref.at[chip], sem.at[2 * chip]))
        copies.append(
            pltpu.make_async_copy(held.at[other], other_ref.at[chip], sem.at[2 * chip + 1])
        )
    run_copies(copies)


def split_rest_kernel(seq_ref, key_ref, earlier_ref, mine_ref, other_ref, held, sem):
    for head in range(HEADS):
        held[head] = key_ref[pl.ds(K_FIRST, BLK - K_FIRST), pl.ds(head * DH, DH)]
    put_heads(seq_ref[0], held, mine_ref, other_ref, sem)


def turn_kernel(seq_ref, row_ref, earlier_ref, mine_ref, other_ref, held, sem):
    for head in range(HEADS):
        held[head] = row_ref[:, pl.ds(head * DH, DH)].T
    put_heads(seq_ref[0], held, mine_ref, other_ref, sem)


def by_core(kernel, seq, array, earlier, shape, name):
    return pl.pallas_call(
        kernel,
        in_specs=[smem_spec(), vmem_spec(), any_spec()],
        out_specs=[any_spec()] * 2,
        out_shape=[jax.ShapeDtypeStruct((CHIPS,) + shape, jnp.bfloat16)] * 2,
        scratch_shapes=[
            pltpu.VMEM((ROWS,) + shape, jnp.bfloat16),
            pltpu.SemaphoreType.DMA((ROWS,)),
        ],
        compiler_params=params(),
        cost_estimate=cost(0, 4 * ROWS * shape[0] * shape[1]),
        name=name,
    )(seq, array, earlier)


def pack_kernel(mine_ref, other_ref, *rest):
    piece_refs, sem = rest[:CHIPS], rest[CHIPS]
    copies = []
    for chip in range(CHIPS):
        copies.append(
            pltpu.make_async_copy(mine_ref.at[chip], piece_refs[chip].at[0], sem.at[2 * chip])
        )
        copies.append(
            pltpu.make_async_copy(other_ref.at[chip], piece_refs[chip].at[1], sem.at[2 * chip + 1])
        )
    run_copies(copies)


def pack(mine, other, name):
    shape = mine.shape[1:]
    return pl.pallas_call(
        pack_kernel,
        in_specs=[vmem_spec()] * 2,
        out_specs=[any_spec()] * CHIPS,
        out_shape=[jax.ShapeDtypeStruct((2,) + shape, jnp.bfloat16)] * CHIPS,
        scratch_shapes=[pltpu.SemaphoreType.DMA((ROWS,))],
        compiler_params=params(),
        cost_estimate=cost(0, 8 * CHIPS * shape[0] * shape[1]),
        name=name,
    )(mine, other)


def to_rows(seq, piece_refs, held, sem, start=0, rows=None):
    copies = []
    for chip in range(CHIPS):
        for which, row in enumerate(same_core(seq, -chip)):
            place = held.at[row] if rows is None else held.at[row, pl.ds(start, rows)]
            copies.append(
                pltpu.make_async_copy(piece_refs[chip].at[which], place, sem.at[2 * chip + which])
            )
    return copies


def nothing_kernel(*refs):
    pass


def after(arrays, earlier):
    count = len(arrays)
    return pl.pallas_call(
        nothing_kernel,
        in_specs=[any_spec()] * (count + len(earlier)),
        out_specs=[any_spec()] * count,
        out_shape=[jax.ShapeDtypeStruct(a.shape, a.dtype) for a in arrays],
        input_output_aliases={i: i for i in range(count)},
        cost_estimate=cost(0, 0),
        name="after",
    )(*arrays, *earlier)


def gather_kernel(parts, pieces, extra, seq_ref, block_ref, *rest):
    in_refs, rest = rest[: max(pieces, 1)], rest[max(pieces, 1) + extra :]
    if pieces:
        all_ref, rest = rest[0], rest[1:]
    send_refs, rest = rest[: len(parts)], rest[len(parts) :]
    if pieces:
        held, in_sem, out_sem = rest
        run_copies(to_rows(seq_ref[0], in_refs, held, in_sem))
        whole = pltpu.make_async_copy(held, all_ref, in_sem.at[0])
        whole.start()
    else:
        held, out_sem, whole = in_refs[0], rest[0], None

    start = 0
    for part, (rows, send_ref) in enumerate(zip(parts, send_refs)):

        def send(slot, carry, start=start, rows=rows, send_ref=send_ref, part=part):
            pltpu.make_async_copy(
                held.at[block_ref[slot], pl.ds(start, rows)], send_ref.at[slot], out_sem.at[part]
            ).start()
            return carry

        lax.fori_loop(0, ROWS * CAP, send, 0)
        start += rows
    for part, send_ref in enumerate(send_refs):
        pltpu.make_async_copy(send_ref, send_ref, out_sem.at[part]).wait()
    if whole is not None:
        whole.wait()


def gather(seq, send_block, arrays, parts, name, earlier=()):
    pieces = len(arrays) if len(arrays) > 1 else 0
    rows, columns = arrays[0].shape[-2:]
    out_shape = [jax.ShapeDtypeStruct((ROWS * CAP, part, columns), jnp.bfloat16) for part in parts]
    scratch = [pltpu.SemaphoreType.DMA((len(parts),))]
    in_specs = [vmem_spec()]
    if pieces:
        out_shape = [jax.ShapeDtypeStruct((ROWS, rows, columns), jnp.bfloat16)] + out_shape
        scratch = [
            pltpu.VMEM((ROWS, rows, columns), jnp.bfloat16),
            pltpu.SemaphoreType.DMA((ROWS,)),
        ] + scratch
        in_specs = [any_spec()] * pieces
    return pl.pallas_call(
        functools.partial(gather_kernel, parts, pieces, len(earlier)),
        in_specs=[smem_spec(), smem_spec()] + in_specs + [any_spec()] * len(earlier),
        out_specs=[any_spec()] * len(out_shape),
        out_shape=out_shape,
        scratch_shapes=scratch,
        compiler_params=params(),
        cost_estimate=cost(0, 2 * ROWS * (CAP + 1) * sum(parts) * columns),
        name=name,
    )(seq, send_block, *arrays, *earlier)


def weights_kernel(held_count, owner_ref, rank_ref, usable_ref, row_ref, seq_ref, own_a, own_b, *rest):
    picks, rest = rest[: 2 * TOPK], rest[2 * TOPK :]
    pieces, rest = rest[:CHIPS], rest[CHIPS + held_count :]
    weight_ref, inverse_ref, queries, scores, sem = rest
    row = row_ref[pl.program_id(0)]

    @pl.when(pl.program_id(0) == 0)
    def _():
        run_copies(to_rows(seq_ref[0], pieces, queries, sem))

    query = queries[row]
    key_pairs = [(own_a[0], own_b[0])] + [
        (picks[2 * j][0, 0], picks[2 * j + 1][0, 0]) for j in range(TOPK)
    ]

    def raw(pair):
        upper = jnp.dot(pair[0], query, preferred_element_type=jnp.float32)
        lower = jnp.dot(pair[1], query, preferred_element_type=jnp.float32)
        return upper * EXP2_SCALE, lower * EXP2_SCALE

    key_at = lax.broadcasted_iota(jnp.int32, (BLK, BLK), 0)
    query_at = lax.broadcasted_iota(jnp.int32, (BLK, BLK), 1)
    upper, lower = raw(key_pairs[0])
    own = jnp.where(query_at >= key_at, jnp.concatenate([upper, lower], axis=0), -jnp.inf)
    scores[0] = own
    top = jnp.max(own, axis=0, keepdims=True)
    inverse_ref[0] = top

    for j in range(TOPK):

        @pl.when(usable_ref[row * TOPK + j] > 0)
        def _(j=j):
            upper, lower = raw(key_pairs[1 + j])
            scores[1 + j, pl.ds(0, K_FIRST), :] = upper
            scores[1 + j, pl.ds(K_FIRST, BLK - K_FIRST), :] = lower
            inverse_ref[0] = jnp.maximum(
                inverse_ref[0],
                jnp.maximum(
                    jnp.max(upper, axis=0, keepdims=True), jnp.max(lower, axis=0, keepdims=True)
                ),
            )

    top = inverse_ref[0]
    exps = jnp.exp2(scores[0] - top)
    weight_ref[0, 0] = exps.astype(jnp.bfloat16)
    inverse_ref[0] = jnp.sum(exps, axis=0, keepdims=True)
    for j in range(TOPK):
        is_usable = usable_ref[row * TOPK + j] > 0

        @pl.when(is_usable)
        def _(j=j):
            exps = jnp.exp2(scores[1 + j] - top)
            weight_ref[0, 1 + j] = exps.astype(jnp.bfloat16)
            inverse_ref[0] = inverse_ref[0] + jnp.sum(exps, axis=0, keepdims=True)

        @pl.when(jnp.logical_not(is_usable))
        def _(j=j):
            weight_ref[0, 1 + j] = jnp.zeros((BLK, BLK), jnp.bfloat16)

    inverse_ref[0] = 1.0 / inverse_ref[0]


def make_weights(tables, seq, rows_at, query_pieces, own_a, own_b, got_a, got_b, held=()):
    owner, rank, usable = tables
    rest = BLK - K_FIRST
    steps = rows_at.shape[0]

    def pick(j, rows):
        def index(i, owner, rank, usable, at, seq):
            return (owner[at[i] * TOPK + j], rank[at[i] * TOPK + j], 0, 0)

        return pl.BlockSpec((1, 1, rows, DH), index)

    in_specs = [
        pl.BlockSpec((1, K_FIRST, DH), lambda i, o, r, u, at, s: (at[i], 0, 0)),
        pl.BlockSpec((1, rest, DH), lambda i, o, r, u, at, s: (at[i], 0, 0)),
    ]
    args = [own_a, own_b]
    for j in range(TOPK):
        in_specs += [pick(j, K_FIRST), pick(j, rest)]
        args += [got_a.reshape(ROWS, CAP, K_FIRST, DH), got_b.reshape(ROWS, CAP, rest, DH)]
    args += [*query_pieces, *held]
    in_specs += [any_spec()] * (CHIPS + len(held))
    blocks = steps * (1 + TOPK)
    prefetched = (owner, rank, usable, rows_at, seq)
    first_held = len(prefetched) + len(args) - len(held)
    return pl.pallas_call(
        functools.partial(weights_kernel, len(held)),
        grid_spec=pltpu.PrefetchScalarGridSpec(
            num_scalar_prefetch=len(prefetched),
            grid=(steps,),
            in_specs=in_specs,
            out_specs=[
                pl.BlockSpec(
                    (1, 1 + TOPK, BLK, BLK), lambda i, o, r, u, at, s: (at[i], 0, 0, 0)
                ),
                pl.BlockSpec((1, 1, BLK), lambda i, o, r, u, at, s: (at[i], 0, 0)),
            ],
            scratch_shapes=[
                pltpu.VMEM((ROWS, DH, BLK), jnp.bfloat16),
                pltpu.VMEM((1 + TOPK, BLK, BLK), jnp.float32),
                pltpu.SemaphoreType.DMA((ROWS,)),
            ],
        ),
        out_shape=[
            jax.ShapeDtypeStruct((ROWS, 1 + TOPK, BLK, BLK), jnp.bfloat16),
            jax.ShapeDtypeStruct((ROWS, 1, BLK), jnp.float32),
        ],
        input_output_aliases={first_held + i: i for i in range(len(held))},
        compiler_params=params(),
        cost_estimate=cost(
            2 * blocks * BLK * BLK * DH, 2 * blocks * (BLK * BLK + BLK * DH), blocks * BLK * BLK
        ),
        name="make_weights",
    )(*prefetched, *args)


def outputs_kernel(start, rows, owner_ref, rank_ref, row_ref, inverse_ref, *rest):
    weight_refs, rest = rest[: 1 + TOPK], rest[1 + TOPK :]
    own_ref, picks, out_ref = rest[0], rest[1 : 1 + TOPK], rest[1 + TOPK]
    total = jnp.dot(
        own_ref[0, pl.ds(start, rows), :], weight_refs[0][0, 0], preferred_element_type=jnp.float32
    )
    for j in range(TOPK):
        total += jnp.dot(
            picks[j][0, 0], weight_refs[1 + j][0, 0], preferred_element_type=jnp.float32
        )
    out_ref[0] = (total * inverse_ref[0]).astype(jnp.bfloat16)


def make_outputs(tables, rows_at, weights, inverse, values, got, start, rows):
    owner, rank, _ = tables
    steps = rows_at.shape[0]

    def pick(j):
        def index(i, owner, rank, at):
            place = at[i] * TOPK + j
            return (owner[place], rank[place], 0, 0)

        return pl.BlockSpec((1, 1, rows, BLK), index)

    blocks = steps * (1 + TOPK)
    return pl.pallas_call(
        functools.partial(outputs_kernel, start, rows),
        grid_spec=pltpu.PrefetchScalarGridSpec(
            num_scalar_prefetch=3,
            grid=(steps,),
            in_specs=[pl.BlockSpec((1, 1, BLK), lambda i, o, r, at: (at[i], 0, 0))]
            + [
                pl.BlockSpec((1, 1, BLK, BLK), lambda i, o, r, at, j=j: (at[i], j, 0, 0))
                for j in range(1 + TOPK)
            ]
            + [pl.BlockSpec((1, DH, BLK), lambda i, o, r, at: (at[i], 0, 0))]
            + [pick(j) for j in range(TOPK)],
            out_specs=pl.BlockSpec((1, rows, BLK), lambda i, *_: (i, 0, 0)),
        ),
        out_shape=jax.ShapeDtypeStruct((steps, rows, BLK), jnp.bfloat16),
        compiler_params=params(),
        cost_estimate=cost(2 * blocks * BLK * BLK * DH, 2 * blocks * BLK * (BLK + rows)),
        name="make_outputs",
    )(
        owner,
        rank,
        rows_at,
        inverse,
        *([weights] * (1 + TOPK)),
        values,
        *([got.reshape(ROWS, CAP, rows, BLK)] * TOPK),
    )


def finish_kernel(seq_ref, first_ref, *rest):
    pieces, (out_ref, last, sem) = rest[:CHIPS], rest[CHIPS:]
    run_copies(to_rows(seq_ref[0], pieces, last, sem))
    for head in range(HEADS):
        whole = jnp.concatenate([first_ref[head], last[head]], axis=0)
        out_ref[:, pl.ds(head * DH, DH)] = whole.T


def finish(seq, first, pieces):
    return pl.pallas_call(
        finish_kernel,
        in_specs=[smem_spec(), vmem_spec()] + [any_spec()] * CHIPS,
        out_specs=vmem_spec(),
        out_shape=jax.ShapeDtypeStruct((BLK, HEADS * DH), jnp.bfloat16),
        scratch_shapes=[
            pltpu.VMEM((ROWS, V_PARTS[1], BLK), jnp.bfloat16),
            pltpu.SemaphoreType.DMA((ROWS,)),
        ],
        compiler_params=params(),
        cost_estimate=cost(0, 4 * BLK * HEADS * DH),
        name="finish",
    )(seq, first, *pieces)


def permute_seq(array, place):
    seq_count, grp_count = lax.axis_size("seq"), lax.axis_size("grp")
    pairs = [
        (s * grp_count + g, place(s) % seq_count * grp_count + g)
        for s in range(seq_count)
        for g in range(grp_count)
    ]
    return lax.ppermute(array, AXES, pairs)


def swap_cores(array):
    return permute_seq(array, lambda s: s ^ 1)


def along_chips(pieces):
    moved = {0: pieces[0]}
    for chip in CHIP_ORDER:
        moved[chip] = permute_seq(pieces[chip], lambda s, chip=chip: s + 2 * chip)
    return [moved[chip] for chip in range(CHIPS)]


def exchange(array, axis):
    return lax.all_to_all(array, axis, split_axis=0, concat_axis=0, tiled=True)


def routes(pick_column, pick_back):
    seq, grp = lax.axis_index("seq"), lax.axis_index("grp")
    requests = ROWS * TOPK
    target = lax.dynamic_index_in_dim(pick_column, seq, 1, keepdims=False).reshape(-1, requests)
    back = lax.dynamic_index_in_dim(pick_back, seq, 1, keepdims=False).reshape(-1, requests)
    column = jnp.arange(target.shape[0], dtype=jnp.int32)[:, None]
    row = (jnp.arange(requests, dtype=jnp.int32) // TOPK)[None, :]
    local_row = row - back - (target >= column).astype(jnp.int32)
    at = jnp.arange(requests, dtype=jnp.int32)
    earlier = at[:, None] > at[None, :]
    hits = target == grp
    place = jnp.sum(hits[:, None, :] & earlier[None], axis=2, dtype=jnp.int32)
    chosen = hits[:, None, :] & (
        place[:, None, :] == jnp.arange(CAP, dtype=jnp.int32)[None, :, None]
    )
    send_block = jnp.sum(
        jnp.where(chosen, jnp.maximum(local_row, 0)[:, None, :], 0), axis=2, dtype=jnp.int32
    ).reshape(-1)
    owner = lax.dynamic_index_in_dim(target, grp, 0, keepdims=False)
    rank = jnp.sum((owner[:, None] == owner[None, :]) & earlier, axis=1, dtype=jnp.int32)
    usable = (lax.dynamic_index_in_dim(local_row, grp, 0, keepdims=False) >= 0).astype(jnp.int32)
    return send_block, (owner, rank, usable)


def body(query_rows, key_rows, value_rows, pick_column, pick_back):
    seq = lax.axis_index("seq").astype(jnp.int32).reshape(1)
    rest = BLK - K_FIRST
    key_first = split_first(key_rows)
    own_a = exchange(key_first, "seq")
    mine, other = by_core(split_rest_kernel, seq, key_rows, key_first, (rest, DH), "split_rest")
    key_pieces = pack(mine, swap_cores(other), "pack_keys")
    mine, other = by_core(turn_kernel, seq, value_rows, key_first, (DH, BLK), "turn_values")
    value_pieces = pack(mine, swap_cores(other), "pack_values")
    mine, other = by_core(turn_kernel, seq, query_rows, key_first, (DH, BLK), "turn_queries")
    query_pieces = pack(mine, swap_cores(other), "pack_queries")

    send_block, tables = routes(pick_column, pick_back)
    ready = [key_pieces[0], value_pieces[0]]
    (send_a,) = gather(seq, send_block, [own_a], (K_FIRST,), "gather_a", earlier=ready)
    got_a = exchange(send_a, "grp")

    key_pieces = along_chips(after(key_pieces, [send_a]))
    own_b, send_b = gather(
        seq, send_block, key_pieces, (rest,), "gather_b", earlier=[query_pieces[0]]
    )
    (send_b,) = after([send_b], [got_a])
    got_b = exchange(send_b, "grp")

    value_pieces = along_chips(after(value_pieces, [key_pieces[CHIP_ORDER[2]]]))
    values, *sends = gather(seq, send_block, value_pieces, V_PARTS, "gather_values")
    query_pieces = along_chips(after(query_pieces, [value_pieces[CHIP_ORDER[2]]]))
    straight = jnp.arange(ROWS, dtype=jnp.int32)
    weights, inverse = make_weights(
        tables, seq, straight, query_pieces, own_a, own_b, got_a, got_b
    )
    ready = [got_b] + [query_pieces[chip] for chip in CHIP_ORDER[:2]]
    (send,) = after(sends[:1], ready)
    got_first = exchange(send, "grp")
    inputs = (weights, inverse, values)
    first = make_outputs(tables, straight, *inputs, got_first, 0, V_PARTS[0])
    (send,) = after(sends[1:], [got_first, inverse])
    got_last = exchange(send, "grp")
    (first,) = after([first], [got_last])
    first = exchange(first, "seq")

    same = (seq + 2 * jnp.arange(CHIPS, dtype=jnp.int32)) % ROWS
    other = swap_cores(make_outputs(tables, same ^ 1, *inputs, got_last, *V_PARTS))
    mine = make_outputs(tables, same, *inputs, got_last, *V_PARTS)
    return finish(seq, first, along_chips(pack(mine, other, "pack_outputs")))


def solution(mesh):
    return jax.shard_map(
        body,
        mesh=mesh,
        in_specs=(P(AXES, None), P(AXES, None), P(AXES, None), P(), P()),
        out_specs=P(AXES, None),
        check_vma=False,
    )
```

```python
import functools

import jax
import jax.numpy as jnp
from jax import lax
from jax.experimental import pallas as pl
from jax.experimental.pallas import tpu as pltpu
from jax.sharding import PartitionSpec as P

HEADS = 16
DH = 128
BLK = 512
TOPK = 3
CAP = 4
ROWS = 16
CHIPS = ROWS // 2
K_FIRST = 224
V_PARTS = (96, 32)
CHIP_ORDER = (4, 3, 5, 2, 6, 1, 7)
QUERY_ORDER = (1, 7, 4, 3, 5, 2, 6)
EXP2_SCALE = DH ** (-0.5) * 1.4426950408889634
VMEM_BYTES = 56 * 1024 * 1024
AXES = ("seq", "grp")


def any_spec():
    return pl.BlockSpec(memory_space=pl.ANY)


def vmem_spec():
    return pl.BlockSpec(memory_space=pltpu.VMEM)


def smem_spec():
    return pl.BlockSpec(memory_space=pltpu.SMEM)


def params():
    return pltpu.CompilerParams(vmem_limit_bytes=VMEM_BYTES)


def cost(flops, moved, exps=0):
    return pl.CostEstimate(flops=flops, bytes_accessed=moved, transcendentals=exps)


def split_first_kernel(key_ref, first_ref):
    for head in range(HEADS):
        first_ref[head] = key_ref[:, pl.ds(head * DH, DH)]


def split_first(key_rows):
    return pl.pallas_call(
        split_first_kernel,
        grid=(1,),
        in_specs=[pl.BlockSpec((K_FIRST, HEADS * DH), lambda i: (0, 0))],
        out_specs=pl.BlockSpec((HEADS, K_FIRST, DH), lambda i: (0, 0, 0)),
        out_shape=jax.ShapeDtypeStruct((HEADS, K_FIRST, DH), jnp.bfloat16),
        compiler_params=params(),
        cost_estimate=cost(0, 4 * K_FIRST * HEADS * DH),
        name="split_first",
    )(key_rows)


def run_copies(copies):
    for copy in copies:
        copy.start()
    for copy in copies:
        copy.wait()


def same_core(seq, chip_shift):
    core = lax.rem(seq, 2)
    at = lax.rem(seq + 2 * chip_shift + ROWS, ROWS)
    return at, at + 1 - 2 * core


def put_heads(seq, held, mine_ref, other_ref, sem):
    copies = []
    for chip in range(CHIPS):
        mine, other = same_core(seq, chip)
        copies.append(pltpu.make_async_copy(held.at[mine], mine_ref.at[chip], sem.at[2 * chip]))
        copies.append(
            pltpu.make_async_copy(held.at[other], other_ref.at[chip], sem.at[2 * chip + 1])
        )
    run_copies(copies)


def split_rest_kernel(seq_ref, key_ref, earlier_ref, mine_ref, other_ref, held, sem):
    for head in range(HEADS):
        held[head] = key_ref[pl.ds(K_FIRST, BLK - K_FIRST), pl.ds(head * DH, DH)]
    put_heads(seq_ref[0], held, mine_ref, other_ref, sem)


def turn_kernel(seq_ref, row_ref, earlier_ref, mine_ref, other_ref, held, sem):
    for head in range(HEADS):
        held[head] = row_ref[:, pl.ds(head * DH, DH)].T
    put_heads(seq_ref[0], held, mine_ref, other_ref, sem)


def by_core(kernel, seq, array, earlier, shape, name):
    return pl.pallas_call(
        kernel,
        in_specs=[smem_spec(), vmem_spec(), any_spec()],
        out_specs=[any_spec()] * 2,
        out_shape=[jax.ShapeDtypeStruct((CHIPS,) + shape, jnp.bfloat16)] * 2,
        scratch_shapes=[
            pltpu.VMEM((ROWS,) + shape, jnp.bfloat16),
            pltpu.SemaphoreType.DMA((ROWS,)),
        ],
        compiler_params=params(),
        cost_estimate=cost(0, 4 * ROWS * shape[0] * shape[1]),
        name=name,
    )(seq, array, earlier)


def pack_kernel(mine_ref, other_ref, *rest):
    piece_refs, sem = rest[:CHIPS], rest[CHIPS]
    copies = []
    for chip in range(CHIPS):
        copies.append(
            pltpu.make_async_copy(mine_ref.at[chip], piece_refs[chip].at[0], sem.at[2 * chip])
        )
        copies.append(
            pltpu.make_async_copy(other_ref.at[chip], piece_refs[chip].at[1], sem.at[2 * chip + 1])
        )
    run_copies(copies)


def pack(mine, other, name):
    shape = mine.shape[1:]
    return pl.pallas_call(
        pack_kernel,
        in_specs=[vmem_spec()] * 2,
        out_specs=[any_spec()] * CHIPS,
        out_shape=[jax.ShapeDtypeStruct((2,) + shape, jnp.bfloat16)] * CHIPS,
        scratch_shapes=[pltpu.SemaphoreType.DMA((ROWS,))],
        compiler_params=params(),
        cost_estimate=cost(0, 8 * CHIPS * shape[0] * shape[1]),
        name=name,
    )(mine, other)


def to_rows(seq, piece_refs, held, sem, start=0, rows=None):
    copies = []
    for chip in range(CHIPS):
        for which, row in enumerate(same_core(seq, -chip)):
            place = held.at[row] if rows is None else held.at[row, pl.ds(start, rows)]
            copies.append(
                pltpu.make_async_copy(piece_refs[chip].at[which], place, sem.at[2 * chip + which])
            )
    return copies


def nothing_kernel(*refs):
    pass


def after(arrays, earlier):
    count = len(arrays)
    return pl.pallas_call(
        nothing_kernel,
        in_specs=[any_spec()] * (count + len(earlier)),
        out_specs=[any_spec()] * count,
        out_shape=[jax.ShapeDtypeStruct(a.shape, a.dtype) for a in arrays],
        input_output_aliases={i: i for i in range(count)},
        cost_estimate=cost(0, 0),
        name="after",
    )(*arrays, *earlier)


def gather_kernel(parts, pieces, extra, seq_ref, block_ref, *rest):
    in_refs, rest = rest[: max(pieces, 1)], rest[max(pieces, 1) + extra :]
    if pieces:
        all_ref, rest = rest[0], rest[1:]
    send_refs, rest = rest[: len(parts)], rest[len(parts) :]
    if pieces:
        held, in_sem, out_sem = rest
        run_copies(to_rows(seq_ref[0], in_refs, held, in_sem))
        whole = pltpu.make_async_copy(held, all_ref, in_sem.at[0])
        whole.start()
    else:
        held, out_sem, whole = in_refs[0], rest[0], None

    start = 0
    for part, (rows, send_ref) in enumerate(zip(parts, send_refs)):

        def send(slot, carry, start=start, rows=rows, send_ref=send_ref, part=part):
            pltpu.make_async_copy(
                held.at[block_ref[slot], pl.ds(start, rows)], send_ref.at[slot], out_sem.at[part]
            ).start()
            return carry

        lax.fori_loop(0, ROWS * CAP, send, 0)
        start += rows
    for part, send_ref in enumerate(send_refs):
        pltpu.make_async_copy(send_ref, send_ref, out_sem.at[part]).wait()
    if whole is not None:
        whole.wait()


def gather(seq, send_block, arrays, parts, name, earlier=()):
    pieces = len(arrays) if len(arrays) > 1 else 0
    rows, columns = arrays[0].shape[-2:]
    out_shape = [jax.ShapeDtypeStruct((ROWS * CAP, part, columns), jnp.bfloat16) for part in parts]
    scratch = [pltpu.SemaphoreType.DMA((len(parts),))]
    in_specs = [vmem_spec()]
    if pieces:
        out_shape = [jax.ShapeDtypeStruct((ROWS, rows, columns), jnp.bfloat16)] + out_shape
        scratch = [
            pltpu.VMEM((ROWS, rows, columns), jnp.bfloat16),
            pltpu.SemaphoreType.DMA((ROWS,)),
        ] + scratch
        in_specs = [any_spec()] * pieces
    return pl.pallas_call(
        functools.partial(gather_kernel, parts, pieces, len(earlier)),
        in_specs=[smem_spec(), smem_spec()] + in_specs + [any_spec()] * len(earlier),
        out_specs=[any_spec()] * len(out_shape),
        out_shape=out_shape,
        scratch_shapes=scratch,
        compiler_params=params(),
        cost_estimate=cost(0, 2 * ROWS * (CAP + 1) * sum(parts) * columns),
        name=name,
    )(seq, send_block, *arrays, *earlier)


def weights_kernel(held_count, owner_ref, rank_ref, usable_ref, row_ref, seq_ref, own_a, own_b, *rest):
    picks, rest = rest[: 2 * TOPK], rest[2 * TOPK :]
    pieces, rest = rest[:CHIPS], rest[CHIPS + held_count :]
    weight_ref, inverse_ref, queries, scores, sem = rest
    row = row_ref[pl.program_id(0)]

    @pl.when(pl.program_id(0) == 0)
    def _():
        run_copies(to_rows(seq_ref[0], pieces, queries, sem))

    query = queries[row]
    key_pairs = [(own_a[0], own_b[0])] + [
        (picks[2 * j][0, 0], picks[2 * j + 1][0, 0]) for j in range(TOPK)
    ]

    def raw(pair):
        upper = jnp.dot(pair[0], query, preferred_element_type=jnp.float32)
        lower = jnp.dot(pair[1], query, preferred_element_type=jnp.float32)
        return upper * EXP2_SCALE, lower * EXP2_SCALE

    key_at = lax.broadcasted_iota(jnp.int32, (BLK, BLK), 0)
    query_at = lax.broadcasted_iota(jnp.int32, (BLK, BLK), 1)
    upper, lower = raw(key_pairs[0])
    own = jnp.where(query_at >= key_at, jnp.concatenate([upper, lower], axis=0), -jnp.inf)
    scores[0] = own
    top = jnp.max(own, axis=0, keepdims=True)
    inverse_ref[0] = top

    for j in range(TOPK):

        @pl.when(usable_ref[row * TOPK + j] > 0)
        def _(j=j):
            upper, lower = raw(key_pairs[1 + j])
            scores[1 + j, pl.ds(0, K_FIRST), :] = upper
            scores[1 + j, pl.ds(K_FIRST, BLK - K_FIRST), :] = lower
            inverse_ref[0] = jnp.maximum(
                inverse_ref[0],
                jnp.maximum(
                    jnp.max(upper, axis=0, keepdims=True), jnp.max(lower, axis=0, keepdims=True)
                ),
            )

    top = inverse_ref[0]
    exps = jnp.exp2(scores[0] - top)
    weight_ref[0, 0] = exps.astype(jnp.bfloat16)
    inverse_ref[0] = jnp.sum(exps, axis=0, keepdims=True)
    for j in range(TOPK):
        is_usable = usable_ref[row * TOPK + j] > 0

        @pl.when(is_usable)
        def _(j=j):
            exps = jnp.exp2(scores[1 + j] - top)
            weight_ref[0, 1 + j] = exps.astype(jnp.bfloat16)
            inverse_ref[0] = inverse_ref[0] + jnp.sum(exps, axis=0, keepdims=True)

        @pl.when(jnp.logical_not(is_usable))
        def _(j=j):
            weight_ref[0, 1 + j] = jnp.zeros((BLK, BLK), jnp.bfloat16)

    inverse_ref[0] = 1.0 / inverse_ref[0]


def make_weights(tables, seq, rows_at, query_pieces, own_a, own_b, got_a, got_b, held=()):
    owner, rank, usable = tables
    rest = BLK - K_FIRST
    steps = rows_at.shape[0]

    def pick(j, rows):
        def index(i, owner, rank, usable, at, seq):
            return (owner[at[i] * TOPK + j], rank[at[i] * TOPK + j], 0, 0)

        return pl.BlockSpec((1, 1, rows, DH), index)

    in_specs = [
        pl.BlockSpec((1, K_FIRST, DH), lambda i, o, r, u, at, s: (at[i], 0, 0)),
        pl.BlockSpec((1, rest, DH), lambda i, o, r, u, at, s: (at[i], 0, 0)),
    ]
    args = [own_a, own_b]
    for j in range(TOPK):
        in_specs += [pick(j, K_FIRST), pick(j, rest)]
        args += [got_a.reshape(ROWS, CAP, K_FIRST, DH), got_b.reshape(ROWS, CAP, rest, DH)]
    args += [*query_pieces, *held]
    in_specs += [any_spec()] * (CHIPS + len(held))
    blocks = steps * (1 + TOPK)
    prefetched = (owner, rank, usable, rows_at, seq)
    first_held = len(prefetched) + len(args) - len(held)
    return pl.pallas_call(
        functools.partial(weights_kernel, len(held)),
        grid_spec=pltpu.PrefetchScalarGridSpec(
            num_scalar_prefetch=len(prefetched),
            grid=(steps,),
            in_specs=in_specs,
            out_specs=[
                pl.BlockSpec(
                    (1, 1 + TOPK, BLK, BLK), lambda i, o, r, u, at, s: (at[i], 0, 0, 0)
                ),
                pl.BlockSpec((1, 1, BLK), lambda i, o, r, u, at, s: (at[i], 0, 0)),
            ],
            scratch_shapes=[
                pltpu.VMEM((ROWS, DH, BLK), jnp.bfloat16),
                pltpu.VMEM((1 + TOPK, BLK, BLK), jnp.float32),
                pltpu.SemaphoreType.DMA((ROWS,)),
            ],
        ),
        out_shape=[
            jax.ShapeDtypeStruct((ROWS, 1 + TOPK, BLK, BLK), jnp.bfloat16),
            jax.ShapeDtypeStruct((ROWS, 1, BLK), jnp.float32),
        ],
        input_output_aliases={first_held + i: i for i in range(len(held))},
        compiler_params=params(),
        cost_estimate=cost(
            2 * blocks * BLK * BLK * DH, 2 * blocks * (BLK * BLK + BLK * DH), blocks * BLK * BLK
        ),
        name="make_weights",
    )(*prefetched, *args)


def outputs_kernel(start, rows, owner_ref, rank_ref, row_ref, inverse_ref, *rest):
    weight_refs, rest = rest[: 1 + TOPK], rest[1 + TOPK :]
    own_ref, picks, out_ref = rest[0], rest[1 : 1 + TOPK], rest[1 + TOPK]
    total = jnp.dot(
        own_ref[0, pl.ds(start, rows), :], weight_refs[0][0, 0], preferred_element_type=jnp.float32
    )
    for j in range(TOPK):
        total += jnp.dot(
            picks[j][0, 0], weight_refs[1 + j][0, 0], preferred_element_type=jnp.float32
        )
    out_ref[0] = (total * inverse_ref[0]).astype(jnp.bfloat16)


def make_outputs(tables, rows_at, weights, inverse, values, got, start, rows):
    owner, rank, _ = tables
    steps = rows_at.shape[0]

    def pick(j):
        def index(i, owner, rank, at):
            place = at[i] * TOPK + j
            return (owner[place], rank[place], 0, 0)

        return pl.BlockSpec((1, 1, rows, BLK), index)

    blocks = steps * (1 + TOPK)
    return pl.pallas_call(
        functools.partial(outputs_kernel, start, rows),
        grid_spec=pltpu.PrefetchScalarGridSpec(
            num_scalar_prefetch=3,
            grid=(steps,),
            in_specs=[pl.BlockSpec((1, 1, BLK), lambda i, o, r, at: (at[i], 0, 0))]
            + [
                pl.BlockSpec((1, 1, BLK, BLK), lambda i, o, r, at, j=j: (at[i], j, 0, 0))
                for j in range(1 + TOPK)
            ]
            + [pl.BlockSpec((1, DH, BLK), lambda i, o, r, at: (at[i], 0, 0))]
            + [pick(j) for j in range(TOPK)],
            out_specs=pl.BlockSpec((1, rows, BLK), lambda i, *_: (i, 0, 0)),
        ),
        out_shape=jax.ShapeDtypeStruct((steps, rows, BLK), jnp.bfloat16),
        compiler_params=params(),
        cost_estimate=cost(2 * blocks * BLK * BLK * DH, 2 * blocks * BLK * (BLK + rows)),
        name="make_outputs",
    )(
        owner,
        rank,
        rows_at,
        inverse,
        *([weights] * (1 + TOPK)),
        values,
        *([got.reshape(ROWS, CAP, rows, BLK)] * TOPK),
    )


def finish_kernel(seq_ref, first_ref, *rest):
    pieces, (out_ref, last, sem) = rest[:CHIPS], rest[CHIPS:]
    run_copies(to_rows(seq_ref[0], pieces, last, sem))
    for head in range(HEADS):
        whole = jnp.concatenate([first_ref[head], last[head]], axis=0)
        out_ref[:, pl.ds(head * DH, DH)] = whole.T


def finish(seq, first, pieces):
    return pl.pallas_call(
        finish_kernel,
        in_specs=[smem_spec(), vmem_spec()] + [any_spec()] * CHIPS,
        out_specs=vmem_spec(),
        out_shape=jax.ShapeDtypeStruct((BLK, HEADS * DH), jnp.bfloat16),
        scratch_shapes=[
            pltpu.VMEM((ROWS, V_PARTS[1], BLK), jnp.bfloat16),
            pltpu.SemaphoreType.DMA((ROWS,)),
        ],
        compiler_params=params(),
        cost_estimate=cost(0, 4 * BLK * HEADS * DH),
        name="finish",
    )(seq, first, *pieces)


def permute_seq(array, place):
    seq_count, grp_count = lax.axis_size("seq"), lax.axis_size("grp")
    pairs = [
        (s * grp_count + g, place(s) % seq_count * grp_count + g)
        for s in range(seq_count)
        for g in range(grp_count)
    ]
    return lax.ppermute(array, AXES, pairs)


def swap_cores(array):
    return permute_seq(array, lambda s: s ^ 1)


def along_chips(pieces, order=CHIP_ORDER):
    moved = {0: pieces[0]}
    for chip in order:
        moved[chip] = permute_seq(pieces[chip], lambda s, chip=chip: s + 2 * chip)
    return [moved[chip] for chip in range(CHIPS)]


def exchange(array, axis):
    return lax.all_to_all(array, axis, split_axis=0, concat_axis=0, tiled=True)


def routes(pick_column, pick_back):
    seq, grp = lax.axis_index("seq"), lax.axis_index("grp")
    requests = ROWS * TOPK
    target = lax.dynamic_index_in_dim(pick_column, seq, 1, keepdims=False).reshape(-1, requests)
    back = lax.dynamic_index_in_dim(pick_back, seq, 1, keepdims=False).reshape(-1, requests)
    column = jnp.arange(target.shape[0], dtype=jnp.int32)[:, None]
    row = (jnp.arange(requests, dtype=jnp.int32) // TOPK)[None, :]
    local_row = row - back - (target >= column).astype(jnp.int32)
    at = jnp.arange(requests, dtype=jnp.int32)
    earlier = at[:, None] > at[None, :]
    hits = target == grp
    place = jnp.sum(hits[:, None, :] & earlier[None], axis=2, dtype=jnp.int32)
    chosen = hits[:, None, :] & (
        place[:, None, :] == jnp.arange(CAP, dtype=jnp.int32)[None, :, None]
    )
    send_block = jnp.sum(
        jnp.where(chosen, jnp.maximum(local_row, 0)[:, None, :], 0), axis=2, dtype=jnp.int32
    ).reshape(-1)
    owner = lax.dynamic_index_in_dim(target, grp, 0, keepdims=False)
    rank = jnp.sum((owner[:, None] == owner[None, :]) & earlier, axis=1, dtype=jnp.int32)
    usable = (lax.dynamic_index_in_dim(local_row, grp, 0, keepdims=False) >= 0).astype(jnp.int32)
    return send_block, (owner, rank, usable)


def body(query_rows, key_rows, value_rows, pick_column, pick_back):
    seq = lax.axis_index("seq").astype(jnp.int32).reshape(1)
    rest = BLK - K_FIRST
    key_first = split_first(key_rows)
    own_a = exchange(key_first, "seq")
    mine, other = by_core(split_rest_kernel, seq, key_rows, key_first, (rest, DH), "split_rest")
    key_pieces = pack(mine, swap_cores(other), "pack_keys")
    mine, other = by_core(turn_kernel, seq, value_rows, key_first, (DH, BLK), "turn_values")
    value_pieces = pack(mine, swap_cores(other), "pack_values")
    mine, other = by_core(turn_kernel, seq, query_rows, key_first, (DH, BLK), "turn_queries")
    query_pieces = pack(mine, swap_cores(other), "pack_queries")

    send_block, tables = routes(pick_column, pick_back)
    ready = [key_pieces[0], value_pieces[0]]
    (send_a,) = gather(seq, send_block, [own_a], (K_FIRST,), "gather_a", earlier=ready)
    got_a = exchange(send_a, "grp")

    key_pieces = along_chips(after(key_pieces, [send_a]))
    own_b, send_b = gather(
        seq, send_block, key_pieces, (rest,), "gather_b", earlier=[query_pieces[0]]
    )
    (send_b,) = after([send_b], [got_a])
    got_b = exchange(send_b, "grp")

    value_pieces = along_chips(after(value_pieces, [key_pieces[CHIP_ORDER[2]]]))
    values, *sends = gather(seq, send_block, value_pieces, V_PARTS, "gather_values")
    query_pieces = along_chips(after(query_pieces, [value_pieces[CHIP_ORDER[2]]]), QUERY_ORDER)
    straight = jnp.arange(ROWS, dtype=jnp.int32)
    same = (seq + 2 * jnp.arange(CHIPS, dtype=jnp.int32)) % ROWS
    keys = (query_pieces, own_a, own_b, got_a, got_b)
    held = make_weights(tables, seq, same ^ 1, *keys)
    weights, inverse = make_weights(tables, seq, same, *keys, held=held)
    ready = [got_b] + [query_pieces[chip] for chip in QUERY_ORDER[:2]]
    (send,) = after(sends[:1], ready)
    got_first = exchange(send, "grp")
    inputs = (weights, inverse, values)
    first = make_outputs(tables, straight, *inputs, got_first, 0, V_PARTS[0])
    (send,) = after(sends[1:], [got_first, held[1]])
    got_last = exchange(send, "grp")
    (first,) = after([first], [got_last])
    first = exchange(first, "seq")

    other = swap_cores(make_outputs(tables, same ^ 1, *inputs, got_last, *V_PARTS))
    mine = make_outputs(tables, same, *inputs, got_last, *V_PARTS)
    return finish(seq, first, along_chips(pack(mine, other, "pack_outputs")))


def solution(mesh):
    return jax.shard_map(
        body,
        mesh=mesh,
        in_specs=(P(AXES, None), P(AXES, None), P(AXES, None), P(), P()),
        out_specs=P(AXES, None),
        check_vma=False,
    )
```
